32 devices in a mesh: dp: 8 (over z, y), tensor: 4 (over x, core).
Axes of the slice: x: 2, y: 2, z: 4, core: 2. Of those that a mesh axis runs over, the one named last changes fastest.
Arguments:
- tokens: bfloat16 [3, 2048, 2048], P(None, 'dp'), may hold values from -6 to 6
- seg_ids: int32 [3, 2048], P(None, 'dp'), may hold values from 0 to 3, as said below
- norm1_gain: float32 [2048], replicated, may hold values from 0.5 to 1.5
- w_query: bfloat16 [2048, 2048], P(None, 'tensor'), may hold values from -0.5 to 0.5
- w_keyval: bfloat16 [2048, 8, 128], P(None, 'tensor'), may hold values from -0.5 to 0.5
- w_out: bfloat16 [2048, 2048], P('tensor'), may hold values from -0.75 to 0.75
- norm2_gain: float32 [2048], replicated, may hold values from 0.5 to 1.5
- w_gate: bfloat16 [2048, 8192], P(None, 'tensor'), may hold values from -0.125 to 0.125
- w_up: bfloat16 [2048, 8192], P(None, 'tensor'), may hold values from -0.125 to 0.125
- w_down: bfloat16 [8192, 2048], P('tensor'), may hold values from -0.5 to 0.5
- cotangent: bfloat16 [3, 2048, 2048], P(None, 'dp'), may hold values from -6 to 6
Outputs:
- layer_out: bfloat16 [3, 2048, 2048], P(None, ('dp', 'tensor'))
- grad_tokens: float32 [3, 2048, 2048], P(None, ('dp', 'tensor'))
- grad_gain1: float32 [2048], P(('dp', 'tensor'))
- grad_query: float32 [2048, 2048], P('dp', 'tensor')
- grad_keyval: float32 [2048, 8, 128], P('dp', 'tensor')
- grad_outproj: float32 [2048, 2048], P('tensor', 'dp')
- grad_gain2: float32 [2048], P(('dp', 'tensor'))
- grad_gate: float32 [2048, 8192], P('dp', 'tensor')
- grad_up: float32 [2048, 8192], P('dp', 'tensor')
- grad_down: float32 [8192, 2048], P('tensor', 'dp')
The draws below stay inside these ranges and needn't reach their ends.
Inputs may be any that keep to these rules, and one draw needn't show every extreme that they name: `seg_ids`: document numbers never fall along a sequence and start at 0; each sequence holds at most 4 documents, and one sequence, drawn from the seed, is a single document.
All inputs are finite; a program needn't handle non-finite values.
Results may differ from the reference program's by a relative error of at most 0.02.
Values may be sent and summed in bfloat16 or wider, within the bound.
No kernel may reach another device: no remote copies, remote signals or barrier semaphores. Data moves between devices by JAX's collectives and lax.ppermute only.
A program may use at most 256 MiB of HBM per device.

```python
import jax
import jax.numpy as jnp
from jax import lax

D = 2048
H = 32
KVH = 8
HD = 64
FF = 8192
SEQS = 3
LENGTH = 2048


def draw_seg_ids(key, part):
    key = jax.random.fold_in(key, 11)
    pick_key, cut_key = jax.random.split(key)
    whole_row = jax.random.randint(pick_key, (), 0, SEQS)
    row_keys = jax.random.split(cut_key, SEQS)
    cuts = jax.vmap(lambda one: jax.random.permutation(one, LENGTH - 1)[:3] + 1)(row_keys)
    position = jnp.arange(LENGTH)
    counted = jnp.sum((position[None, :, None] >= cuts[:, None, :]).astype(jnp.int32), axis=2)
    rows = jnp.arange(SEQS)
    return jnp.where(rows[:, None] == whole_row, 0, counted).astype(jnp.int32)


def shard_levels(stream_key, extent, pieces, smallest, largest):
    gain, own = 1.0, jax.random.fold_in(stream_key, 6)
    for axis_at, blocks in pieces:
        draws = jnp.exp(jax.random.uniform(jax.random.fold_in(own, axis_at), (blocks,), jnp.float32, smallest / len(pieces), largest / len(pieces)))
        gain = gain * jnp.repeat(draws, extent[axis_at] // blocks).reshape([-1 if axis == axis_at else 1 for axis in range(len(extent))])
    return gain


def centred(key, dims, width, reach, shards=(), dtype=jnp.bfloat16):
    drawn = jax.random.normal(key, dims, jnp.float32) * width
    if len(shards) > 0:
        drawn = shard_levels(key, dims, shards, -0.22, 0.18) * drawn
    return jnp.clip(drawn, min=-reach, max=reach).astype(dtype)


def setup_inputs(seed: int = 0) -> dict:
    key_list = jax.random.split(jax.random.key(seed), 12)
    tokens = centred(key_list[0], (SEQS, LENGTH, D), 1.0, 6.0, ((1, 8),))
    seg_ids = draw_seg_ids(jax.random.fold_in(key_list[11], 71), 0)
    norm1_gain = jnp.clip(1.0 + 0.1 * jax.random.normal(key_list[2], (D,), jnp.float32), 0.5, 1.5)
    w_query = centred(key_list[3], (D, H * HD), (D // 16) ** -0.5, 0.5, ((1, 4),))
    w_keyval = centred(key_list[4], (D, KVH, 2 * HD), (D // 16) ** -0.5, 0.5, ((1, 4),))
    w_out = centred(key_list[5], (H * HD, D), HD ** -0.5, 0.75, ((0, 4),))
    norm2_gain = jnp.clip(1.0 + 0.1 * jax.random.normal(key_list[6], (D,), jnp.float32), 0.5, 1.5)
    w_gate = centred(key_list[7], (D, FF), D ** -0.5, 0.125, ((1, 4),))
    w_up = centred(key_list[8], (D, FF), D ** -0.5, 0.125, ((1, 4),))
    w_down = centred(key_list[9], (FF, D), (FF // 64) ** -0.5, 0.5, ((0, 4),))
    cotangent = centred(key_list[10], (SEQS, LENGTH, D), 1.0, 6.0, ((1, 8),))
    return dict(tokens=tokens, seg_ids=seg_ids, norm1_gain=norm1_gain, w_query=w_query, w_keyval=w_keyval, w_out=w_out, norm2_gain=norm2_gain, w_gate=w_gate, w_up=w_up, w_down=w_down, cotangent=cotangent)


EPS = 1e-05
SCALE = 0.015625
RESID = 0.22
THETA = 10000000.0
NEG = -1e+30
HIGH_PRECISION = lax.Precision.HIGHEST

@jax.custom_vjp
def low(v):
    return lax.optimization_barrier(v.astype(jnp.bfloat16)).astype(jnp.float32)

@jax.custom_vjp
def lowered_backward(v):
    return v

def low_keep(v):
    return (low(v), None)

def low_pass(kept, grad):
    return (grad,)

def back_keep(v):
    return (v, None)

def back_low(kept, grad):
    return (low(grad),)
low.defvjp(low_keep, low_pass)
lowered_backward.defvjp(back_keep, back_low)

def rope_tables(positions, head_dim):
    half = head_dim // 2
    inverse = jnp.power(jnp.float32(THETA), -(jnp.arange(half).astype(jnp.float32) * (2.0 / head_dim)))
    angle = positions.astype(jnp.float32)[:, None] * inverse[None, :]
    return (jnp.cos(angle), jnp.sin(angle))

def rotate(vector, cosine, sine):
    half = vector.shape[-1] // 2
    first = vector[..., :half]
    second = vector[..., half:]
    return jnp.concatenate([first * cosine - second * sine, second * cosine + first * sine], -1)

def rms_scale(vector):
    return lax.rsqrt(lax.optimization_barrier(jnp.mean(vector * vector, axis=-1, keepdims=True)) + EPS)

def reference(tokens, seg_ids, norm1_gain, w_query, w_keyval, w_out, norm2_gain, w_gate, w_up, w_down, cotangent):
    group = H // KVH
    cosine, sine = rope_tables(jnp.arange(LENGTH), HD)
    cosine = cosine[:, None, :]
    sine = sine[:, None, :]
    position = jnp.arange(LENGTH)
    causal = position[None, :] <= position[:, None]
    seg_pairs = jnp.repeat(seg_ids, KVH, axis=0)

    def head_block(items):
        query, key, value, segment = items
        allowed = causal & (segment[:, None] == segment[None, :])
        scores = lowered_backward(jnp.einsum('gqd,kd->gqk', query, key, precision=HIGH_PRECISION) * SCALE)
        scores = jnp.where(allowed[None], scores, NEG)
        peak = lax.optimization_barrier(jnp.max(scores, axis=-1, keepdims=True))
        total = jnp.log(lax.optimization_barrier(jnp.sum(jnp.exp(scores - peak), axis=-1, keepdims=True))) + peak
        probs = low(jnp.exp(scores - total))
        return low(lowered_backward(jnp.einsum('gqk,kd->gqd', probs, value, precision=HIGH_PRECISION)))

    def forward(xf, gain1, query_weight, keyval_weight, output_weight, gain2, gate_weight, up_weight, down_weight):
        first_normed = low(xf * rms_scale(xf) * gain1)
        query_projected = lowered_backward(jnp.einsum('ucf,fy->ucy', first_normed, query_weight, precision=HIGH_PRECISION))
        keyval_projected = lowered_backward(jnp.einsum('ymt,txj->ymxj', first_normed, keyval_weight, precision=HIGH_PRECISION))
        query = low(rotate(query_projected.reshape(SEQS, LENGTH, H, HD), cosine, sine))
        key = low(rotate(keyval_projected[..., :HD], cosine, sine))
        value = low(keyval_projected[..., HD:])
        q_pairs = query.reshape(SEQS, LENGTH, KVH, group, HD).transpose(0, 2, 3, 1, 4).reshape(SEQS * KVH, group, LENGTH, HD)
        k_pairs = key.transpose(0, 2, 1, 3).reshape(SEQS * KVH, LENGTH, HD)
        v_pairs = value.transpose(0, 2, 1, 3).reshape(SEQS * KVH, LENGTH, HD)
        attention_output = lax.map(jax.checkpoint(head_block), (q_pairs, k_pairs, v_pairs, seg_pairs))
        attention_output = attention_output.reshape(SEQS, KVH, group, LENGTH, HD).transpose(0, 3, 1, 2, 4).reshape(SEQS, LENGTH, H * HD)
        mixed_tokens = lowered_backward(jnp.einsum('hum,mo->huo', attention_output, output_weight, precision=HIGH_PRECISION))
        resid = xf + RESID * mixed_tokens
        second_normed = low(resid * rms_scale(resid) * gain2)
        gate_activation = lowered_backward(jnp.einsum('xey,yu->xeu', second_normed, gate_weight, precision=HIGH_PRECISION))
        up_activation = lowered_backward(jnp.einsum('xey,yu->xeu', second_normed, up_weight, precision=HIGH_PRECISION))
        hidden_activation = low(jax.nn.silu(gate_activation) * up_activation)
        feedforward_output = lowered_backward(jnp.einsum('xkt,tp->xkp', hidden_activation, down_weight, precision=HIGH_PRECISION))
        return resid + RESID * feedforward_output
    floats = (tokens.astype(jnp.float32), norm1_gain.astype(jnp.float32), w_query.astype(jnp.float32), w_keyval.astype(jnp.float32), w_out.astype(jnp.float32), norm2_gain.astype(jnp.float32), w_gate.astype(jnp.float32), w_up.astype(jnp.float32), w_down.astype(jnp.float32))
    layer_out, pull = jax.vjp(forward, *floats)
    grads = pull(cotangent.astype(jnp.float32))
    return (layer_out.astype(jnp.bfloat16), grads[0], grads[1], grads[2], grads[3], grads[4], grads[5], grads[6], grads[7], grads[8])
```

```python
import math

import jax
import jax.numpy as jnp
from jax import lax
from jax.experimental import pallas as pl
from jax.experimental.pallas import tpu as pltpu
from jax.sharding import PartitionSpec as P

EPS = 1e-05
SCALE = 0.015625
RESID = 0.22
THETA = 10000000.0
NEG = -1e30
PAD = 16
VMEM = 56 * 1024 * 1024
F32 = jnp.float32
BF16 = jnp.bfloat16
NT = (((1,), (1,)), ((), ()))
TN = (((0,), (0,)), ((), ()))


def dot(a, b, dims=None):
    if dims is None:
        return jnp.dot(a, b, preferred_element_type=F32)
    return lax.dot_general(a, b, dims, preferred_element_type=F32)


def params():
    return pltpu.CompilerParams(vmem_limit_bytes=VMEM)


def cost(flops, nbytes):
    return pl.CostEstimate(flops=int(flops), bytes_accessed=int(nbytes), transcendentals=0)


def slot_order(bits):
    slots = [0]
    for bit in reversed(bits):
        slots = slots + [k ^ (1 << bit) for k in slots]
    return slots


def swap(value, axis, distance):
    size = lax.axis_size(axis)
    return lax.ppermute(value, axis, [(i, i ^ distance) for i in range(size)])


def rope_tables(positions, head_dim):
    half = head_dim // 2
    inverse = jnp.power(F32(THETA), -(jnp.arange(half).astype(F32) * (2.0 / head_dim)))
    angle = positions.astype(F32)[:, None] * inverse[None, :]
    return (jnp.cos(angle), jnp.sin(angle))


def rotate_lanes(x, cosine, sine, half):
    width = x.shape[1]
    lane = lax.broadcasted_iota(jnp.int32, x.shape, 1)
    ahead = pltpu.roll(x, width - half, 1)
    behind = pltpu.roll(x, half, 1)
    partner = jnp.where((lane & (2 * half - 1)) < half, ahead, behind)
    times = width // cosine.shape[1]
    if times > 1:
        cosine = jnp.concatenate([cosine] * times, 1)
        sine = jnp.concatenate([sine] * times, 1)
    return x * cosine + partner * sine


def norm_keyval(tokens, gain, weight, counts, cosine, sine, half):
    seqs, block, width = tokens.shape
    out = weight.shape[1]

    def kernel(tok_ref, gain_ref, w_ref, count_ref, cos_ref, sin_ref, n_ref, kv_ref):
        xf = tok_ref[0].astype(F32)
        scale = lax.rsqrt(jnp.mean(xf * xf, axis=-1, keepdims=True) + EPS)
        normed = (xf * scale * gain_ref[...]).astype(BF16)
        n_ref[0] = normed
        raw = dot(normed, w_ref[...])
        kv_ref[0, :block, :] = rotate_lanes(raw, cos_ref[...], sin_ref[...], half).astype(BF16)
        kv_ref[0, block:, :] = count_ref[0]

    whole = lambda shape: pl.BlockSpec(shape, lambda s: (0,) * len(shape))
    return pl.pallas_call(
        kernel,
        grid=(seqs,),
        in_specs=[
            pl.BlockSpec((1, block, width), lambda s: (s, 0, 0)),
            whole((1, width)),
            whole((width, out)),
            pl.BlockSpec((1, PAD, out), lambda s: (s, 0, 0)),
            whole(cosine.shape),
            whole(sine.shape),
        ],
        out_specs=[
            pl.BlockSpec((1, block, width), lambda s: (s, 0, 0)),
            pl.BlockSpec((1, block + PAD, out), lambda s: (s, 0, 0)),
        ],
        out_shape=[
            jax.ShapeDtypeStruct((seqs, block, width), BF16),
            jax.ShapeDtypeStruct((seqs, block + PAD, out), BF16),
        ],
        compiler_params=params(),
        cost_estimate=cost(2 * seqs * block * width * out, 4 * seqs * block * width),
        name="norm_keyval",
    )(tokens, gain.reshape(1, width), weight, counts, cosine, sine)


def project_query(normed, weight, cosine, sine, half):
    seqs, block, width = normed.shape
    out = weight.shape[1]

    def kernel(n_ref, w_ref, cos_ref, sin_ref, q_ref):
        raw = dot(n_ref[0], w_ref[...])
        q_ref[0] = rotate_lanes(raw, cos_ref[...], sin_ref[...], half).astype(BF16)

    whole = lambda shape: pl.BlockSpec(shape, lambda s: (0,) * len(shape))
    return pl.pallas_call(
        kernel,
        grid=(seqs,),
        in_specs=[
            pl.BlockSpec((1, block, width), lambda s: (s, 0, 0)),
            whole((width, out)),
            whole(cosine.shape),
            whole(sine.shape),
        ],
        out_specs=pl.BlockSpec((1, block, out), lambda s: (s, 0, 0)),
        out_shape=jax.ShapeDtypeStruct((seqs, block, out), BF16),
        compiler_params=params(),
        cost_estimate=cost(2 * seqs * block * width * out, 2 * seqs * block * width),
        name="project_query",
    )(normed, weight, cosine, sine)


def stacked_lanes(x, group, hd, low):
    rows = x.shape[1]
    flat = jnp.concatenate([x[h * hd : (h + 1) * hd] for h in range(group)], 1)
    zero = jnp.zeros((hd, group * rows), flat.dtype)
    return jnp.concatenate([flat, zero] if low else [zero, flat], 0)


def stacked_rows(x, group, hd, low):
    parts = []
    for h in range(group):
        at = (h * hd) // (2 * hd) * (2 * hd)
        piece = x[:, at : at + 2 * hd]
        if (h % 2 == 0) != low:
            piece = pltpu.roll(piece, hd, 1)
        lane = lax.broadcasted_iota(jnp.int32, piece.shape, 1)
        parts.append(jnp.where((lane < hd) == low, piece, 0.0))
    return jnp.concatenate(parts, 0)


def mask_bias(chunk, block, position_block, doc_start, group):
    key_pos = chunk * block + lax.broadcasted_iota(jnp.int32, (block, block), 0)
    query_pos = position_block * block + lax.broadcasted_iota(jnp.int32, (block, block), 1)
    visible = (key_pos >= doc_start) & (key_pos <= query_pos)
    bias = jnp.where(visible, 0.0, NEG)
    return jnp.concatenate([bias] * group, 1)


def attend(query, keyval_all, doc_start, scalars, kv_local, hd):
    seqs, block, q_width = query.shape
    blocks = keyval_all.shape[0]
    group = q_width // kv_local // hd
    wide = group * block

    def kernel(sc, q_ref, kv_ref, doc_ref, o_ref, lse_ref, acc):
        seq = pl.program_id(0)
        mine = sc[0]
        start = sc[1 + seq]
        clear = sc[1 + seqs + seq]
        q_lanes = stacked_lanes((q_ref[0].astype(F32) * SCALE).T.astype(BF16), group, hd, True)
        doc = doc_ref[0]

        def scores_of(chunk, masked):
            kv = kv_ref[chunk, 0, :block, :]
            scores = dot(kv, q_lanes)
            if masked:
                scores = scores + mask_bias(chunk, block, mine, doc, group)
            return kv, scores

        kv, scores = scores_of(mine, True)
        peak = jnp.max(scores, axis=0, keepdims=True)
        probs = jnp.exp(scores - peak)
        total = jnp.sum(probs, axis=0, keepdims=True)
        acc[...] = dot(kv, probs.astype(BF16), TN)

        def step(masked):
            def run(chunk, carry):
                peak, total = carry
                kv, scores = scores_of(chunk, masked)
                higher = jnp.maximum(peak, jnp.max(scores, axis=0, keepdims=True))
                shrink = jnp.exp(peak - higher)
                probs = jnp.exp(scores - higher)
                total = total * shrink + jnp.sum(probs, axis=0, keepdims=True)
                acc[...] = acc[...] * shrink + dot(kv, probs.astype(BF16), TN)
                return higher, total

            return run

        carry = lax.fori_loop(start, clear, step(True), (peak, total))
        peak, total = lax.fori_loop(clear, mine, step(False), carry)
        lse_ref[0, 0] = peak + jnp.log(total)
        result = acc[hd:] / total
        result = jnp.concatenate([result[:, h * block : (h + 1) * block] for h in range(group)], 0)
        o_ref[0] = result.T.astype(BF16)

    return pl.pallas_call(
        kernel,
        grid_spec=pltpu.PrefetchScalarGridSpec(
            num_scalar_prefetch=1,
            grid=(seqs, kv_local),
            in_specs=[
                pl.BlockSpec((1, block, group * hd), lambda s, h, sc: (s, 0, h)),
                pl.BlockSpec((blocks, 1, block + PAD, 2 * hd), lambda s, h, sc: (0, s, 0, h)),
                pl.BlockSpec((1, 1, block), lambda s, h, sc: (s, 0, 0)),
            ],
            out_specs=[
                pl.BlockSpec((1, block, group * hd), lambda s, h, sc: (s, 0, h)),
                pl.BlockSpec((1, 1, 1, wide), lambda s, h, sc: (s, h, 0, 0)),
            ],
            scratch_shapes=[pltpu.VMEM((2 * hd, wide), F32)],
        ),
        out_shape=[
            jax.ShapeDtypeStruct((seqs, block, q_width), BF16),
            jax.ShapeDtypeStruct((seqs, kv_local, 1, wide), F32),
        ],
        compiler_params=params(),
        cost_estimate=cost(
            8 * seqs * block * q_width * blocks * block, 4 * seqs * blocks * block * 2 * hd
        ),
        name="attend",
    )(scalars, query, keyval_all, doc_start)


def attend_back(query, keyval_all, doc_start, attended, d_att, lse, cosine, sine, scalars, kv_local, hd):
    seqs, block, q_width = query.shape
    blocks = keyval_all.shape[0]
    group = q_width // kv_local // hd
    wide = group * block
    base = 1 + 2 * seqs

    def kernel(
        sc, q_ref, kv_ref, doc_ref, o_ref, do_ref, lse_ref, cos_ref, sin_ref, dq_ref, dkv_ref, acc
    ):
        seq = pl.program_id(0)
        mine = sc[0]
        start = sc[1 + seq]
        clear = sc[1 + seqs + seq]
        doc = doc_ref[0]
        q = q_ref[0].astype(F32) * SCALE
        d_out = do_ref[0].astype(F32)
        d_out_t = d_out.T
        q_lanes = stacked_lanes(q.T.astype(BF16), group, hd, True)
        o_lanes = d_out_t * o_ref[0].astype(F32).T
        delta = jnp.concatenate(
            [
                jnp.sum(o_lanes[h * hd : (h + 1) * hd], axis=0, keepdims=True)
                for h in range(group)
            ],
            1,
        )
        d_lanes = stacked_lanes(d_out_t.astype(BF16), group, hd, False)
        q_rows = stacked_rows(q, group, hd, True).astype(BF16)
        d_rows = stacked_rows(d_out, group, hd, False).astype(BF16)
        total = lse_ref[0, 0]
        acc[...] = jnp.zeros_like(acc)

        def work(chunk, masked):
            kv = kv_ref[chunk, 0, :block, :]
            scores = dot(kv, q_lanes)
            if masked:
                scores = scores + mask_bias(chunk, block, mine, doc, group)
            probs = jnp.exp(scores - total)
            d_probs = dot(kv, d_lanes)
            d_scores = (probs * (d_probs - delta)).astype(BF16)
            d_kv = dot(probs.astype(BF16), d_rows) + dot(d_scores, q_rows)
            dkv_ref[sc[base + chunk], 0] = d_kv.astype(BF16)
            acc[...] += dot(kv, d_scores, TN)

        def clean(chunk, carry):
            dkv_ref[sc[base + chunk], 0] = jnp.zeros((block, 2 * hd), BF16)
            return carry

        def step(masked):
            def run(chunk, carry):
                work(chunk, masked)
                return carry

            return run

        lax.fori_loop(0, start, clean, 0)
        lax.fori_loop(start, clear, step(True), 0)
        lax.fori_loop(clear, mine, step(False), 0)
        work(mine, True)
        lax.fori_loop(mine + 1, blocks, clean, 0)
        dq = acc[:hd] * SCALE
        dq = jnp.concatenate([dq[:, h * block : (h + 1) * block] for h in range(group)], 0)
        dq_ref[0] = rotate_lanes(dq.T, cos_ref[...], -sin_ref[...], hd // 2).astype(BF16)

    queries = pl.BlockSpec((1, block, group * hd), lambda s, h, sc: (s, 0, h))
    return pl.pallas_call(
        kernel,
        grid_spec=pltpu.PrefetchScalarGridSpec(
            num_scalar_prefetch=1,
            grid=(seqs, kv_local),
            in_specs=[
                queries,
                pl.BlockSpec((blocks, 1, block + PAD, 2 * hd), lambda s, h, sc: (0, s, 0, h)),
                pl.BlockSpec((1, 1, block), lambda s, h, sc: (s, 0, 0)),
                queries,
                queries,
                pl.BlockSpec((1, 1, 1, wide), lambda s, h, sc: (s, h, 0, 0)),
                pl.BlockSpec(cosine.shape, lambda s, h, sc: (0, 0)),
                pl.BlockSpec(sine.shape, lambda s, h, sc: (0, 0)),
            ],
            out_specs=[
                queries,
                pl.BlockSpec((blocks, 1, block, 2 * hd), lambda s, h, sc: (0, s, 0, h)),
            ],
            scratch_shapes=[pltpu.VMEM((2 * hd, wide), F32)],
        ),
        out_shape=[
            jax.ShapeDtypeStruct((seqs, block, q_width), BF16),
            jax.ShapeDtypeStruct((blocks, seqs, block, kv_local * 2 * hd), BF16),
        ],
        compiler_params=params(),
        cost_estimate=cost(
            20 * seqs * block * q_width * blocks * block, 8 * seqs * blocks * block * 2 * hd
        ),
        name="attend_back",
    )(scalars, query, keyval_all, doc_start, attended, d_att, lse, cosine, sine)


def feed_forward(normed, d_ffn, w_gate, w_up, w_down):
    rows, width = normed.shape
    hidden = w_gate.shape[1]
    tile = math.gcd(hidden, 512)
    steps = hidden // tile
    half = rows // 2

    def kernel(
        n_ref, dy_ref, wg_ref, wu_ref, wd_ref, h_ref, dg_ref, du_ref, fk, fs, nk, ns, f_acc, n_acc
    ):
        at = pl.program_id(0)
        normed = n_ref[...]
        gate = dot(normed, wg_ref[...])
        up = dot(normed, wu_ref[...])
        d_hidden = dot(dy_ref[...], wd_ref[...], NT)
        sigma = jax.nn.sigmoid(gate)
        swish = gate * sigma
        hidden_tile = (swish * up).astype(BF16)
        d_gate = (d_hidden * up * sigma * (1.0 + gate * (1.0 - sigma))).astype(BF16)
        d_up = (d_hidden * swish).astype(BF16)
        h_ref[...] = hidden_tile
        dg_ref[...] = d_gate
        du_ref[...] = d_up
        ffn = dot(hidden_tile, wd_ref[...])
        d_normed = dot(d_gate, wg_ref[...], NT) + dot(d_up, wu_ref[...], NT)

        @pl.when(at == 0)
        def _():
            f_acc[...] = ffn
            n_acc[...] = d_normed

        @pl.when(at > 0)
        def _():
            f_acc[...] += ffn
            n_acc[...] += d_normed

        @pl.when(at == steps - 1)
        def _():
            fk[...] = f_acc[:half].astype(BF16)
            fs[...] = f_acc[half:].astype(BF16)
            nk[...] = n_acc[:half].astype(BF16)
            ns[...] = n_acc[half:].astype(BF16)

    whole = lambda r: pl.BlockSpec((r, width), lambda j: (0, 0))
    return pl.pallas_call(
        kernel,
        grid=(steps,),
        in_specs=[
            whole(rows),
            whole(rows),
            pl.BlockSpec((width, tile), lambda j: (0, j)),
            pl.BlockSpec((width, tile), lambda j: (0, j)),
            pl.BlockSpec((tile, width), lambda j: (j, 0)),
        ],
        out_specs=[pl.BlockSpec((rows, tile), lambda j: (0, j))] * 3 + [whole(half)] * 4,
        out_shape=[jax.ShapeDtypeStruct((rows, hidden), BF16)] * 3
        + [jax.ShapeDtypeStruct((half, width), BF16)] * 4,
        scratch_shapes=[pltpu.VMEM((rows, width), F32)] * 2,
        compiler_params=params(),
        cost_estimate=cost(12 * rows * width * hidden, 6 * width * hidden + 6 * rows * hidden),
        name="feed_forward",
    )(normed, d_ffn, w_gate, w_up, w_down)


def transposed_slots(array, blocks_at):
    rows, width = array.shape
    count = blocks_at.shape[0]
    piece = width // count

    def kernel(at, a_ref, o_ref):
        o_ref[...] = a_ref[...].astype(F32).T.astype(BF16)

    return pl.pallas_call(
        kernel,
        grid_spec=pltpu.PrefetchScalarGridSpec(
            num_scalar_prefetch=1,
            grid=(count,),
            in_specs=[pl.BlockSpec((rows, piece), lambda i, at: (0, at[i]))],
            out_specs=pl.BlockSpec((piece, rows), lambda i, at: (i, 0)),
        ),
        out_shape=jax.ShapeDtypeStruct((width, rows), BF16),
        compiler_params=params(),
        cost_estimate=cost(0, 4 * rows * width),
        name="transposed_slots",
    )(blocks_at, array)


def body(
    tokens,
    seg_ids,
    norm1_gain,
    w_query,
    w_keyval,
    w_out,
    norm2_gain,
    w_gate,
    w_up,
    w_down,
    cotangent,
):
    seqs, block, width = tokens.shape
    kv_local = w_keyval.shape[1]
    hd = w_keyval.shape[2] // 2
    q_width = w_query.shape[1]
    kv_width = kv_local * 2 * hd
    dp = lax.axis_size("dp")
    nt = lax.axis_size("tensor")
    share = block // nt
    rows = seqs * block
    d_at = lax.axis_index("dp")
    t_at = lax.axis_index("tensor")
    t_bits = list(range(nt.bit_length() - 1))
    d_bits = list(range(dp.bit_length() - 1))
    t_slots = slot_order(t_bits)
    d_slots = slot_order(d_bits)
    d_order = d_at ^ jnp.array(d_slots, jnp.int32)

    def token_slots(array):
        return jnp.stack(
            [lax.dynamic_slice_in_dim(array, (t_at ^ k) * share, share, 1) for k in t_slots]
        )

    def token_order(array):
        where = jnp.array([t_slots.index(k) for k in range(nt)], jnp.int32)
        return jnp.concatenate(
            [
                lax.dynamic_index_in_dim(array, where[t_at ^ j], 0, keepdims=False)
                for j in range(nt)
            ],
            1,
        )

    def sum_shares(keep, send):
        for at, bit in enumerate(t_bits):
            total = keep.astype(F32) + swap(send, "tensor", 1 << bit).astype(F32)
            if at + 1 < len(t_bits):
                half = total.shape[0] // 2
                keep, send = total[:half], total[half:].astype(BF16)
        return total

    def gather_shares(array):
        for bit in reversed(t_bits):
            array = jnp.concatenate([array, swap(array, "tensor", 1 << bit)], 0)
        return array

    def summed_rows(left, right):
        half = left.shape[0] // 2
        send = dot(left[half:], right).astype(BF16)
        got = swap(send, "dp", 1 << d_bits[0])
        keep = dot(left[:half], right)
        for bit in d_bits[1:]:
            half = half // 2
            send = (keep[half:] + got[half:].astype(F32)).astype(BF16)
            keep = keep[:half] + got[:half].astype(F32)
            got = swap(send, "dp", 1 << bit)
        return keep + got.astype(F32)

    positions = d_at * block + jnp.arange(block)
    cosine, sine = rope_tables(positions, hd)
    cos_q = jnp.concatenate([cosine] * 4, 1)
    sin_q = jnp.concatenate([-sine, sine] * 2, 1)
    ones = jnp.ones((block, hd), F32)
    cos_kv = jnp.concatenate([cosine, cosine, ones], 1)
    sin_kv = jnp.concatenate([-sine, sine, 0.0 * ones], 1)
    counts = jnp.stack([jnp.sum((seg_ids == v).astype(F32), axis=1) for v in range(3)], 1)
    counts = jnp.pad(counts[:, None, :], ((0, 0), (0, PAD - 1), (0, kv_width - 3))).astype(BF16)
    keyval_weight = w_keyval.reshape(width, kv_width)
    first_normed, keyval = norm_keyval(
        tokens, norm1_gain, keyval_weight, counts, cos_kv, sin_kv, hd // 2
    )
    keyval_all = lax.all_gather(keyval, "dp", axis=0)
    query = project_query(first_normed, w_query, cos_q, sin_q, hd // 2)

    cot_slots = token_slots(cotangent)
    d_ffn = (RESID * cot_slots.astype(F32)).astype(BF16).reshape(rows, width)
    d_ffn_t = transposed_slots(d_ffn, d_order)
    first_normed_t = transposed_slots(first_normed.reshape(rows, width), d_order)
    xf_share = lax.dynamic_slice_in_dim(tokens, t_at * share, share, 1).astype(F32)

    before = jnp.sum(keyval_all[:, :, block, :3].astype(F32), axis=0).astype(jnp.int32)
    doc_start = jnp.sum(
        jnp.where(seg_ids[:, :, None] > jnp.arange(3), before[:, None, :], 0), axis=2
    )
    start = doc_start[:, 0] // block
    clear = jnp.clip((doc_start[:, -1] + block - 1) // block, start, d_at)
    where = jnp.array([d_slots.index(k) for k in range(dp)], jnp.int32)
    slot_of = where[d_at ^ jnp.arange(dp)]
    scalars = jnp.concatenate([d_at[None].astype(jnp.int32), start, clear, slot_of])
    doc_start = doc_start[:, None, :]
    attended, lse = attend(query, keyval_all, doc_start, scalars, kv_local, hd)

    att_slots = token_slots(attended)
    half = nt // 2
    mixed_send = dot(att_slots[half:], w_out, (((3,), (0,)), ((), ()))).astype(BF16)
    mixed_keep = dot(att_slots[:half], w_out, (((3,), (0,)), ((), ())))
    mixed = sum_shares(mixed_keep, mixed_send)[0]
    resid = xf_share + RESID * mixed
    scale2 = lax.rsqrt(jnp.mean(resid * resid, axis=-1, keepdims=True) + EPS)
    second_normed = (resid * scale2 * norm2_gain).astype(BF16)
    second_all = gather_shares(second_normed[None]).reshape(rows, width)
    hidden, d_gate, d_up, ffn_keep, ffn_send, d_keep, d_send = feed_forward(
        second_all, d_ffn, w_gate, w_up, w_down
    )
    halves = (half, seqs, share, width)
    d_norm2 = sum_shares(d_keep.reshape(halves), d_send.reshape(halves))[0]
    second_t = transposed_slots(second_all, d_order)
    grad_down = summed_rows(d_ffn_t, hidden).T
    grad_gate = summed_rows(second_t, d_gate)
    grad_up = summed_rows(second_t, d_up)
    ffn = sum_shares(ffn_keep.reshape(halves), ffn_send.reshape(halves))[0]
    layer_out = (resid + RESID * ffn).astype(BF16)

    d_out = cot_slots[0].astype(F32)
    scaled = norm2_gain * d_norm2
    d_resid = (
        d_out
        + scale2 * scaled
        - resid * scale2**3 * jnp.mean(scaled * resid, axis=-1, keepdims=True)
    )
    d_mixed = gather_shares((RESID * d_resid).astype(BF16)[None])
    d_att = token_order(dot(d_mixed, w_out, (((3,), (1,)), ((), ()))).astype(BF16))
    d_mixed = d_mixed.reshape(rows, width)
    d_query, d_keyval = attend_back(
        query, keyval_all, doc_start, attended, d_att, lse, cos_q, sin_q, scalars, kv_local, hd
    )
    grad_outproj = summed_rows(
        transposed_slots(d_mixed, d_order), att_slots.reshape(rows, q_width)
    ).T
    grad_query = summed_rows(first_normed_t, d_query.reshape(rows, q_width))
    for bit in d_bits:
        part = d_keyval.shape[0] // 2
        d_keyval = d_keyval[:part].astype(F32) + swap(
            d_keyval[part:].astype(BF16), "dp", 1 << bit
        ).astype(F32)
    d_keyval = d_keyval[0].reshape(seqs, block, kv_local, 2 * hd)
    first = d_keyval[..., : hd // 2]
    second = d_keyval[..., hd // 2 : hd]
    cosine = cosine[:, None, :]
    sine = sine[:, None, :]
    d_keyval = (
        jnp.concatenate(
            [first * cosine + second * sine, second * cosine - first * sine, d_keyval[..., hd:]], -1
        )
        .astype(BF16)
        .reshape(seqs, block, kv_width)
    )
    grad_keyval = summed_rows(first_normed_t, d_keyval.reshape(rows, kv_width))
    dq_slots = token_slots(d_query)
    dkv_slots = token_slots(d_keyval)
    contract = (((3,), (1,)), ((), ()))

    def back(at):
        return dot(dq_slots[at], w_query, contract) + dot(dkv_slots[at], keyval_weight, contract)

    d_norm1 = sum_shares(back(slice(0, half)), back(slice(half, nt)).astype(BF16))[0]
    scale1 = lax.rsqrt(jnp.mean(xf_share * xf_share, axis=-1, keepdims=True) + EPS)
    scaled = norm1_gain * d_norm1
    grad_tokens = (
        d_resid
        + scale1 * scaled
        - xf_share * scale1**3 * jnp.mean(scaled * xf_share, axis=-1, keepdims=True)
    )

    piece = width // dp

    def own_rows(array):
        return lax.dynamic_slice_in_dim(array, d_at * piece, piece, 0).astype(F32)

    def gain_share(parts, gain):
        total = sum(jnp.sum(own_rows(w) * g, axis=1) for w, g in parts)
        total = (total / own_rows(gain)).reshape(nt, piece // nt)
        total = jnp.stack(
            [lax.dynamic_index_in_dim(total, t_at ^ k, 0, keepdims=False) for k in t_slots]
        )
        for bit in t_bits:
            part = total.shape[0] // 2
            total = total[:part] + swap(total[part:], "tensor", 1 << bit)
        return total[0]

    grad_gain1 = gain_share([(w_query, grad_query), (keyval_weight, grad_keyval)], norm1_gain)
    grad_gain2 = gain_share([(w_gate, grad_gate), (w_up, grad_up)], norm2_gain)
    return (
        layer_out,
        grad_tokens,
        grad_gain1,
        grad_query,
        grad_keyval.reshape(piece, kv_local, 2 * hd),
        grad_outproj,
        grad_gain2,
        grad_gate,
        grad_up,
        grad_down,
    )


def solution(mesh):
    placed = (
        P(None, "dp", None),
        P(None, "dp"),
        P(),
        P(None, "tensor"),
        P(None, "tensor", None),
        P("tensor", None),
        P(),
        P(None, "tensor"),
        P(None, "tensor"),
        P("tensor", None),
        P(None, "dp", None),
    )
    return jax.shard_map(
        body,
        mesh=mesh,
        in_specs=placed,
        out_specs=(
            P(None, ("dp", "tensor"), None),
            P(None, ("dp", "tensor"), None),
            P(("dp", "tensor")),
            P("dp", "tensor"),
            P("dp", "tensor", None),
            P("tensor", "dp"),
            P(("dp", "tensor")),
            P("dp", "tensor"),
            P("dp", "tensor"),
            P("tensor", "dp"),
        ),
        check_vma=False,
    )
```

```python
import math

import jax
import jax.numpy as jnp
from jax import lax
from jax.experimental import pallas as pl
from jax.experimental.pallas import tpu as pltpu
from jax.sharding import PartitionSpec as P

EPS = 1e-05
SCALE = 0.015625
RESID = 0.22
THETA = 10000000.0
NEG = -1e30
PAD = 16
VMEM = 56 * 1024 * 1024
F32 = jnp.float32
BF16 = jnp.bfloat16
NT = (((1,), (1,)), ((), ()))
TN = (((0,), (0,)), ((), ()))


def dot(a, b, dims=None):
    if dims is None:
        return jnp.dot(a, b, preferred_element_type=F32)
    return lax.dot_general(a, b, dims, preferred_element_type=F32)


def params():
    return pltpu.CompilerParams(vmem_limit_bytes=VMEM)


def cost(flops, nbytes):
    return pl.CostEstimate(flops=int(flops) // 1024, bytes_accessed=int(nbytes) // 1024, transcendentals=0)


def slot_order(bits):
    slots = [0]
    for bit in reversed(bits):
        slots = slots + [k ^ (1 << bit) for k in slots]
    return slots


def swap(value, axis, distance, up=False):
    pairs = [(i, i ^ distance) for i in range(lax.axis_size(axis))]
    return lax.ppermute(value, axis, [(i, j) for i, j in pairs if j > i or not up])


def rope_tables(positions, head_dim):
    half = head_dim // 2
    inverse = jnp.power(F32(THETA), -(jnp.arange(half).astype(F32) * (2.0 / head_dim)))
    angle = positions.astype(F32)[:, None] * inverse[None, :]
    return (jnp.cos(angle), jnp.sin(angle))


def rotate_lanes(x, cosine, sine, half):
    width = x.shape[1]
    lane = lax.broadcasted_iota(jnp.int32, x.shape, 1)
    ahead = pltpu.roll(x, width - half, 1)
    behind = pltpu.roll(x, half, 1)
    partner = jnp.where((lane & (2 * half - 1)) < half, ahead, behind)
    times = width // cosine.shape[1]
    if times > 1:
        cosine = jnp.concatenate([cosine] * times, 1)
        sine = jnp.concatenate([sine] * times, 1)
    return x * cosine + partner * sine


def whole(array):
    rank = array.ndim
    return pl.BlockSpec(array.shape, lambda *_: (0,) * rank)


def norm_keyval(tokens, seg_ids, gain, weight, cosine, sine, core, half, split):
    seqs, block, width = tokens.shape
    out = weight.shape[1]
    share = block // (2 * split)

    def kernel(at, tok_ref, seg_ref, gain_ref, w_ref, cos_ref, sin_ref, n_ref, a_ref, b_ref):
        pieces = []
        for rel in range(2):
            for x in range(split):
                begin = pl.multiple_of((2 * x + (at[0] ^ rel)) * share, share)
                pieces.append(tok_ref[0, pl.ds(begin, share), :])
        xf = jnp.concatenate(pieces, 0).astype(F32)
        scale = lax.rsqrt(jnp.mean(xf * xf, axis=-1, keepdims=True) + EPS)
        normed = (xf * scale * gain_ref[...]).astype(BF16)
        n_ref[...] = normed.reshape(n_ref.shape)
        raw = dot(normed, w_ref[...])
        keyval = rotate_lanes(raw, cos_ref[...], sin_ref[...], half).astype(BF16)
        a_ref[0, : block // 2, :] = keyval[: block // 2]
        b_ref[0] = keyval[block // 2 :]
        lane = lax.broadcasted_iota(jnp.int32, (PAD, out), 1)
        row = jnp.zeros((PAD, out), F32)
        for v in range(3):
            count = jnp.sum(jnp.where(seg_ref[0] == v, 1.0, 0.0))
            row = jnp.where(lane == v, count, row)
        a_ref[0, block // 2 :, :] = row.astype(BF16)

    return pl.pallas_call(
        kernel,
        grid_spec=pltpu.PrefetchScalarGridSpec(
            num_scalar_prefetch=1,
            grid=(seqs,),
            in_specs=[
                pl.BlockSpec((1, block, width), lambda s, at: (s, 0, 0)),
                pl.BlockSpec((1, 1, block), lambda s, at: (s, 0, 0)),
                pl.BlockSpec((1, width), lambda s, at: (0, 0)),
                whole(weight),
                whole(cosine),
                whole(sine),
            ],
            out_specs=[
                pl.BlockSpec((2, split, 1, share, width), lambda s, at: (0, 0, s, 0, 0)),
                pl.BlockSpec((1, block // 2 + PAD, out), lambda s, at: (s, 0, 0)),
                pl.BlockSpec((1, block // 2, out), lambda s, at: (s, 0, 0)),
            ],
        ),
        out_shape=[
            jax.ShapeDtypeStruct((2, split, seqs, share, width), BF16),
            jax.ShapeDtypeStruct((seqs, block // 2 + PAD, out), BF16),
            jax.ShapeDtypeStruct((seqs, block // 2, out), BF16),
        ],
        compiler_params=params(),
        cost_estimate=cost(2 * seqs * block * width * out, 4 * seqs * block * width),
        name="norm_keyval",
    )(core, tokens, seg_ids[:, None, :], gain.reshape(1, width), weight, cosine, sine)


def project_query(normed, weight, cosine, sine, half):
    _, split, seqs, share, width = normed.shape
    block = 2 * split * share
    out = weight.shape[1]

    def kernel(n_ref, w_ref, cos_ref, sin_ref, q_ref):
        raw = dot(n_ref[...].reshape(block, width), w_ref[...])
        q_ref[0] = rotate_lanes(raw, cos_ref[...], sin_ref[...], half).astype(BF16)

    return pl.pallas_call(
        kernel,
        grid=(seqs,),
        in_specs=[
            pl.BlockSpec((2, split, 1, share, width), lambda s: (0, 0, s, 0, 0)),
            whole(weight),
            whole(cosine),
            whole(sine),
        ],
        out_specs=pl.BlockSpec((1, block, out), lambda s: (s, 0, 0)),
        out_shape=jax.ShapeDtypeStruct((seqs, block, out), BF16),
        compiler_params=params(),
        cost_estimate=cost(2 * seqs * block * width * out, 2 * seqs * block * width),
        name="project_query",
    )(normed, weight, cosine, sine)


def stacked_lanes(x, group, hd, low):
    rows = x.shape[1]
    flat = jnp.concatenate([x[h * hd : (h + 1) * hd] for h in range(group)], 1)
    zero = jnp.zeros((hd, group * rows), flat.dtype)
    return jnp.concatenate([flat, zero] if low else [zero, flat], 0)


def stacked_rows(x, group, hd, low):
    parts = []
    for h in range(group):
        at = (h * hd) // (2 * hd) * (2 * hd)
        piece = x[:, at : at + 2 * hd]
        if (h % 2 == 0) != low:
            piece = pltpu.roll(piece, hd, 1)
        lane = lax.broadcasted_iota(jnp.int32, piece.shape, 1)
        parts.append(jnp.where((lane < hd) == low, piece, 0.0))
    return jnp.concatenate(parts, 0)


def keyval_of(chunk, sc, base, refs, blocks, half):
    parts = []
    for low, high, table in ((refs[0], refs[1], 0), (refs[2], refs[3], blocks)):
        at = sc[base + table + chunk]
        one = low[jnp.minimum(at, blocks // 2 - 1), 0, :half, :]
        two = high[jnp.maximum(at - blocks // 2, 0), 0, :half, :]
        parts.append(jnp.where(at < blocks // 2, one, two))
    return jnp.concatenate(parts, 0)


def keyval_specs(blocks, half, width):
    return [
        pl.BlockSpec((blocks // 2, 1, rows, width), lambda s, h, sc: (0, s, 0, h))
        for rows in (half + PAD, half + PAD, half, half)
    ]


def mask_bias(chunk, block, position_block, doc_start, core, share, group):
    half = block // 2

    def place(axis):
        row = lax.broadcasted_iota(jnp.int32, (block, block), axis)
        rel = jnp.where(row >= half, 1, 0)
        row = row - half * rel
        return (row // share * 2 + (rel ^ core)) * share + row % share

    key_pos = chunk * block + place(0)
    query_pos = position_block * block + place(1)
    visible = (key_pos >= doc_start) & (key_pos <= query_pos)
    bias = jnp.where(visible, 0.0, NEG)
    return jnp.concatenate([bias] * group, 1)


def attend(query, keyval_all, doc_start, scalars, kv_local, hd, split):
    seqs, block, q_width = query.shape
    blocks = 2 * keyval_all[0].shape[0]
    group = q_width // kv_local // hd
    wide = group * block
    share = block // (2 * split)

    base = 2 + 2 * seqs
    half = block // 2

    def kernel(sc, q_ref, *refs):
        kv_refs, (doc_ref, keep_ref, send_ref, lse_ref, acc) = refs[:4], refs[4:]
        seq = pl.program_id(0)
        mine = sc[0]
        core = sc[1]
        start = sc[2 + seq]
        clear = sc[2 + seqs + seq]
        q_lanes = stacked_lanes((q_ref[0].astype(F32) * SCALE).T.astype(BF16), group, hd, True)
        doc = doc_ref[0]

        def scores_of(chunk, masked):
            kv = keyval_of(chunk, sc, base, kv_refs, blocks, half)
            scores = dot(kv, q_lanes)
            if masked:
                scores = scores + mask_bias(chunk, block, mine, doc, core, share, group)
            return kv, scores

        kv, scores = scores_of(mine, True)
        peak = jnp.max(scores, axis=0, keepdims=True)
        probs = jnp.exp(scores - peak)
        total = jnp.sum(probs, axis=0, keepdims=True)
        acc[...] = dot(kv, probs.astype(BF16), TN)

        def step(masked):
            def run(chunk, carry):
                peak, total = carry
                kv, scores = scores_of(chunk, masked)
                higher = jnp.maximum(peak, jnp.max(scores, axis=0, keepdims=True))
                shrink = jnp.exp(peak - higher)
                probs = jnp.exp(scores - higher)
                total = total * shrink + jnp.sum(probs, axis=0, keepdims=True)
                acc[...] = acc[...] * shrink + dot(kv, probs.astype(BF16), TN)
                return higher, total

            return run

        carry = lax.fori_loop(start, clear, step(True), (peak, total))
        peak, total = lax.fori_loop(clear, mine, step(False), carry)
        lse_ref[0, 0] = peak + jnp.log(total)
        result = acc[hd:] / total
        result = jnp.concatenate([result[:, h * block : (h + 1) * block] for h in range(group)], 0)
        result = result.T.astype(BF16)
        keep_ref[...] = result[:half].reshape(keep_ref.shape)
        send_ref[...] = result[half:].reshape(send_ref.shape)

    return pl.pallas_call(
        kernel,
        grid_spec=pltpu.PrefetchScalarGridSpec(
            num_scalar_prefetch=1,
            grid=(seqs, kv_local),
            in_specs=[
                pl.BlockSpec((1, block, group * hd), lambda s, h, sc: (s, 0, h)),
                *keyval_specs(blocks, half, 2 * hd),
                pl.BlockSpec((1, 1, block), lambda s, h, sc: (s, 0, 0)),
            ],
            out_specs=[
                pl.BlockSpec((split, 1, share, group * hd), lambda s, h, sc: (0, s, 0, h)),
                pl.BlockSpec((split, 1, share, group * hd), lambda s, h, sc: (0, s, 0, h)),
                pl.BlockSpec((1, 1, 1, wide), lambda s, h, sc: (s, h, 0, 0)),
            ],
            scratch_shapes=[pltpu.VMEM((2 * hd, wide), F32)],
        ),
        out_shape=[
            jax.ShapeDtypeStruct((split, seqs, share, q_width), BF16),
            jax.ShapeDtypeStruct((split, seqs, share, q_width), BF16),
            jax.ShapeDtypeStruct((seqs, kv_local, 1, wide), F32),
        ],
        compiler_params=params(),
        cost_estimate=cost(
            8 * seqs * block * q_width * blocks * block, 4 * seqs * blocks * block * 2 * hd
        ),
        name="attend",
    )(scalars, query, *keyval_all, doc_start)


def attend_back(
    query, keyval_all, doc_start, attended, d_mixed, w_out, lse, cosine, sine, scalars, kv_local, hd
):
    seqs, block, q_width = query.shape
    split, _, share, _ = attended[0].shape
    width = w_out.shape[1]
    blocks = 2 * keyval_all[0].shape[0]
    group = q_width // kv_local // hd
    wide = group * block
    base = 2 + 2 * seqs
    half = block // 2

    def kernel(sc, q_ref, *refs):
        kv_refs, refs = refs[:4], refs[4:]
        doc_ref, ok_ref, os_ref, keep_ref, send_ref, w_ref, lse_ref, cos_ref, sin_ref = refs[:9]
        dqk_ref, dqs_ref, ako, aso, bko, bso, acc, ak_ref, as_ref, bk_ref, bs_ref = refs[9:]
        seq = pl.program_id(0)
        mine = sc[0]
        core = sc[1]
        start = sc[2 + seq]
        clear = sc[2 + seqs + seq]
        doc = doc_ref[0]
        q = q_ref[0].astype(F32) * SCALE
        mixed = jnp.concatenate(
            [keep_ref[...].reshape(half, width), send_ref[...].reshape(half, width)], 0
        )
        d_out = dot(mixed, w_ref[...], NT).astype(BF16).astype(F32)
        d_out_t = d_out.T
        q_lanes = stacked_lanes(q.T.astype(BF16), group, hd, True)
        attended = jnp.concatenate(
            [ok_ref[...].reshape(half, group * hd), os_ref[...].reshape(half, group * hd)], 0
        )
        o_lanes = d_out_t * attended.astype(F32).T
        delta = jnp.concatenate(
            [
                jnp.sum(o_lanes[h * hd : (h + 1) * hd], axis=0, keepdims=True)
                for h in range(group)
            ],
            1,
        )
        d_lanes = stacked_lanes(d_out_t.astype(BF16), group, hd, False)
        q_rows = stacked_rows(q, group, hd, True).astype(BF16)
        d_rows = stacked_rows(d_out, group, hd, False).astype(BF16)
        total = lse_ref[0, 0]
        acc[...] = jnp.zeros_like(acc)

        def put(chunk, value):
            for table, kept, sent, rows in (
                (0, ak_ref, as_ref, value[:half]),
                (blocks, bk_ref, bs_ref, value[half:]),
            ):
                at = sc[base + table + chunk]
                kept[jnp.minimum(at, blocks // 2)] = rows
                sent[jnp.where(at < blocks // 2, blocks // 2, at - blocks // 2)] = rows

        def work(chunk, masked):
            kv = keyval_of(chunk, sc, base, kv_refs, blocks, half)
            scores = dot(kv, q_lanes)
            if masked:
                scores = scores + mask_bias(chunk, block, mine, doc, core, share, group)
            probs = jnp.exp(scores - total)
            d_probs = dot(kv, d_lanes)
            d_scores = (probs * (d_probs - delta)).astype(BF16)
            d_kv = dot(probs.astype(BF16), d_rows) + dot(d_scores, q_rows)
            put(chunk, d_kv.astype(BF16))
            acc[...] += dot(kv, d_scores, TN)

        def clean(chunk, carry):
            put(chunk, jnp.zeros((block, 2 * hd), BF16))
            return carry

        def step(masked):
            def run(chunk, carry):
                work(chunk, masked)
                return carry

            return run

        lax.fori_loop(0, start, clean, 0)
        lax.fori_loop(start, clear, step(True), 0)
        lax.fori_loop(clear, mine, step(False), 0)
        work(mine, True)
        lax.fori_loop(mine + 1, blocks, clean, 0)
        for out, ref in ((ako, ak_ref), (aso, as_ref), (bko, bk_ref), (bso, bs_ref)):
            out[:, 0] = ref[: blocks // 2]
        dq = acc[:hd] * SCALE
        dq = jnp.concatenate([dq[:, h * block : (h + 1) * block] for h in range(group)], 0)
        dq = rotate_lanes(dq.T, cos_ref[...], -sin_ref[...], hd // 2)
        dq = dq.astype(BF16)
        dqk_ref[...] = dq[:half].reshape(dqk_ref.shape)
        dqs_ref[...] = dq[half:].reshape(dqs_ref.shape)

    ordered = pl.BlockSpec((split, 1, share, group * hd), lambda s, h, sc: (0, s, 0, h))
    mixed = pl.BlockSpec((split, 1, share, width), lambda s, h, sc: (0, s, 0, 0))
    parts = pl.BlockSpec((blocks // 2, 1, half, 2 * hd), lambda s, h, sc: (0, s, 0, h))
    return pl.pallas_call(
        kernel,
        grid_spec=pltpu.PrefetchScalarGridSpec(
            num_scalar_prefetch=1,
            grid=(seqs, kv_local),
            in_specs=[
                pl.BlockSpec((1, block, group * hd), lambda s, h, sc: (s, 0, h)),
                *keyval_specs(blocks, half, 2 * hd),
                pl.BlockSpec((1, 1, block), lambda s, h, sc: (s, 0, 0)),
                ordered,
                ordered,
                mixed,
                mixed,
                pl.BlockSpec((group * hd, width), lambda s, h, sc: (h, 0)),
                pl.BlockSpec((1, 1, 1, wide), lambda s, h, sc: (s, h, 0, 0)),
                whole(cosine),
                whole(sine),
            ],
            out_specs=[ordered] * 2 + [parts] * 4,
            scratch_shapes=[pltpu.VMEM((2 * hd, wide), F32)]
            + [pltpu.VMEM((blocks // 2 + 1, half, 2 * hd), BF16)] * 4,
        ),
        out_shape=[jax.ShapeDtypeStruct((split, seqs, share, q_width), BF16)] * 2
        + [jax.ShapeDtypeStruct((blocks // 2, seqs, half, kv_local * 2 * hd), BF16)] * 4,
        compiler_params=params(),
        cost_estimate=cost(
            20 * seqs * block * q_width * blocks * block, 8 * seqs * blocks * block * 2 * hd
        ),
        name="attend_back",
    )(scalars, query, *keyval_all, doc_start, *attended, *d_mixed, w_out, lse, cosine, sine)


def finish_keyval(first, last, cosine, sine, half, split):
    _, seqs, part, width = first[0].shape
    share = part // split
    terms = first + last
    count = len(first)

    def kernel(*refs):
        cos_ref, sin_ref, keep_ref, send_ref = refs[2 * count :]
        halves = [
            sum(ref[0, 0].astype(F32) for ref in some)
            for some in (refs[:count], refs[count : 2 * count])
        ]
        x = jnp.concatenate(halves, 0)
        x = rotate_lanes(x, cos_ref[...], -sin_ref[...], half).astype(BF16)
        keep_ref[...] = x[:part].reshape(keep_ref.shape)
        send_ref[...] = x[part:].reshape(send_ref.shape)

    out = pl.BlockSpec((split, 1, share, width), lambda s: (0, s, 0, 0))
    return pl.pallas_call(
        kernel,
        grid=(seqs,),
        in_specs=[pl.BlockSpec((1, 1, part, width), lambda s: (0, s, 0, 0))] * (2 * count)
        + [whole(cosine), whole(sine)],
        out_specs=[out] * 2,
        out_shape=[jax.ShapeDtypeStruct((split, seqs, share, width), BF16)] * 2,
        compiler_params=params(),
        cost_estimate=cost(0, 16 * seqs * part * width),
        name="finish_keyval",
    )(*terms, cosine, sine)


def mix(parts, weights, xf, gain):
    rows, deep = parts[0].shape
    width = weights[0].shape[1]
    count = len(parts)
    tile = math.gcd(width, 512)
    steps = width // tile

    def kernel(*refs):
        x_ref, gain_ref, resid_ref, n_ref, acc = refs[2 * count :]
        j = pl.program_id(0)
        left = jnp.concatenate([refs[k][...] for k in range(count)], 1)
        right = jnp.concatenate([refs[count + k][...] for k in range(count)], 0)
        resid = x_ref[...].astype(F32) + RESID * dot(left, right)
        resid_ref[...] = resid
        acc[j] = resid

        @pl.when(j == steps - 1)
        def _():
            square = sum(jnp.sum(acc[i] * acc[i], axis=-1, keepdims=True) for i in range(steps))
            scale = lax.rsqrt(square / width + EPS)
            for i in range(steps):
                at = pl.ds(i * tile, tile)
                n_ref[:, at] = (acc[i] * scale * gain_ref[:, at]).astype(BF16)

    fixed = lambda r, c: pl.BlockSpec((r, c), lambda j: (0, 0))
    return pl.pallas_call(
        kernel,
        grid=(steps,),
        in_specs=[fixed(rows, deep)] * count
        + [pl.BlockSpec((deep, tile), lambda j: (0, j))] * count
        + [pl.BlockSpec((rows, tile), lambda j: (0, j)), fixed(1, width)],
        out_specs=[pl.BlockSpec((rows, tile), lambda j: (0, j)), fixed(rows, width)],
        out_shape=[
            jax.ShapeDtypeStruct((rows, width), F32),
            jax.ShapeDtypeStruct((rows, width), BF16),
        ],
        scratch_shapes=[pltpu.VMEM((steps, rows, tile), F32)],
        compiler_params=params(),
        cost_estimate=cost(2 * rows * count * deep * width, 2 * count * deep * width),
        name="mix",
    )(*parts, *weights, xf, gain.reshape(1, width))


def resid_back(terms, resid, d_out, gain):
    rows, width = resid.shape
    tile = math.gcd(rows, 128)
    count = len(terms)

    def kernel(*refs):
        resid_ref, dy_ref, gain_ref, d_ref, mixed_ref = refs[count:]
        d_norm = sum(ref[...].astype(F32) for ref in refs[:count])
        resid = resid_ref[...]
        scale = lax.rsqrt(jnp.mean(resid * resid, axis=-1, keepdims=True) + EPS)
        scaled = gain_ref[...] * d_norm
        inner = jnp.mean(scaled * resid, axis=-1, keepdims=True)
        d_resid = dy_ref[...].astype(F32) + scale * scaled - resid * (scale**3 * inner)
        d_ref[...] = d_resid
        mixed_ref[...] = (RESID * d_resid).astype(BF16)

    one = pl.BlockSpec((tile, width), lambda i: (i, 0))
    return pl.pallas_call(
        kernel,
        grid=(rows // tile,),
        in_specs=[one] * (count + 2) + [pl.BlockSpec((1, width), lambda i: (0, 0))],
        out_specs=[one] * 2,
        out_shape=[
            jax.ShapeDtypeStruct((rows, width), F32),
            jax.ShapeDtypeStruct((rows, width), BF16),
        ],
        compiler_params=params(),
        cost_estimate=cost(0, 16 * rows * width),
        name="resid_back",
    )(*terms, resid, d_out, gain.reshape(1, width))


def hidden_back(d_ffn, w_down):
    rows, width = d_ffn.shape
    hidden = w_down.shape[0]
    tile = math.gcd(hidden, 512)

    def kernel(dy_ref, w_ref, o_ref):
        o_ref[...] = dot(dy_ref[...], w_ref[...], NT)

    return pl.pallas_call(
        kernel,
        grid=(hidden // tile,),
        in_specs=[whole(d_ffn), pl.BlockSpec((tile, width), lambda j: (j, 0))],
        out_specs=pl.BlockSpec((rows, tile), lambda j: (0, j)),
        out_shape=jax.ShapeDtypeStruct((rows, hidden), F32),
        compiler_params=params(),
        cost_estimate=cost(2 * rows * width * hidden, 2 * hidden * (rows + width)),
        name="hidden_back",
    )(d_ffn, w_down)


def feed_forward(normed, d_ffn, d_hidden, w_gate, w_up, w_down):
    back = d_hidden is not None
    part, width = normed[0].shape
    rows = 2 * part
    hidden = w_gate.shape[1]
    tile = math.gcd(hidden, 512)
    steps = hidden // tile

    sources = (d_hidden,) if back else d_ffn
    count = len(sources)

    def kernel(nk, ns, *refs):
        wg_ref, wu_ref, wd_ref, h_ref, dg_ref, du_ref, n_ref, *rest = refs[count:]
        at = pl.program_id(0)
        if not back:
            dy_ref, *rest = rest

        @pl.when(at == 0)
        def _():
            n_ref[:part] = nk[...]
            n_ref[part:] = ns[...]
            if not back:
                dy_ref[:part] = refs[0][...]
                dy_ref[part:] = refs[1][...]

        normed = n_ref[...]
        gate = dot(normed, wg_ref[...])
        up = dot(normed, wu_ref[...])
        d_hidden = refs[0][...] if back else dot(dy_ref[...], wd_ref[...], NT)
        sigma = jax.nn.sigmoid(gate)
        swish = gate * sigma
        hidden_tile = (swish * up).astype(BF16)
        d_gate = (d_hidden * up * sigma * (1.0 + gate * (1.0 - sigma))).astype(BF16)
        d_up = (d_hidden * swish).astype(BF16)
        h_ref[...] = hidden_tile
        dg_ref[...] = d_gate
        du_ref[...] = d_up
        if not back:
            return
        f_keep, f_send, dn_keep, dn_send, f_acc, n_acc = rest
        ffn = dot(hidden_tile, wd_ref[...])
        d_normed = dot(d_gate, wg_ref[...], NT) + dot(d_up, wu_ref[...], NT)

        @pl.when(at == 0)
        def _():
            f_acc[...] = ffn
            n_acc[...] = d_normed

        @pl.when(at > 0)
        def _():
            f_acc[...] += ffn
            n_acc[...] += d_normed

        @pl.when(at == steps - 1)
        def _():
            f_keep[...] = f_acc[:part].astype(BF16)
            f_send[...] = f_acc[part:].astype(BF16)
            dn_keep[...] = n_acc[:part].astype(BF16)
            dn_send[...] = n_acc[part:].astype(BF16)

    fixed = lambda r: pl.BlockSpec((r, width), lambda j: (0, 0))
    once = lambda r: pl.BlockSpec((r, width), lambda j: (0, 0), pipeline_mode=pl.Buffered(1))
    extra = 4 if back else 0
    return pl.pallas_call(
        kernel,
        grid=(steps,),
        in_specs=[once(part)] * 2
        + (
            [pl.BlockSpec((rows, tile), lambda j: (0, j))] if back else [once(part)] * 2
        )
        + [
            pl.BlockSpec((width, tile), lambda j: (0, j)),
            pl.BlockSpec((width, tile), lambda j: (0, j)),
            pl.BlockSpec((tile, width), lambda j: (j, 0)),
        ],
        out_specs=[pl.BlockSpec((rows, tile), lambda j: (0, j))] * 3
        + [fixed(rows)] * count
        + [fixed(part)] * extra,
        out_shape=[jax.ShapeDtypeStruct((rows, hidden), BF16)] * 3
        + [jax.ShapeDtypeStruct((rows, width), BF16)] * count
        + [jax.ShapeDtypeStruct((part, width), BF16)] * extra,
        scratch_shapes=[pltpu.VMEM((rows, width), F32)] * (extra // 2),
        compiler_params=params(),
        cost_estimate=cost(
            (10 if back else 6) * rows * width * hidden, 6 * width * hidden
        ),
        name="feed_forward" if back else "feed_forward_other",
    )(*normed, *sources, w_gate, w_up, w_down)


def grad_rows(lefts, rights, blocks_at, pieces, turned):
    count = blocks_at.shape[0]
    width = lefts[0].shape[1]
    piece = width // pieces
    columns = rights[0].shape[1]
    tile = math.gcd(columns, 512)
    pairs = len(lefts)
    half = count // 2 * piece

    def kernel(at, *refs):
        keep, send = refs[-2:]
        total = None
        for p in range(pairs):
            left = jnp.concatenate([refs[p * count + i][...] for i in range(count)], 1)
            right = refs[pairs * count + p][...]
            term = dot(right, left, TN) if turned else dot(left, right, TN)
            total = term if total is None else total + term
        keep[...] = total[:, :half] if turned else total[:half]
        send[...] = (total[:, half:] if turned else total[half:]).astype(BF16)

    specs = [
        pl.BlockSpec((left.shape[0], piece), lambda j, at, i=i: (0, at[i]))
        for left in lefts
        for i in range(count)
    ] + [pl.BlockSpec((right.shape[0], tile), lambda j, at: (0, j)) for right in rights]
    tokens = sum(left.shape[0] for left in lefts)
    return pl.pallas_call(
        kernel,
        grid_spec=pltpu.PrefetchScalarGridSpec(
            num_scalar_prefetch=1,
            grid=(columns // tile,),
            in_specs=specs,
            out_specs=[
                pl.BlockSpec((tile, half), lambda j, at: (j, 0))
                if turned
                else pl.BlockSpec((half, tile), lambda j, at: (0, j))
            ]
            * 2,
        ),
        out_shape=[
            jax.ShapeDtypeStruct((columns, half) if turned else (half, columns), dtype)
            for dtype in (F32, BF16)
        ],
        compiler_params=params(),
        cost_estimate=cost(4 * tokens * half * columns, 2 * tokens * (2 * half + columns)),
        name="grad_rows",
    )(blocks_at, *[left for left in lefts for _ in range(count)], *rights)


def body(
    tokens,
    seg_ids,
    norm1_gain,
    w_query,
    w_keyval,
    w_out,
    norm2_gain,
    w_gate,
    w_up,
    w_down,
    cotangent,
):
    seqs, block, width = tokens.shape
    kv_local = w_keyval.shape[1]
    hd = w_keyval.shape[2] // 2
    q_width = w_query.shape[1]
    kv_width = kv_local * 2 * hd
    dp = lax.axis_size("dp")
    nt = lax.axis_size("tensor")
    split = nt // 2
    share = block // nt
    piece = width // dp
    part = seqs * block // 2
    d_at = lax.axis_index("dp")
    t_at = lax.axis_index("tensor")
    core = t_at & 1
    x_at = t_at >> 1
    x_bits = list(range(1, nt.bit_length() - 1))
    d_bits = list(range(dp.bit_length() - 1))
    shared = d_bits[-1]
    near = d_bits[:-1]

    def ordered(array, rel):
        array = array.reshape(seqs, split, 2, share, *array.shape[2:])
        array = lax.dynamic_index_in_dim(array, core ^ rel, 2, keepdims=False)
        return jnp.swapaxes(array, 0, 1)

    def own(array):
        return lax.dynamic_index_in_dim(array.reshape(split, seqs, share, width), x_at, 0, False)

    def other_core(array):
        return swap(array, "tensor", 1)

    def flat(array):
        return array.reshape(-1, array.shape[-1])

    def tie(*arrays):
        return lax.optimization_barrier(arrays)

    def scatter_x_start(total):
        total = total.reshape(-1, seqs, share, width)
        for bit in reversed(x_bits):
            total = total.reshape(2, -1, seqs, share, width)
            mine = (t_at >> bit) & 1
            send = lax.dynamic_index_in_dim(total, mine ^ 1, 0, False).astype(BF16)
            total = lax.dynamic_index_in_dim(total, mine, 0, False).astype(F32)
            got = swap(send, "tensor", 1 << bit)
            if bit == x_bits[0]:
                return total[0], got[0]
            total = total + got.astype(F32)

    def gather_x(total):
        total = total[None]
        for bit in x_bits:
            got = swap(total, "tensor", 1 << bit)
            low = (t_at >> bit) & 1 == 0
            total = jnp.concatenate(
                [jnp.where(low, total, got), jnp.where(low, got, total)], 0
            )
        return total

    class Summing:
        def __init__(self, keep, send, order, axis=0):
            self.terms, self.send, self.order, self.axis = [keep], send, list(order), axis
            self.size, self.result = keep.shape[axis], None

        def start(self):
            self.terms.append(swap(self.send, "dp", 1 << self.order.pop(0)))

        def add(self):
            self.size //= 2
            self.send = self.total(self.size).astype(BF16)

        def end(self):
            self.result = self.total(0)

        def total(self, first):
            return sum(
                lax.slice_in_dim(term, first, first + self.size, 1, self.axis).astype(F32)
                for term in self.terms
            )

    def weight_grad(lefts, rights, order, turned=False):
        slots = d_at ^ jnp.array(slot_order(order), jnp.int32)
        keep, send = grad_rows(lefts, rights, slots, dp, turned)
        return Summing(keep, send, order, int(turned))

    place = jnp.arange(block).reshape(2, split, share)
    place = ((place // share) % split * 2 + (place // (block // 2) ^ core)) * share + place % share
    positions = d_at * block + place.reshape(block)
    cosine, sine = rope_tables(positions, hd)
    cos_q = jnp.concatenate([cosine] * 4, 1)
    sin_q = jnp.concatenate([-sine, sine] * 2, 1)
    ones = jnp.ones((block, hd), F32)
    cos_kv = jnp.concatenate([cosine, cosine, ones], 1)
    sin_kv = jnp.concatenate([-sine, sine, 0.0 * ones], 1)
    keyval_weight = w_keyval.reshape(width, kv_width)
    order_first = d_bits
    order_last = d_bits[1:-1] + d_bits[:1] + d_bits[-1:]
    d_share = lax.dynamic_slice_in_dim(cotangent, t_at * share, share, 1)
    d_share = swap((RESID * d_share.astype(F32)).astype(BF16), "dp", 1 << shared)
    first_normed, *keyval = norm_keyval(
        tokens, seg_ids, norm1_gain, keyval_weight, cos_kv, sin_kv, core[None], hd // 2, split
    )
    cot = jnp.concatenate([flat(ordered(cotangent, rel)) for rel in range(2)], 0)
    d_ffn = (RESID * cot.astype(F32)).astype(BF16)
    cot_keep = flat(ordered(cotangent, 0))
    xf_keep = flat(ordered(tokens, 0))
    d_ffn, keyval[0], keyval[1] = tie(d_ffn, keyval[0], keyval[1])
    keyval_all = [array[None] for array in keyval]
    for at in range(len(d_bits)):
        got = [
            swap(array, "dp", 1 << order[-1 - at], up=at == 0)
            for array, order in zip(keyval_all, (order_first, order_last))
        ]
        if at == 0:
            d_hidden = hidden_back(d_ffn, w_down)
            *got, d_hidden, d_share = tie(*got, d_hidden, d_share)
            weights = {0: w_out}
            for bit in x_bits:
                for k in list(weights):
                    weights[k | 1 << bit] = swap(weights[k], "tensor", 1 << bit)
        if at == len(d_bits) - 1:
            query = project_query(first_normed, w_query, cos_q, sin_q, hd // 2)
            *got, query = tie(*got, query)
        if at == len(d_bits) - 1:
            keyval_all = [array for pair in zip(keyval_all, got) for array in pair]
        else:
            keyval_all = [jnp.concatenate([a, b], 0) for a, b in zip(keyval_all, got)]
    for k in list(weights):
        weights[k | 1] = other_core(weights[k])

    before = sum(
        jnp.sum(array[:, :, block // 2, :3].astype(F32), axis=0) for array in keyval_all[:2]
    ).astype(jnp.int32)
    seg_ordered = jnp.stack([ordered(seg_ids, rel) for rel in range(2)])
    seg_ordered = seg_ordered.transpose(2, 0, 1, 3).reshape(seqs, block)
    doc_start = jnp.sum(
        jnp.where(seg_ordered[:, :, None] > jnp.arange(3), before[:, None, :], 0), axis=2
    )
    start = jnp.min(doc_start, axis=1) // block
    clear = jnp.clip((jnp.max(doc_start, axis=1) + block - 1) // block, start, d_at)

    def slot_of(order):
        slots = slot_order(order)
        table = jnp.array([slots.index(k) for k in range(dp)], jnp.int32)
        return table[d_at ^ jnp.arange(dp)]

    scalars = jnp.concatenate(
        [d_at[None], core[None], start, clear, slot_of(order_first), slot_of(order_last)]
    ).astype(jnp.int32)
    doc_start = doc_start[:, None, :]
    attended_keep, attended_send, lse = attend(
        query, keyval_all, doc_start, scalars, kv_local, hd, split
    )
    parts = {0: flat(attended_keep), 1: other_core(flat(attended_send))}
    for bit in x_bits:
        for k in list(parts):
            parts[k | 1 << bit] = swap(parts[k], "tensor", 1 << bit)
    groups = sorted(parts)
    resid, second_keep = mix(
        [parts[k] for k in groups], [weights[k] for k in groups], xf_keep, norm2_gain
    )
    second_send = other_core(second_keep)
    second_other = swap(second_keep, "dp", 1 << shared)
    d_share, second_send = tie(d_share, second_send)
    d_ffn_other = flat(gather_x(d_share))
    hidden, d_gate, d_up, second, ffn_keep, ffn_send, d_keep, d_send = feed_forward(
        (second_keep, second_send), None, d_hidden, w_gate, w_up, w_down
    )
    second_other, d_ffn_other, d_keep = tie(second_other, d_ffn_other, d_keep)
    d_part = (d_keep.astype(F32) + other_core(d_send).astype(F32)).astype(BF16)
    terms = [d_part]
    for bit in x_bits:
        if len(terms) > 1:
            terms = [sum(term.astype(F32) for term in terms).astype(BF16)]
        terms = [terms[0], swap(terms[0], "tensor", 1 << bit)]
    second_others = (second_other, other_core(second_other))
    d_ffn_others = (d_ffn_other, other_core(d_ffn_other))
    ffn_sum = (ffn_keep.astype(F32) + other_core(ffn_send).astype(F32)).astype(BF16)
    second_other, ffn_sum, terms[0] = tie(second_other, ffn_sum, terms[0])
    second_others = (second_other, second_others[1])
    hidden_o, d_gate_o, d_up_o, second_o, d_ffn_o = feed_forward(
        second_others, d_ffn_others, None, w_gate, w_up, w_down
    )
    resid, hidden_o = tie(resid, hidden_o)
    chain = [resid]

    def step(*arrays):
        *arrays, chain[0] = tie(*arrays, chain[0])
        return arrays if len(arrays) > 1 else arrays[0]

    def done(*arrays):
        *arrays, chain[0] = tie(*arrays, chain[0])
        return arrays if len(arrays) > 1 else arrays[0]

    def arrive(*sums):
        for one in sums:
            one.terms[-1] = step(one.terms[-1])

    def more(*sums):
        for one in sums:
            if one.order:
                one.add()
                one.send = done(one.send)
                one.start()
            else:
                one.end()
                one.result = done(one.result)

    terms = step(*terms) if len(terms) > 1 else [step(*terms)]
    ffn, ffn_got = scatter_x_start(step(ffn_sum))
    d_resid, d_mixed_keep = done(*resid_back(terms, resid, cot_keep, norm2_gain))
    d_mixed_send = other_core(d_mixed_keep)
    d_gate = step(d_gate)
    gate = weight_grad([second, second_o], [d_gate, d_gate_o], near)
    gate.send = done(gate.send)
    gate.start()
    d_up = step(d_up)
    up = weight_grad([second, second_o], [d_up, d_up_o], near[1:] + near[:1])
    up.send = done(up.send)
    up.start()
    d_mixed_send, ffn_got = step(d_mixed_send, ffn_got)
    out = weight_grad(
        [d_mixed_keep, d_mixed_send], [flat(attended_keep), flat(attended_send)], order_last, True
    )
    out.send = done(out.send)
    out.start()
    hidden = step(hidden)
    down = weight_grad([d_ffn, d_ffn_o], [hidden, hidden_o], near, True)
    down.send = done(down.send)
    down.start()
    query = step(query)
    tokens_of = (split, seqs, share, width)
    d_query_keep, d_query_send, *d_keyval = done(
        *attend_back(
            query,
            keyval_all,
            doc_start,
            (attended_keep, attended_send),
            (d_mixed_keep.reshape(tokens_of), d_mixed_send.reshape(tokens_of)),
            w_out,
            lse,
            cos_q,
            sin_q,
            scalars,
            kv_local,
            hd,
        )
    )
    d_query_keep, d_query_send = flat(d_query_keep), flat(d_query_send)
    kv_first = Summing(d_keyval[0], d_keyval[1], order_first)
    kv_last = Summing(d_keyval[2], d_keyval[3], order_last)
    arrive(gate, out)
    kv_first.start()
    kv_last.start()
    arrive(up)
    first_normed = first_normed.reshape(2, part, width)
    d_query_keep = step(d_query_keep)
    grad_q = weight_grad([first_normed[0], first_normed[1]], [d_query_keep, d_query_send], d_bits)
    grad_q.send = done(grad_q.send)
    d_query_keep = step(d_query_keep)
    back_send, back_keep = done(dot(d_query_send, w_query, NT), dot(d_query_keep, w_query, NT))
    arrive(down, kv_first, kv_last)
    more(kv_first, kv_last)
    more(gate, up, out)
    arrive(kv_first, kv_last)
    more(kv_first, kv_last)
    more(down)
    arrive(gate, up, out)
    more(gate, up)
    for _ in range(3, len(d_bits)):
        arrive(kv_first, kv_last)
        more(kv_first, kv_last)
    arrive(kv_first, kv_last)
    d_keyval_keep, d_keyval_send = (
        flat(array)
        for array in done(
            *finish_keyval(kv_first.terms, kv_last.terms, cos_kv, sin_kv, hd // 2, split)
        )
    )
    back_send = done((back_send + dot(d_keyval_send, keyval_weight, NT)).astype(BF16))
    back_got = other_core(back_send)
    grad_q.start()
    d_keyval_keep = step(d_keyval_keep)
    grad_kv = weight_grad(
        [first_normed[0], first_normed[1]], [d_keyval_keep, d_keyval_send], order_last
    )
    grad_kv.send = done(grad_kv.send)
    grad_kv.start()
    more(out)
    back_got = step(back_got)
    back_keep = back_keep + dot(d_keyval_keep, keyval_weight, NT) + back_got.astype(F32)
    back_keep = done(back_keep)
    d_norm1, back_got = scatter_x_start(back_keep)
    arrive(down, grad_q)
    more(down, grad_q)
    arrive(grad_kv)
    more(grad_kv)
    d_norm1 = d_norm1 + step(back_got).astype(F32)
    xf_share = own(xf_keep).astype(F32)
    scale1 = lax.rsqrt(jnp.mean(xf_share * xf_share, axis=-1, keepdims=True) + EPS)
    scaled = norm1_gain * d_norm1
    grad_tokens = done(
        own(d_resid)
        + scale1 * scaled
        - xf_share * scale1**3 * jnp.mean(scaled * xf_share, axis=-1, keepdims=True)
    )
    live = [out, gate, up, down, grad_q, grad_kv]
    while live := [rows for rows in live if rows.result is None]:
        for rows in live:
            arrive(rows)
            more(rows)
    grad_gate, grad_up, grad_down = gate.result, up.result, down.result
    grad_outproj, grad_query, grad_keyval = out.result, grad_q.result, grad_kv.result
    ffn = ffn.astype(F32) + ffn_got.astype(F32)
    layer_out = (own(chain[0]) + RESID * ffn).astype(BF16)
    def own_rows(array):
        return lax.dynamic_slice_in_dim(array, d_at * piece, piece, 0).astype(F32)

    def gain_share(parts, gain):
        total = sum(jnp.sum(own_rows(w) * g, axis=1) for w, g in parts)
        total = (total / own_rows(gain)).reshape(nt, piece // nt)
        for bit in reversed([0] + x_bits):
            total = total.reshape(2, -1, piece // nt)
            mine = (t_at >> bit) & 1
            send = lax.dynamic_index_in_dim(total, mine ^ 1, 0, False)
            total = lax.dynamic_index_in_dim(total, mine, 0, False)
            total = total + swap(send, "tensor", 1 << bit)
        return total[0]

    grad_gain1 = gain_share([(w_query, grad_query), (keyval_weight, grad_keyval)], norm1_gain)
    grad_gain2 = gain_share([(w_gate, grad_gate), (w_up, grad_up)], norm2_gain)
    return (
        layer_out,
        grad_tokens,
        grad_gain1,
        grad_query,
        grad_keyval.reshape(piece, kv_local, 2 * hd),
        grad_outproj,
        grad_gain2,
        grad_gate,
        grad_up,
        grad_down,
    )


def solution(mesh):
    placed = (
        P(None, "dp", None),
        P(None, "dp"),
        P(),
        P(None, "tensor"),
        P(None, "tensor", None),
        P("tensor", None),
        P(),
        P(None, "tensor"),
        P(None, "tensor"),
        P("tensor", None),
        P(None, "dp", None),
    )
    return jax.shard_map(
        body,
        mesh=mesh,
        in_specs=placed,
        out_specs=(
            P(None, ("dp", "tensor"), None),
            P(None, ("dp", "tensor"), None),
            P(("dp", "tensor")),
            P("dp", "tensor"),
            P("dp", "tensor", None),
            P("tensor", "dp"),
            P(("dp", "tensor")),
            P("dp", "tensor"),
            P("dp", "tensor"),
            P("tensor", "dp"),
        ),
        check_vma=False,
    )
```

```python
import math

import jax
import jax.numpy as jnp
from jax import lax
from jax.experimental import pallas as pl
from jax.experimental.pallas import tpu as pltpu
from jax.sharding import PartitionSpec as P

EPS = 1e-05
SCALE = 0.015625
RESID = 0.22
THETA = 10000000.0
NEG = -1e30
PAD = 16
VMEM = 56 * 1024 * 1024
F32 = jnp.float32
BF16 = jnp.bfloat16
NT = (((1,), (1,)), ((), ()))
TN = (((0,), (0,)), ((), ()))


def dot(a, b, dims=None):
    if dims is None:
        return jnp.dot(a, b, preferred_element_type=F32)
    return lax.dot_general(a, b, dims, preferred_element_type=F32)


def params():
    return pltpu.CompilerParams(vmem_limit_bytes=VMEM)


def cost(flops, nbytes):
    return pl.CostEstimate(flops=int(flops) // 1024, bytes_accessed=int(nbytes) // 1024, transcendentals=0)


def slot_order(bits):
    slots = [0]
    for bit in reversed(bits):
        slots = slots + [k ^ (1 << bit) for k in slots]
    return slots


def swap(value, axis, distance, up=False):
    pairs = [(i, i ^ distance) for i in range(lax.axis_size(axis))]
    return lax.ppermute(value, axis, [(i, j) for i, j in pairs if j > i or not up])


def rope_tables(positions, head_dim):
    half = head_dim // 2
    inverse = jnp.power(F32(THETA), -(jnp.arange(half).astype(F32) * (2.0 / head_dim)))
    angle = positions.astype(F32)[:, None] * inverse[None, :]
    return (jnp.cos(angle), jnp.sin(angle))


def rotate_lanes(x, cosine, sine, half):
    width = x.shape[1]
    lane = lax.broadcasted_iota(jnp.int32, x.shape, 1)
    ahead = pltpu.roll(x, width - half, 1)
    behind = pltpu.roll(x, half, 1)
    partner = jnp.where((lane & (2 * half - 1)) < half, ahead, behind)
    times = width // cosine.shape[1]
    if times > 1:
        cosine = jnp.concatenate([cosine] * times, 1)
        sine = jnp.concatenate([sine] * times, 1)
    return x * cosine + partner * sine


def whole(array):
    rank = array.ndim
    return pl.BlockSpec(array.shape, lambda *_: (0,) * rank)


def norm_keyval(tokens, seg_ids, gain, weight, cosine, sine, core, half, split):
    seqs, block, width = tokens.shape
    out = weight.shape[1]
    share = block // (2 * split)

    def kernel(at, tok_ref, seg_ref, gain_ref, w_ref, cos_ref, sin_ref, n_ref, a_ref, b_ref):
        pieces = []
        for rel in range(2):
            for x in range(split):
                begin = pl.multiple_of((2 * x + (at[0] ^ rel)) * share, share)
                pieces.append(tok_ref[0, pl.ds(begin, share), :])
        xf = jnp.concatenate(pieces, 0).astype(F32)
        scale = lax.rsqrt(jnp.mean(xf * xf, axis=-1, keepdims=True) + EPS)
        normed = (xf * scale * gain_ref[...]).astype(BF16)
        n_ref[...] = normed.reshape(n_ref.shape)
        raw = dot(normed, w_ref[...])
        keyval = rotate_lanes(raw, cos_ref[...], sin_ref[...], half).astype(BF16)
        a_ref[0, : block // 2, :] = keyval[: block // 2]
        b_ref[0] = keyval[block // 2 :]
        lane = lax.broadcasted_iota(jnp.int32, (PAD, out), 1)
        row = jnp.zeros((PAD, out), F32)
        for v in range(3):
            count = jnp.sum(jnp.where(seg_ref[0] == v, 1.0, 0.0))
            row = jnp.where(lane == v, count, row)
        a_ref[0, block // 2 :, :] = row.astype(BF16)

    return pl.pallas_call(
        kernel,
        grid_spec=pltpu.PrefetchScalarGridSpec(
            num_scalar_prefetch=1,
            grid=(seqs,),
            in_specs=[
                pl.BlockSpec((1, block, width), lambda s, at: (s, 0, 0)),
                pl.BlockSpec((1, 1, block), lambda s, at: (s, 0, 0)),
                pl.BlockSpec((1, width), lambda s, at: (0, 0)),
                whole(weight),
                whole(cosine),
                whole(sine),
            ],
            out_specs=[
                pl.BlockSpec((2, split, 1, share, width), lambda s, at: (0, 0, s, 0, 0)),
                pl.BlockSpec((1, block // 2 + PAD, out), lambda s, at: (s, 0, 0)),
                pl.BlockSpec((1, block // 2, out), lambda s, at: (s, 0, 0)),
            ],
        ),
        out_shape=[
            jax.ShapeDtypeStruct((2, split, seqs, share, width), BF16),
            jax.ShapeDtypeStruct((seqs, block // 2 + PAD, out), BF16),
            jax.ShapeDtypeStruct((seqs, block // 2, out), BF16),
        ],
        compiler_params=params(),
        cost_estimate=cost(2 * seqs * block * width * out, 4 * seqs * block * width),
        name="norm_keyval",
    )(core, tokens, seg_ids[:, None, :], gain.reshape(1, width), weight, cosine, sine)


def project_query(normed, weight, cosine, sine, half):
    _, split, seqs, share, width = normed.shape
    block = 2 * split * share
    out = weight.shape[1]

    def kernel(n_ref, w_ref, cos_ref, sin_ref, q_ref):
        raw = dot(n_ref[...].reshape(block, width), w_ref[...])
        q_ref[0] = rotate_lanes(raw, cos_ref[...], sin_ref[...], half).astype(BF16)

    return pl.pallas_call(
        kernel,
        grid=(seqs,),
        in_specs=[
            pl.BlockSpec((2, split, 1, share, width), lambda s: (0, 0, s, 0, 0)),
            whole(weight),
            whole(cosine),
            whole(sine),
        ],
        out_specs=pl.BlockSpec((1, block, out), lambda s: (s, 0, 0)),
        out_shape=jax.ShapeDtypeStruct((seqs, block, out), BF16),
        compiler_params=params(),
        cost_estimate=cost(2 * seqs * block * width * out, 2 * seqs * block * width),
        name="project_query",
    )(normed, weight, cosine, sine)


def stacked_lanes(x, group, hd, low):
    rows = x.shape[1]
    flat = jnp.concatenate([x[h * hd : (h + 1) * hd] for h in range(group)], 1)
    zero = jnp.zeros((hd, group * rows), flat.dtype)
    return jnp.concatenate([flat, zero] if low else [zero, flat], 0)


def stacked_rows(x, group, hd, low):
    parts = []
    for h in range(group):
        at = (h * hd) // (2 * hd) * (2 * hd)
        piece = x[:, at : at + 2 * hd]
        if (h % 2 == 0) != low:
            piece = pltpu.roll(piece, hd, 1)
        lane = lax.broadcasted_iota(jnp.int32, piece.shape, 1)
        parts.append(jnp.where((lane < hd) == low, piece, 0.0))
    return jnp.concatenate(parts, 0)


def keyval_of(last, count, sc, base, refs, blocks, half):
    parts = []
    for back in reversed(range(count)):
        chunk = jnp.maximum(last - back, 0) if back else last
        for low, high, table in ((refs[0], refs[1], 0), (refs[2], refs[3], blocks)):
            at = sc[base + table + chunk]
            one = low[jnp.minimum(at, blocks // 2 - 1), 0, :half, :]
            two = high[jnp.maximum(at - blocks // 2, 0), 0, :half, :]
            parts.append(jnp.where(at < blocks // 2, one, two))
    return jnp.concatenate(parts, 0)


def keyval_specs(blocks, half, width):
    return [
        pl.BlockSpec((blocks // 2, 1, rows, width), lambda s, h, sc: (0, s, 0, h))
        for rows in (half + PAD, half + PAD, half, half)
    ]


def mask_bias(last, count, block, position_block, doc_start, core, share, group):
    half = block // 2

    def place(axis):
        row = lax.broadcasted_iota(jnp.int32, (count * block, block), axis)
        chunk = row // block * block if axis == 0 else 0
        row = row - chunk
        rel = jnp.where(row >= half, 1, 0)
        row = row - half * rel
        return (row // share * 2 + (rel ^ core)) * share + row % share + chunk

    key_pos = (last - count + 1) * block + place(0)
    query_pos = position_block * block + place(1)
    visible = (key_pos >= doc_start) & (key_pos <= query_pos)
    bias = jnp.where(visible, 0.0, NEG)
    return jnp.concatenate([bias] * group, 1)


def pair_loops(mine, start, clear, visit, carry):
    whole_pairs = jnp.maximum(mine - 1 - clear, 0) // 2
    pairs = (mine - start) // 2
    run = lambda masked: lambda p, carry: visit(mine - 2 * p, masked, carry)
    carry = lax.fori_loop(1, 1 + whole_pairs, run(False), carry)
    return lax.fori_loop(1 + whole_pairs, 1 + pairs, run(True), carry)


def attend(query, keyval_all, doc_start, scalars, kv_local, hd, split):
    seqs, block, q_width = query.shape
    blocks = 2 * keyval_all[0].shape[0]
    group = q_width // kv_local // hd
    wide = group * block
    share = block // (2 * split)

    base = 2 + 2 * seqs
    half = block // 2

    def kernel(sc, q_ref, *refs):
        kv_refs, (doc_ref, keep_ref, send_ref, lse_ref, acc) = refs[:4], refs[4:]
        seq = pl.program_id(0)
        mine = sc[0]
        core = sc[1]
        start = sc[2 + seq]
        clear = sc[2 + seqs + seq]
        q_lanes = stacked_lanes((q_ref[0].astype(F32) * SCALE).T.astype(BF16), group, hd, True)
        doc = doc_ref[0]

        def scores_of(last, masked):
            kv = keyval_of(last, 2, sc, base, kv_refs, blocks, half)
            scores = dot(kv, q_lanes)
            if masked:
                scores = scores + mask_bias(last, 2, block, mine, doc, core, share, group)
            return kv, scores

        kv, scores = scores_of(mine, True)
        peak = jnp.max(scores, axis=0, keepdims=True)
        probs = jnp.exp(scores - peak)
        total = jnp.sum(probs, axis=0, keepdims=True)
        acc[...] = dot(kv, probs.astype(BF16), TN)

        def visit(last, masked, carry):
            peak, total = carry
            kv, scores = scores_of(last, masked)
            higher = jnp.maximum(peak, jnp.max(scores, axis=0, keepdims=True))
            shrink = jnp.exp(peak - higher)
            probs = jnp.exp(scores - higher)
            total = total * shrink + jnp.sum(probs, axis=0, keepdims=True)
            acc[...] = acc[...] * shrink + dot(kv, probs.astype(BF16), TN)
            return higher, total

        peak, total = pair_loops(mine, start, clear, visit, (peak, total))
        lse_ref[0, 0] = peak + jnp.log(total)
        result = acc[hd:] / total
        result = jnp.concatenate([result[:, h * block : (h + 1) * block] for h in range(group)], 0)
        result = result.T.astype(BF16)
        keep_ref[...] = result[:half].reshape(keep_ref.shape)
        send_ref[...] = result[half:].reshape(send_ref.shape)

    return pl.pallas_call(
        kernel,
        grid_spec=pltpu.PrefetchScalarGridSpec(
            num_scalar_prefetch=1,
            grid=(seqs, kv_local),
            in_specs=[
                pl.BlockSpec((1, block, group * hd), lambda s, h, sc: (s, 0, h)),
                *keyval_specs(blocks, half, 2 * hd),
                pl.BlockSpec((1, 1, block), lambda s, h, sc: (s, 0, 0)),
            ],
            out_specs=[
                pl.BlockSpec((split, 1, share, group * hd), lambda s, h, sc: (0, s, 0, h)),
                pl.BlockSpec((split, 1, share, group * hd), lambda s, h, sc: (0, s, 0, h)),
                pl.BlockSpec((1, 1, 1, wide), lambda s, h, sc: (s, h, 0, 0)),
            ],
            scratch_shapes=[pltpu.VMEM((2 * hd, wide), F32)],
        ),
        out_shape=[
            jax.ShapeDtypeStruct((split, seqs, share, q_width), BF16),
            jax.ShapeDtypeStruct((split, seqs, share, q_width), BF16),
            jax.ShapeDtypeStruct((seqs, kv_local, 1, wide), F32),
        ],
        compiler_params=params(),
        cost_estimate=cost(
            8 * seqs * block * q_width * blocks * block, 4 * seqs * blocks * block * 2 * hd
        ),
        name="attend",
    )(scalars, query, *keyval_all, doc_start)


def attend_back(
    query, keyval_all, doc_start, attended, d_mixed, w_out, lse, cosine, sine, scalars, kv_local, hd
):
    seqs, block, q_width = query.shape
    split, _, share, _ = attended[0].shape
    width = w_out.shape[1]
    blocks = 2 * keyval_all[0].shape[0]
    group = q_width // kv_local // hd
    wide = group * block
    base = 2 + 2 * seqs
    half = block // 2

    def kernel(sc, q_ref, *refs):
        kv_refs, refs = refs[:4], refs[4:]
        doc_ref, ok_ref, os_ref, keep_ref, send_ref, w_ref, lse_ref, cos_ref, sin_ref = refs[:9]
        dqk_ref, dqs_ref, ako, aso, bko, bso, acc, ak_ref, as_ref, bk_ref, bs_ref = refs[9:]
        seq = pl.program_id(0)
        mine = sc[0]
        core = sc[1]
        start = sc[2 + seq]
        clear = sc[2 + seqs + seq]
        doc = doc_ref[0]
        q = q_ref[0].astype(F32) * SCALE
        mixed = jnp.concatenate(
            [keep_ref[...].reshape(half, width), send_ref[...].reshape(half, width)], 0
        )
        d_out = dot(mixed, w_ref[...], NT).astype(BF16).astype(F32)
        d_out_t = d_out.T
        q_lanes = stacked_lanes(q.T.astype(BF16), group, hd, True)
        attended = jnp.concatenate(
            [ok_ref[...].reshape(half, group * hd), os_ref[...].reshape(half, group * hd)], 0
        )
        o_lanes = d_out_t * attended.astype(F32).T
        delta = jnp.concatenate(
            [
                jnp.sum(o_lanes[h * hd : (h + 1) * hd], axis=0, keepdims=True)
                for h in range(group)
            ],
            1,
        )
        d_lanes = stacked_lanes(d_out_t.astype(BF16), group, hd, False)
        q_rows = stacked_rows(q, group, hd, True).astype(BF16)
        d_rows = stacked_rows(d_out, group, hd, False).astype(BF16)
        total = lse_ref[0, 0]
        acc[...] = jnp.zeros_like(acc)

        def put(chunk, value):
            for table, kept, sent, rows in (
                (0, ak_ref, as_ref, value[:half]),
                (blocks, bk_ref, bs_ref, value[half:]),
            ):
                at = sc[base + table + chunk]
                kept[jnp.minimum(at, blocks // 2)] = rows
                sent[jnp.where(at < blocks // 2, blocks // 2, at - blocks // 2)] = rows

        def work(chunk, masked):
            kv = keyval_of(chunk, 1, sc, base, kv_refs, blocks, half)
            scores = dot(kv, q_lanes)
            if masked:
                scores = scores + mask_bias(chunk, 1, block, mine, doc, core, share, group)
            probs = jnp.exp(scores - total)
            d_probs = dot(kv, d_lanes)
            d_scores = (probs * (d_probs - delta)).astype(BF16)
            d_kv = dot(probs.astype(BF16), d_rows) + dot(d_scores, q_rows)
            put(chunk, d_kv.astype(BF16))
            acc[...] += dot(kv, d_scores, TN)

        def clean(chunk, carry):
            put(chunk, jnp.zeros((block, 2 * hd), BF16))
            return carry

        def step(masked):
            def run(chunk, carry):
                work(chunk, masked)
                return carry

            return run

        lax.fori_loop(0, start, clean, 0)
        lax.fori_loop(start, clear, step(True), 0)
        lax.fori_loop(clear, mine, step(False), 0)
        work(mine, True)
        lax.fori_loop(mine + 1, blocks, clean, 0)
        for out, ref in ((ako, ak_ref), (aso, as_ref), (bko, bk_ref), (bso, bs_ref)):
            out[:, 0] = ref[: blocks // 2]
        dq = acc[:hd] * SCALE
        dq = jnp.concatenate([dq[:, h * block : (h + 1) * block] for h in range(group)], 0)
        dq = rotate_lanes(dq.T, cos_ref[...], -sin_ref[...], hd // 2)
        dq = dq.astype(BF16)
        dqk_ref[...] = dq[:half].reshape(dqk_ref.shape)
        dqs_ref[...] = dq[half:].reshape(dqs_ref.shape)

    ordered = pl.BlockSpec((split, 1, share, group * hd), lambda s, h, sc: (0, s, 0, h))
    mixed = pl.BlockSpec((split, 1, share, width), lambda s, h, sc: (0, s, 0, 0))
    parts = pl.BlockSpec((blocks // 2, 1, half, 2 * hd), lambda s, h, sc: (0, s, 0, h))
    return pl.pallas_call(
        kernel,
        grid_spec=pltpu.PrefetchScalarGridSpec(
            num_scalar_prefetch=1,
            grid=(seqs, kv_local),
            in_specs=[
                pl.BlockSpec((1, block, group * hd), lambda s, h, sc: (s, 0, h)),
                *keyval_specs(blocks, half, 2 * hd),
                pl.BlockSpec((1, 1, block), lambda s, h, sc: (s, 0, 0)),
                ordered,
                ordered,
                mixed,
                mixed,
                pl.BlockSpec((group * hd, width), lambda s, h, sc: (h, 0)),
                pl.BlockSpec((1, 1, 1, wide), lambda s, h, sc: (s, h, 0, 0)),
                whole(cosine),
                whole(sine),
            ],
            out_specs=[ordered] * 2 + [parts] * 4,
            scratch_shapes=[pltpu.VMEM((2 * hd, wide), F32)]
            + [pltpu.VMEM((blocks // 2 + 1, half, 2 * hd), BF16)] * 4,
        ),
        out_shape=[jax.ShapeDtypeStruct((split, seqs, share, q_width), BF16)] * 2
        + [jax.ShapeDtypeStruct((blocks // 2, seqs, half, kv_local * 2 * hd), BF16)] * 4,
        compiler_params=params(),
        cost_estimate=cost(
            20 * seqs * block * q_width * blocks * block, 8 * seqs * blocks * block * 2 * hd
        ),
        name="attend_back",
    )(scalars, query, *keyval_all, doc_start, *attended, *d_mixed, w_out, lse, cosine, sine)


def finish_keyval(first, last, cosine, sine, half, split):
    _, seqs, part, width = first[0].shape
    share = part // split
    terms = first + last
    count = len(first)

    def kernel(*refs):
        cos_ref, sin_ref, keep_ref, send_ref = refs[2 * count :]
        halves = [
            sum(ref[0, 0].astype(F32) for ref in some)
            for some in (refs[:count], refs[count : 2 * count])
        ]
        x = jnp.concatenate(halves, 0)
        x = rotate_lanes(x, cos_ref[...], -sin_ref[...], half).astype(BF16)
        keep_ref[...] = x[:part].reshape(keep_ref.shape)
        send_ref[...] = x[part:].reshape(send_ref.shape)

    out = pl.BlockSpec((split, 1, share, width), lambda s: (0, s, 0, 0))
    return pl.pallas_call(
        kernel,
        grid=(seqs,),
        in_specs=[pl.BlockSpec((1, 1, part, width), lambda s: (0, s, 0, 0))] * (2 * count)
        + [whole(cosine), whole(sine)],
        out_specs=[out] * 2,
        out_shape=[jax.ShapeDtypeStruct((split, seqs, share, width), BF16)] * 2,
        compiler_params=params(),
        cost_estimate=cost(0, 16 * seqs * part * width),
        name="finish_keyval",
    )(*terms, cosine, sine)


def mix(parts, weights, xf, gain):
    rows, deep = parts[0].shape
    width = weights[0].shape[1]
    count = len(parts)
    tile = math.gcd(width, 512)
    steps = width // tile

    def kernel(*refs):
        x_ref, gain_ref, resid_ref, n_ref, acc = refs[2 * count :]
        j = pl.program_id(0)
        left = jnp.concatenate([refs[k][...] for k in range(count)], 1)
        right = jnp.concatenate([refs[count + k][...] for k in range(count)], 0)
        resid = x_ref[...].astype(F32) + RESID * dot(left, right)
        resid_ref[...] = resid
        acc[j] = resid

        @pl.when(j == steps - 1)
        def _():
            square = sum(jnp.sum(acc[i] * acc[i], axis=-1, keepdims=True) for i in range(steps))
            scale = lax.rsqrt(square / width + EPS)
            for i in range(steps):
                at = pl.ds(i * tile, tile)
                n_ref[:, at] = (acc[i] * scale * gain_ref[:, at]).astype(BF16)

    fixed = lambda r, c: pl.BlockSpec((r, c), lambda j: (0, 0))
    return pl.pallas_call(
        kernel,
        grid=(steps,),
        in_specs=[fixed(rows, deep)] * count
        + [pl.BlockSpec((deep, tile), lambda j: (0, j))] * count
        + [pl.BlockSpec((rows, tile), lambda j: (0, j)), fixed(1, width)],
        out_specs=[pl.BlockSpec((rows, tile), lambda j: (0, j)), fixed(rows, width)],
        out_shape=[
            jax.ShapeDtypeStruct((rows, width), F32),
            jax.ShapeDtypeStruct((rows, width), BF16),
        ],
        scratch_shapes=[pltpu.VMEM((steps, rows, tile), F32)],
        compiler_params=params(),
        cost_estimate=cost(2 * rows * count * deep * width, 2 * count * deep * width),
        name="mix",
    )(*parts, *weights, xf, gain.reshape(1, width))


def resid_back(terms, resid, d_out, gain):
    rows, width = resid.shape
    tile = math.gcd(rows, 128)
    count = len(terms)

    def kernel(*refs):
        resid_ref, dy_ref, gain_ref, d_ref, mixed_ref = refs[count:]
        d_norm = sum(ref[...].astype(F32) for ref in refs[:count])
        resid = resid_ref[...]
        scale = lax.rsqrt(jnp.mean(resid * resid, axis=-1, keepdims=True) + EPS)
        scaled = gain_ref[...] * d_norm
        inner = jnp.mean(scaled * resid, axis=-1, keepdims=True)
        d_resid = dy_ref[...].astype(F32) + scale * scaled - resid * (scale**3 * inner)
        d_ref[...] = d_resid
        mixed_ref[...] = (RESID * d_resid).astype(BF16)

    one = pl.BlockSpec((tile, width), lambda i: (i, 0))
    return pl.pallas_call(
        kernel,
        grid=(rows // tile,),
        in_specs=[one] * (count + 2) + [pl.BlockSpec((1, width), lambda i: (0, 0))],
        out_specs=[one] * 2,
        out_shape=[
            jax.ShapeDtypeStruct((rows, width), F32),
            jax.ShapeDtypeStruct((rows, width), BF16),
        ],
        compiler_params=params(),
        cost_estimate=cost(0, 16 * rows * width),
        name="resid_back",
    )(*terms, resid, d_out, gain.reshape(1, width))


def hidden_back(d_ffn, w_down):
    rows, width = d_ffn.shape
    hidden = w_down.shape[0]
    tile = math.gcd(hidden, 512)

    def kernel(dy_ref, w_ref, o_ref):
        o_ref[...] = dot(dy_ref[...], w_ref[...], NT)

    return pl.pallas_call(
        kernel,
        grid=(hidden // tile,),
        in_specs=[whole(d_ffn), pl.BlockSpec((tile, width), lambda j: (j, 0))],
        out_specs=pl.BlockSpec((rows, tile), lambda j: (0, j)),
        out_shape=jax.ShapeDtypeStruct((rows, hidden), F32),
        compiler_params=params(),
        cost_estimate=cost(2 * rows * width * hidden, 2 * hidden * (rows + width)),
        name="hidden_back",
    )(d_ffn, w_down)


def feed_forward(normed, d_ffn, d_hidden, w_gate, w_up, w_down):
    back = d_hidden is not None
    part, width = normed[0].shape
    rows = 2 * part
    hidden = w_gate.shape[1]
    tile = math.gcd(hidden, 512)
    steps = hidden // tile

    sources = (d_hidden,) if back else d_ffn
    count = len(sources)

    def kernel(nk, ns, *refs):
        wg_ref, wu_ref, wd_ref, h_ref, dg_ref, du_ref, n_ref, *rest = refs[count:]
        at = pl.program_id(0)
        if not back:
            dy_ref, *rest = rest

        @pl.when(at == 0)
        def _():
            n_ref[:part] = nk[...]
            n_ref[part:] = ns[...]
            if not back:
                dy_ref[:part] = refs[0][...]
                dy_ref[part:] = refs[1][...]

        normed = n_ref[...]
        gate = dot(normed, wg_ref[...])
        up = dot(normed, wu_ref[...])
        d_hidden = refs[0][...] if back else dot(dy_ref[...], wd_ref[...], NT)
        sigma = jax.nn.sigmoid(gate)
        swish = gate * sigma
        hidden_tile = (swish * up).astype(BF16)
        d_gate = (d_hidden * up * sigma * (1.0 + gate * (1.0 - sigma))).astype(BF16)
        d_up = (d_hidden * swish).astype(BF16)
        h_ref[...] = hidden_tile
        dg_ref[...] = d_gate
        du_ref[...] = d_up
        if not back:
            return
        f_keep, f_send, dn_keep, dn_send, f_acc, n_acc = rest
        ffn = dot(hidden_tile, wd_ref[...])
        d_normed = dot(d_gate, wg_ref[...], NT) + dot(d_up, wu_ref[...], NT)

        @pl.when(at == 0)
        def _():
            f_acc[...] = ffn
            n_acc[...] = d_normed

        @pl.when(at > 0)
        def _():
            f_acc[...] += ffn
            n_acc[...] += d_normed

        @pl.when(at == steps - 1)
        def _():
            f_keep[...] = f_acc[:part].astype(BF16)
            f_send[...] = f_acc[part:].astype(BF16)
            dn_keep[...] = n_acc[:part].astype(BF16)
            dn_send[...] = n_acc[part:].astype(BF16)

    fixed = lambda r: pl.BlockSpec((r, width), lambda j: (0, 0))
    once = lambda r: pl.BlockSpec((r, width), lambda j: (0, 0), pipeline_mode=pl.Buffered(1))
    extra = 4 if back else 0
    return pl.pallas_call(
        kernel,
        grid=(steps,),
        in_specs=[once(part)] * 2
        + (
            [pl.BlockSpec((rows, tile), lambda j: (0, j))] if back else [once(part)] * 2
        )
        + [
            pl.BlockSpec((width, tile), lambda j: (0, j)),
            pl.BlockSpec((width, tile), lambda j: (0, j)),
            pl.BlockSpec((tile, width), lambda j: (j, 0)),
        ],
        out_specs=[pl.BlockSpec((rows, tile), lambda j: (0, j))] * 3
        + [fixed(rows)] * count
        + [fixed(part)] * extra,
        out_shape=[jax.ShapeDtypeStruct((rows, hidden), BF16)] * 3
        + [jax.ShapeDtypeStruct((rows, width), BF16)] * count
        + [jax.ShapeDtypeStruct((part, width), BF16)] * extra,
        scratch_shapes=[pltpu.VMEM((rows, width), F32)] * (extra // 2),
        compiler_params=params(),
        cost_estimate=cost(
            (10 if back else 6) * rows * width * hidden, 6 * width * hidden
        ),
        name="feed_forward" if back else "feed_forward_other",
    )(*normed, *sources, w_gate, w_up, w_down)


def grad_rows(lefts, rights, blocks_at, pieces, turned, base=(), dtypes=(F32, BF16)):
    count = blocks_at.shape[0]
    width = lefts[0].shape[1]
    piece = width // pieces
    columns = rights[0].shape[1]
    tile = math.gcd(columns, 512)
    pairs = len(lefts)
    half = count // 2 * piece

    def kernel(at, *refs):
        keep, send = refs[-2:]
        total = None
        for p in range(pairs):
            left = jnp.concatenate([refs[p * count + i][...] for i in range(count)], 1)
            right = refs[pairs * count + p][...]
            term = dot(right, left, TN) if turned else dot(left, right, TN)
            total = term if total is None else total + term
        if base:
            total = total + jnp.concatenate(
                [refs[-4][...].astype(F32), refs[-3][...].astype(F32)], int(turned)
            )
        keep[...] = (total[:, :half] if turned else total[:half]).astype(dtypes[0])
        send[...] = (total[:, half:] if turned else total[half:]).astype(dtypes[1])

    specs = [
        pl.BlockSpec((left.shape[0], piece), lambda j, at, i=i: (0, at[i]))
        for left in lefts
        for i in range(count)
    ] + [pl.BlockSpec((right.shape[0], tile), lambda j, at: (0, j)) for right in rights]
    tokens = sum(left.shape[0] for left in lefts)
    halves = [
        pl.BlockSpec((tile, half), lambda j, at: (j, 0))
        if turned
        else pl.BlockSpec((half, tile), lambda j, at: (0, j))
    ] * 2
    return pl.pallas_call(
        kernel,
        grid_spec=pltpu.PrefetchScalarGridSpec(
            num_scalar_prefetch=1,
            grid=(columns // tile,),
            in_specs=specs + halves[: len(base)],
            out_specs=halves,
        ),
        out_shape=[
            jax.ShapeDtypeStruct((columns, half) if turned else (half, columns), dtype)
            for dtype in dtypes
        ],
        compiler_params=params(),
        cost_estimate=cost(4 * tokens * half * columns, 2 * tokens * (2 * half + columns)),
        name="grad_rows",
    )(blocks_at, *[left for left in lefts for _ in range(count)], *rights, *base)


def body(
    tokens,
    seg_ids,
    norm1_gain,
    w_query,
    w_keyval,
    w_out,
    norm2_gain,
    w_gate,
    w_up,
    w_down,
    cotangent,
):
    seqs, block, width = tokens.shape
    kv_local = w_keyval.shape[1]
    hd = w_keyval.shape[2] // 2
    q_width = w_query.shape[1]
    kv_width = kv_local * 2 * hd
    dp = lax.axis_size("dp")
    nt = lax.axis_size("tensor")
    split = nt // 2
    share = block // nt
    piece = width // dp
    part = seqs * block // 2
    d_at = lax.axis_index("dp")
    t_at = lax.axis_index("tensor")
    core = t_at & 1
    x_at = t_at >> 1
    x_bits = list(range(1, nt.bit_length() - 1))
    d_bits = list(range(dp.bit_length() - 1))
    shared = d_bits[-1]
    near = d_bits[:-1]

    def ordered(array, rel):
        array = array.reshape(seqs, split, 2, share, *array.shape[2:])
        array = lax.dynamic_index_in_dim(array, core ^ rel, 2, keepdims=False)
        return jnp.swapaxes(array, 0, 1)

    def own(array):
        return lax.dynamic_index_in_dim(array.reshape(split, seqs, share, width), x_at, 0, False)

    def other_core(array):
        return swap(array, "tensor", 1)

    def flat(array):
        return array.reshape(-1, array.shape[-1])

    def tie(*arrays):
        return lax.optimization_barrier(arrays)

    def scatter_x_start(total, keep_order=lambda array: array):
        total = total.reshape(-1, seqs, share, width)
        for bit in reversed(x_bits):
            total = total.reshape(2, -1, seqs, share, width)
            mine = (t_at >> bit) & 1
            send = lax.dynamic_index_in_dim(total, mine ^ 1, 0, False).astype(BF16)
            total = lax.dynamic_index_in_dim(total, mine, 0, False).astype(F32)
            got = swap(keep_order(send), "tensor", 1 << bit)
            if bit == x_bits[0]:
                return total[0], got[0]
            total = total + got.astype(F32)

    def gather_x(total):
        total = total[None]
        for bit in x_bits:
            got = swap(total, "tensor", 1 << bit)
            low = (t_at >> bit) & 1 == 0
            total = jnp.concatenate(
                [jnp.where(low, total, got), jnp.where(low, got, total)], 0
            )
        return total

    class Summing:
        def __init__(self, keep, send, order, axis=0):
            self.terms, self.send, self.order, self.axis = [keep], send, list(order), axis
            self.size, self.result = keep.shape[axis], None

        def start(self):
            self.terms.append(swap(self.send, "dp", 1 << self.order.pop(0)))

        def add(self):
            self.size //= 2
            self.send = self.total(self.size).astype(BF16)

        def end(self):
            self.result = self.total(0)

        def total(self, first):
            return sum(
                lax.slice_in_dim(term, first, first + self.size, 1, self.axis).astype(F32)
                for term in self.terms
            )

    def slots_of(order):
        return d_at ^ jnp.array(slot_order(order), jnp.int32)

    def weight_grad(lefts, rights, order, turned=False, base=()):
        keep, send = grad_rows(lefts, rights, slots_of(order), dp, turned, base)
        return Summing(keep, send, order, int(turned))

    place = jnp.arange(block).reshape(2, split, share)
    place = ((place // share) % split * 2 + (place // (block // 2) ^ core)) * share + place % share
    positions = d_at * block + place.reshape(block)
    cosine, sine = rope_tables(positions, hd)
    cos_q = jnp.concatenate([cosine] * 4, 1)
    sin_q = jnp.concatenate([-sine, sine] * 2, 1)
    ones = jnp.ones((block, hd), F32)
    cos_kv = jnp.concatenate([cosine, cosine, ones], 1)
    sin_kv = jnp.concatenate([-sine, sine, 0.0 * ones], 1)
    keyval_weight = w_keyval.reshape(width, kv_width)
    order_first = d_bits
    order_last = d_bits[1:-1] + d_bits[:1] + d_bits[-1:]
    first_normed, *keyval = norm_keyval(
        tokens, seg_ids, norm1_gain, keyval_weight, cos_kv, sin_kv, core[None], hd // 2, split
    )
    cot = jnp.concatenate([flat(ordered(cotangent, rel)) for rel in range(2)], 0)
    d_ffn = (RESID * cot.astype(F32)).astype(BF16)
    cot_keep = flat(ordered(cotangent, 0))
    xf_keep = flat(ordered(tokens, 0))
    d_ffn, keyval[0], keyval[1] = tie(d_ffn, keyval[0], keyval[1])
    keyval_all = [array[None] for array in keyval]
    for at in range(len(d_bits)):
        got = [
            swap(array, "dp", 1 << order[-1 - at], up=at == 0)
            for array, order in zip(keyval_all, (order_first, order_last))
        ]
        if at == 0:
            d_hidden = hidden_back(d_ffn, w_down)
            *got, d_hidden = tie(*got, d_hidden)
            weights = {0: w_out}
            for bit in x_bits:
                for k in list(weights):
                    weights[k | 1 << bit] = swap(weights[k], "tensor", 1 << bit)
        if at == len(d_bits) - 1:
            query = project_query(first_normed, w_query, cos_q, sin_q, hd // 2)
            d_share = lax.dynamic_slice_in_dim(cotangent, t_at * share, share, 1)
            *got, query, d_share = tie(*got, query, d_share)
            d_share = swap((RESID * d_share.astype(F32)).astype(BF16), "dp", 1 << shared)
        if at == len(d_bits) - 1:
            keyval_all = [array for pair in zip(keyval_all, got) for array in pair]
        else:
            keyval_all = [jnp.concatenate([a, b], 0) for a, b in zip(keyval_all, got)]
    for k in list(weights):
        weights[k | 1] = other_core(weights[k])

    before = sum(
        jnp.sum(array[:, :, block // 2, :3].astype(F32), axis=0) for array in keyval_all[:2]
    ).astype(jnp.int32)
    seg_ordered = jnp.stack([ordered(seg_ids, rel) for rel in range(2)])
    seg_ordered = seg_ordered.transpose(2, 0, 1, 3).reshape(seqs, block)
    doc_start = jnp.sum(
        jnp.where(seg_ordered[:, :, None] > jnp.arange(3), before[:, None, :], 0), axis=2
    )
    start = jnp.min(doc_start, axis=1) // block
    clear = jnp.clip((jnp.max(doc_start, axis=1) + block - 1) // block, start, d_at)

    def slot_of(order):
        slots = slot_order(order)
        table = jnp.array([slots.index(k) for k in range(dp)], jnp.int32)
        return table[d_at ^ jnp.arange(dp)]

    scalars = jnp.concatenate(
        [d_at[None], core[None], start, clear, slot_of(order_first), slot_of(order_last)]
    ).astype(jnp.int32)
    doc_start = doc_start[:, None, :]
    attended_keep, attended_send, lse = attend(
        query, keyval_all, doc_start, scalars, kv_local, hd, split
    )
    parts = {0: flat(attended_keep), 1: other_core(flat(attended_send))}
    for bit in x_bits:
        for k in list(parts):
            parts[k | 1 << bit] = swap(parts[k], "tensor", 1 << bit)
    groups = sorted(parts)
    d_share, parts[groups[nt // 2]] = tie(d_share, parts[groups[nt // 2]])
    resid, second_keep = mix(
        [parts[k] for k in groups], [weights[k] for k in groups], xf_keep, norm2_gain
    )
    second_send = other_core(second_keep)
    second_other = swap(second_keep, "dp", 1 << shared)
    d_share, second_send = tie(d_share, second_send)
    d_ffn_other = flat(gather_x(d_share))
    hidden, d_gate, d_up, second, ffn_keep, ffn_send, d_keep, d_send = feed_forward(
        (second_keep, second_send), None, d_hidden, w_gate, w_up, w_down
    )
    up_order = near[1:] + near[:1]
    gate_own = grad_rows([second], [d_gate], slots_of(near), dp, False, (), (BF16, BF16))
    d_up, *gate_own = tie(d_up, *gate_own)
    up_own = grad_rows([second], [d_up], slots_of(up_order), dp, False, (), (BF16, BF16))
    second_other, d_ffn_other, d_keep, *up_own = tie(second_other, d_ffn_other, d_keep, *up_own)
    d_part = (d_keep.astype(F32) + other_core(d_send).astype(F32)).astype(BF16)
    terms = [d_part]
    for bit in x_bits:
        if len(terms) > 1:
            terms = [sum(term.astype(F32) for term in terms).astype(BF16)]
        terms = [terms[0], swap(terms[0], "tensor", 1 << bit)]
    second_others = (second_other, other_core(second_other))
    d_ffn_others = (d_ffn_other, other_core(d_ffn_other))
    ffn_sum = (ffn_keep.astype(F32) + other_core(ffn_send).astype(F32)).astype(BF16)
    second_other, ffn_sum, terms[0] = tie(second_other, ffn_sum, terms[0])
    second_others = (second_other, second_others[1])
    hidden_o, d_gate_o, d_up_o, second_o, d_ffn_o = feed_forward(
        second_others, d_ffn_others, None, w_gate, w_up, w_down
    )
    def own_rows(array):
        return lax.dynamic_slice_in_dim(array, d_at * piece, piece, 0).astype(F32)

    def gain_share(total, gain):
        total = (total / own_rows(gain)).reshape(nt, piece // nt)
        pieces = [lax.dynamic_index_in_dim(total, t_at ^ k, 0, False) for k in range(nt)]
        return sum([pieces[0]] + [swap(pieces[k], "tensor", k) for k in range(1, nt)])

    def row_sum(weight, grad):
        return jnp.sum(own_rows(weight) * grad, axis=1)

    resid, hidden_o = tie(resid, hidden_o)
    chain = [resid]

    def step(*arrays):
        *arrays, chain[0] = tie(*arrays, chain[0])
        return arrays if len(arrays) > 1 else arrays[0]

    def done(*arrays):
        *arrays, chain[0] = tie(*arrays, chain[0])
        return arrays if len(arrays) > 1 else arrays[0]

    def arrive(*sums):
        for one in sums:
            one.terms[-1] = step(one.terms[-1])

    def more(*sums):
        for one in sums:
            if one.order:
                one.add()
                one.send = done(one.send)
                one.start()
            else:
                one.end()
                one.result = done(one.result)

    terms = step(*terms) if len(terms) > 1 else [step(*terms)]
    ffn, ffn_got = scatter_x_start(step(ffn_sum))
    d_resid, d_mixed_keep = done(*resid_back(terms, resid, cot_keep, norm2_gain))
    d_mixed_send = other_core(d_mixed_keep)
    d_gate_o = step(d_gate_o)
    gate = weight_grad([second_o], [d_gate_o], near, False, gate_own)
    gate.send = done(gate.send)
    gate.start()
    d_up_o = step(d_up_o)
    up = weight_grad([second_o], [d_up_o], up_order, False, up_own)
    up.send = done(up.send)
    up.start()
    d_mixed_send = step(d_mixed_send)
    out = weight_grad(
        [d_mixed_keep, d_mixed_send], [flat(attended_keep), flat(attended_send)], order_last, True
    )
    out.send = done(out.send)
    out.start()
    hidden = step(hidden)
    down = weight_grad([d_ffn, d_ffn_o], [hidden, hidden_o], near, True)
    down.send = done(down.send)
    down.start()
    query = step(query)
    tokens_of = (split, seqs, share, width)
    d_query_keep, d_query_send, *d_keyval = done(
        *attend_back(
            query,
            keyval_all,
            doc_start,
            (attended_keep, attended_send),
            (d_mixed_keep.reshape(tokens_of), d_mixed_send.reshape(tokens_of)),
            w_out,
            lse,
            cos_q,
            sin_q,
            scalars,
            kv_local,
            hd,
        )
    )
    d_query_keep, d_query_send = flat(d_query_keep), flat(d_query_send)
    kv_first = Summing(d_keyval[0], d_keyval[1], order_first)
    kv_last = Summing(d_keyval[2], d_keyval[3], order_last)
    arrive(gate, out)
    ffn_got = step(ffn_got)
    kv_first.start()
    kv_last.start()
    arrive(up)
    first_normed = first_normed.reshape(2, part, width)
    d_query_keep = step(d_query_keep)
    grad_q = weight_grad([first_normed[0], first_normed[1]], [d_query_keep, d_query_send], d_bits)
    grad_q.send = done(grad_q.send)
    d_query_keep = step(d_query_keep)
    back_send, back_keep = done(dot(d_query_send, w_query, NT), dot(d_query_keep, w_query, NT))
    arrive(down, kv_first, kv_last)
    more(kv_first, kv_last)
    for rows in (gate, up, out):
        rows.add()
        rows.send = done(rows.send)
    arrive(kv_first, kv_last)
    more(kv_first, kv_last)
    for rows in (gate, up, out):
        rows.send = step(rows.send)
        rows.start()
    more(down)
    for _ in range(3, len(d_bits)):
        arrive(kv_first, kv_last)
        more(kv_first, kv_last)
    arrive(kv_first, kv_last)
    d_keyval_keep, d_keyval_send = (
        flat(array)
        for array in done(
            *finish_keyval(kv_first.terms, kv_last.terms, cos_kv, sin_kv, hd // 2, split)
        )
    )
    back_send = done((back_send + dot(d_keyval_send, keyval_weight, NT)).astype(BF16))
    back_got = other_core(back_send)
    arrive(gate, up, out)
    grad_q.start()
    d_keyval_keep = step(d_keyval_keep)
    grad_kv = weight_grad(
        [first_normed[0], first_normed[1]], [d_keyval_keep, d_keyval_send], order_last
    )
    grad_kv.send = done(grad_kv.send)
    grad_kv.start()
    more(out)
    back_got = step(back_got)
    back_keep = back_keep + dot(d_keyval_keep, keyval_weight, NT) + back_got.astype(F32)
    back_keep = done(back_keep)
    d_norm1, back_got = scatter_x_start(back_keep, done)
    more(gate, up)
    arrive(down, grad_q)
    more(down, grad_q)
    arrive(grad_kv)
    more(grad_kv)
    d_norm1 = d_norm1 + step(back_got).astype(F32)
    xf_share = own(xf_keep).astype(F32)
    scale1 = lax.rsqrt(jnp.mean(xf_share * xf_share, axis=-1, keepdims=True) + EPS)
    scaled = norm1_gain * d_norm1
    grad_tokens = done(
        own(d_resid)
        + scale1 * scaled
        - xf_share * scale1**3 * jnp.mean(scaled * xf_share, axis=-1, keepdims=True)
    )
    def second_gain():
        gate.result, up.result = step(gate.result, up.result)
        total = done(row_sum(w_gate, gate.result) + row_sum(w_up, up.result))
        return gain_share(total, norm2_gain)

    early = len(near) == 2
    if early:
        grad_gain2 = second_gain()
    live = [out, gate, up, down, grad_q, grad_kv]
    while live := [rows for rows in live if rows.result is None]:
        for rows in live:
            arrive(rows)
            more(rows)
    if not early:
        grad_gain2 = second_gain()
    grad_gate, grad_up, grad_down = gate.result, up.result, down.result
    grad_outproj, grad_query, grad_keyval = out.result, grad_q.result, grad_kv.result
    ffn = ffn.astype(F32) + ffn_got.astype(F32)
    layer_out = (own(chain[0]) + RESID * ffn).astype(BF16)
    total = row_sum(w_query, grad_query) + row_sum(keyval_weight, grad_keyval)
    grad_gain1 = gain_share(total, norm1_gain)
    return (
        layer_out,
        grad_tokens,
        grad_gain1,
        grad_query,
        grad_keyval.reshape(piece, kv_local, 2 * hd),
        grad_outproj,
        grad_gain2,
        grad_gate,
        grad_up,
        grad_down,
    )


def solution(mesh):
    placed = (
        P(None, "dp", None),
        P(None, "dp"),
        P(),
        P(None, "tensor"),
        P(None, "tensor", None),
        P("tensor", None),
        P(),
        P(None, "tensor"),
        P(None, "tensor"),
        P("tensor", None),
        P(None, "dp", None),
    )
    return jax.shard_map(
        body,
        mesh=mesh,
        in_specs=placed,
        out_specs=(
            P(None, ("dp", "tensor"), None),
            P(None, ("dp", "tensor"), None),
            P(("dp", "tensor")),
            P("dp", "tensor"),
            P("dp", "tensor", None),
            P("tensor", "dp"),
            P(("dp", "tensor")),
            P("dp", "tensor"),
            P("dp", "tensor"),
            P("tensor", "dp"),
        ),
        check_vma=False,
    )
```

```python
import math

import jax
import jax.numpy as jnp
from jax import lax
from jax.experimental import pallas as pl
from jax.experimental.pallas import tpu as pltpu
from jax.sharding import PartitionSpec as P

EPS = 1e-05
SCALE = 0.015625
RESID = 0.22
THETA = 10000000.0
NEG = -1e30
PAD = 16
VMEM = 56 * 1024 * 1024
F32 = jnp.float32
BF16 = jnp.bfloat16
NT = (((1,), (1,)), ((), ()))
TN = (((0,), (0,)), ((), ()))


def dot(a, b, dims=None):
    if dims is None:
        return jnp.dot(a, b, preferred_element_type=F32)
    return lax.dot_general(a, b, dims, preferred_element_type=F32)


def params():
    return pltpu.CompilerParams(vmem_limit_bytes=VMEM)


def cost(flops, nbytes):
    return pl.CostEstimate(flops=int(flops) // 1024, bytes_accessed=int(nbytes) // 1024, transcendentals=0)


def slot_order(bits):
    slots = [0]
    for bit in reversed(bits):
        slots = slots + [k ^ (1 << bit) for k in slots]
    return slots


def swap(value, axis, distance, up=False):
    pairs = [(i, i ^ distance) for i in range(lax.axis_size(axis))]
    return lax.ppermute(value, axis, [(i, j) for i, j in pairs if j > i or not up])


def rope_tables(positions, head_dim):
    half = head_dim // 2
    inverse = jnp.power(F32(THETA), -(jnp.arange(half).astype(F32) * (2.0 / head_dim)))
    angle = positions.astype(F32)[:, None] * inverse[None, :]
    return (jnp.cos(angle), jnp.sin(angle))


def rotate_lanes(x, cosine, sine, half):
    width = x.shape[1]
    lane = lax.broadcasted_iota(jnp.int32, x.shape, 1)
    ahead = pltpu.roll(x, width - half, 1)
    behind = pltpu.roll(x, half, 1)
    partner = jnp.where((lane & (2 * half - 1)) < half, ahead, behind)
    times = width // cosine.shape[1]
    if times > 1:
        cosine = jnp.concatenate([cosine] * times, 1)
        sine = jnp.concatenate([sine] * times, 1)
    return x * cosine + partner * sine


def whole(array):
    rank = array.ndim
    return pl.BlockSpec(array.shape, lambda *_: (0,) * rank)


def norm_keyval(tokens, seg_ids, gain, weight, cosine, sine, core, half, split):
    seqs, block, width = tokens.shape
    out = weight.shape[1]
    share = block // (2 * split)

    def kernel(at, tok_ref, seg_ref, gain_ref, w_ref, cos_ref, sin_ref, n_ref, a_ref, b_ref):
        pieces = []
        for rel in range(2):
            for x in range(split):
                begin = pl.multiple_of((2 * x + (at[0] ^ rel)) * share, share)
                pieces.append(tok_ref[0, pl.ds(begin, share), :])
        xf = jnp.concatenate(pieces, 0).astype(F32)
        scale = lax.rsqrt(jnp.mean(xf * xf, axis=-1, keepdims=True) + EPS)
        normed = (xf * scale * gain_ref[...]).astype(BF16)
        n_ref[...] = normed.reshape(n_ref.shape)
        raw = dot(normed, w_ref[...])
        keyval = rotate_lanes(raw, cos_ref[...], sin_ref[...], half).astype(BF16)
        a_ref[0, : block // 2, :] = keyval[: block // 2]
        b_ref[0] = keyval[block // 2 :]
        lane = lax.broadcasted_iota(jnp.int32, (PAD, out), 1)
        row = jnp.zeros((PAD, out), F32)
        for v in range(3):
            count = jnp.sum(jnp.where(seg_ref[0] == v, 1.0, 0.0))
            row = jnp.where(lane == v, count, row)
        a_ref[0, block // 2 :, :] = row.astype(BF16)

    return pl.pallas_call(
        kernel,
        grid_spec=pltpu.PrefetchScalarGridSpec(
            num_scalar_prefetch=1,
            grid=(seqs,),
            in_specs=[
                pl.BlockSpec((1, block, width), lambda s, at: (s, 0, 0)),
                pl.BlockSpec((1, 1, block), lambda s, at: (s, 0, 0)),
                pl.BlockSpec((1, width), lambda s, at: (0, 0)),
                whole(weight),
                whole(cosine),
                whole(sine),
            ],
            out_specs=[
                pl.BlockSpec((2, split, 1, share, width), lambda s, at: (0, 0, s, 0, 0)),
                pl.BlockSpec((1, block // 2 + PAD, out), lambda s, at: (s, 0, 0)),
                pl.BlockSpec((1, block // 2, out), lambda s, at: (s, 0, 0)),
            ],
        ),
        out_shape=[
            jax.ShapeDtypeStruct((2, split, seqs, share, width), BF16),
            jax.ShapeDtypeStruct((seqs, block // 2 + PAD, out), BF16),
            jax.ShapeDtypeStruct((seqs, block // 2, out), BF16),
        ],
        compiler_params=params(),
        cost_estimate=cost(2 * seqs * block * width * out, 4 * seqs * block * width),
        name="norm_keyval",
    )(core, tokens, seg_ids[:, None, :], gain.reshape(1, width), weight, cosine, sine)


def project_query(normed, weight, cosine, sine, half):
    _, split, seqs, share, width = normed.shape
    block = 2 * split * share
    out = weight.shape[1]

    def kernel(n_ref, w_ref, cos_ref, sin_ref, q_ref):
        raw = dot(n_ref[...].reshape(block, width), w_ref[...])
        q_ref[0] = rotate_lanes(raw, cos_ref[...], sin_ref[...], half).astype(BF16)

    return pl.pallas_call(
        kernel,
        grid=(seqs,),
        in_specs=[
            pl.BlockSpec((2, split, 1, share, width), lambda s: (0, 0, s, 0, 0)),
            whole(weight),
            whole(cosine),
            whole(sine),
        ],
        out_specs=pl.BlockSpec((1, block, out), lambda s: (s, 0, 0)),
        out_shape=jax.ShapeDtypeStruct((seqs, block, out), BF16),
        compiler_params=params(),
        cost_estimate=cost(2 * seqs * block * width * out, 2 * seqs * block * width),
        name="project_query",
    )(normed, weight, cosine, sine)


def stacked_lanes(x, group, hd, low):
    rows = x.shape[1]
    flat = jnp.concatenate([x[h * hd : (h + 1) * hd] for h in range(group)], 1)
    zero = jnp.zeros((hd, group * rows), flat.dtype)
    return jnp.concatenate([flat, zero] if low else [zero, flat], 0)


def stacked_rows(x, group, hd, low):
    parts = []
    for h in range(group):
        at = (h * hd) // (2 * hd) * (2 * hd)
        piece = x[:, at : at + 2 * hd]
        if (h % 2 == 0) != low:
            piece = pltpu.roll(piece, hd, 1)
        lane = lax.broadcasted_iota(jnp.int32, piece.shape, 1)
        parts.append(jnp.where((lane < hd) == low, piece, 0.0))
    return jnp.concatenate(parts, 0)


def keyval_of(last, count, sc, base, refs, blocks, half):
    parts = []
    for back in reversed(range(count)):
        chunk = jnp.maximum(last - back, 0) if back else last
        for low, high, table in ((refs[0], refs[1], 0), (refs[2], refs[3], blocks)):
            at = sc[base + table + chunk]
            one = low[jnp.minimum(at, blocks // 2 - 1), 0, :half, :]
            two = high[jnp.maximum(at - blocks // 2, 0), 0, :half, :]
            parts.append(jnp.where(at < blocks // 2, one, two))
    return jnp.concatenate(parts, 0)


def keyval_specs(blocks, half, width):
    return [
        pl.BlockSpec((blocks // 2, 1, rows, width), lambda s, h, sc: (0, s, 0, h))
        for rows in (half + PAD, half + PAD, half, half)
    ]


def mask_bias(last, count, block, position_block, doc_start, core, share, group):
    half = block // 2

    def place(axis):
        row = lax.broadcasted_iota(jnp.int32, (count * block, block), axis)
        chunk = row // block * block if axis == 0 else 0
        row = row - chunk
        rel = jnp.where(row >= half, 1, 0)
        row = row - half * rel
        return (row // share * 2 + (rel ^ core)) * share + row % share + chunk

    key_pos = (last - count + 1) * block + place(0)
    query_pos = position_block * block + place(1)
    visible = (key_pos >= doc_start) & (key_pos <= query_pos)
    bias = jnp.where(visible, 0.0, NEG)
    return jnp.concatenate([bias] * group, 1)


def pair_loops(mine, start, clear, visit, carry):
    whole_pairs = jnp.maximum(mine - 1 - clear, 0) // 2
    pairs = (mine - start) // 2
    run = lambda masked: lambda p, carry: visit(mine - 2 * p, masked, carry)
    carry = lax.fori_loop(1, 1 + whole_pairs, run(False), carry)
    return lax.fori_loop(1 + whole_pairs, 1 + pairs, run(True), carry)


def attend(query, keyval_all, doc_start, scalars, kv_local, hd, split):
    seqs, block, q_width = query.shape
    blocks = 2 * keyval_all[0].shape[0]
    group = q_width // kv_local // hd
    wide = group * block
    share = block // (2 * split)

    base = 2 + 2 * seqs
    half = block // 2

    def kernel(sc, q_ref, *refs):
        kv_refs, (doc_ref, keep_ref, send_ref, lse_ref, acc) = refs[:4], refs[4:]
        seq = pl.program_id(0)
        mine = sc[0]
        core = sc[1]
        start = sc[2 + seq]
        clear = sc[2 + seqs + seq]
        q_lanes = stacked_lanes((q_ref[0].astype(F32) * SCALE).astype(BF16).T, group, hd, True)
        doc = doc_ref[0]

        def scores_of(last, masked):
            kv = keyval_of(last, 2, sc, base, kv_refs, blocks, half)
            scores = dot(kv, q_lanes)
            if masked:
                scores = scores + mask_bias(last, 2, block, mine, doc, core, share, group)
            return kv, scores

        kv, scores = scores_of(mine, True)
        peak = jnp.max(scores, axis=0, keepdims=True)
        probs = jnp.exp(scores - peak)
        total = jnp.sum(probs, axis=0, keepdims=True)
        acc[...] = dot(kv, probs.astype(BF16), TN)

        def visit(last, masked, carry):
            peak, total = carry
            kv, scores = scores_of(last, masked)
            higher = jnp.maximum(peak, jnp.max(scores, axis=0, keepdims=True))
            shrink = jnp.exp(peak - higher)
            probs = jnp.exp(scores - higher)
            total = total * shrink + jnp.sum(probs, axis=0, keepdims=True)
            acc[...] = acc[...] * shrink + dot(kv, probs.astype(BF16), TN)
            return higher, total

        peak, total = pair_loops(mine, start, clear, visit, (peak, total))
        lse_ref[0, 0] = peak + jnp.log(total)
        result = acc[hd:] / total
        result = jnp.concatenate([result[:, h * block : (h + 1) * block] for h in range(group)], 0)
        result = result.T.astype(BF16)
        keep_ref[...] = result[:half].reshape(keep_ref.shape)
        send_ref[...] = result[half:].reshape(send_ref.shape)

    return pl.pallas_call(
        kernel,
        grid_spec=pltpu.PrefetchScalarGridSpec(
            num_scalar_prefetch=1,
            grid=(seqs, kv_local),
            in_specs=[
                pl.BlockSpec((1, block, group * hd), lambda s, h, sc: (s, 0, h)),
                *keyval_specs(blocks, half, 2 * hd),
                pl.BlockSpec((1, 1, block), lambda s, h, sc: (s, 0, 0)),
            ],
            out_specs=[
                pl.BlockSpec((split, 1, share, group * hd), lambda s, h, sc: (0, s, 0, h)),
                pl.BlockSpec((split, 1, share, group * hd), lambda s, h, sc: (0, s, 0, h)),
                pl.BlockSpec((1, 1, 1, wide), lambda s, h, sc: (s, h, 0, 0)),
            ],
            scratch_shapes=[pltpu.VMEM((2 * hd, wide), F32)],
        ),
        out_shape=[
            jax.ShapeDtypeStruct((split, seqs, share, q_width), BF16),
            jax.ShapeDtypeStruct((split, seqs, share, q_width), BF16),
            jax.ShapeDtypeStruct((seqs, kv_local, 1, wide), F32),
        ],
        compiler_params=params(),
        cost_estimate=cost(
            8 * seqs * block * q_width * blocks * block, 4 * seqs * blocks * block * 2 * hd
        ),
        name="attend",
    )(scalars, query, *keyval_all, doc_start)


def attend_back(
    query, keyval_all, doc_start, attended, d_mixed, w_out, lse, cosine, sine, scalars, kv_local, hd
):
    seqs, block, q_width = query.shape
    split, _, share, _ = attended[0].shape
    width = w_out.shape[1]
    blocks = 2 * keyval_all[0].shape[0]
    group = q_width // kv_local // hd
    wide = group * block
    base = 2 + 2 * seqs
    half = block // 2

    def kernel(sc, q_ref, *refs):
        kv_refs, refs = refs[:4], refs[4:]
        doc_ref, ok_ref, os_ref, keep_ref, send_ref, w_ref, lse_ref, cos_ref, sin_ref = refs[:9]
        dqk_ref, dqs_ref, ako, aso, bko, bso, acc, ak_ref, as_ref, bk_ref, bs_ref = refs[9:]
        seq = pl.program_id(0)
        mine = sc[0]
        core = sc[1]
        start = sc[2 + seq]
        clear = sc[2 + seqs + seq]
        doc = doc_ref[0]
        q = q_ref[0].astype(F32) * SCALE
        mixed = jnp.concatenate(
            [keep_ref[...].reshape(half, width), send_ref[...].reshape(half, width)], 0
        )
        d_out = dot(mixed, w_ref[...], NT).astype(BF16)
        d_out_t = d_out.T
        d_out = d_out.astype(F32)
        q_lanes = stacked_lanes(q.astype(BF16).T, group, hd, True)
        attended = jnp.concatenate(
            [ok_ref[...].reshape(half, group * hd), os_ref[...].reshape(half, group * hd)], 0
        )
        o_lanes = d_out_t.astype(F32) * attended.T.astype(F32)
        delta = jnp.concatenate(
            [
                jnp.sum(o_lanes[h * hd : (h + 1) * hd], axis=0, keepdims=True)
                for h in range(group)
            ],
            1,
        )
        d_lanes = stacked_lanes(d_out_t, group, hd, False)
        q_rows = stacked_rows(q, group, hd, True).astype(BF16)
        d_rows = stacked_rows(d_out, group, hd, False).astype(BF16)
        total = lse_ref[0, 0]
        acc[...] = jnp.zeros_like(acc)

        def put(chunk, value):
            for table, kept, sent, rows in (
                (0, ak_ref, as_ref, value[:half]),
                (blocks, bk_ref, bs_ref, value[half:]),
            ):
                at = sc[base + table + chunk]
                kept[jnp.minimum(at, blocks // 2)] = rows
                sent[jnp.where(at < blocks // 2, blocks // 2, at - blocks // 2)] = rows

        def work(chunk, masked):
            kv = keyval_of(chunk, 1, sc, base, kv_refs, blocks, half)
            scores = dot(kv, q_lanes)
            if masked:
                scores = scores + mask_bias(chunk, 1, block, mine, doc, core, share, group)
            probs = jnp.exp(scores - total)
            d_probs = dot(kv, d_lanes)
            d_scores = (probs * (d_probs - delta)).astype(BF16)
            d_kv = dot(probs.astype(BF16), d_rows) + dot(d_scores, q_rows)
            put(chunk, d_kv.astype(BF16))
            acc[...] += dot(kv, d_scores, TN)

        def clean(chunk, carry):
            put(chunk, jnp.zeros((block, 2 * hd), BF16))
            return carry

        def step(masked):
            def run(chunk, carry):
                work(chunk, masked)
                return carry

            return run

        lax.fori_loop(0, start, clean, 0)
        lax.fori_loop(start, clear, step(True), 0)
        lax.fori_loop(clear, mine, step(False), 0)
        work(mine, True)
        lax.fori_loop(mine + 1, blocks, clean, 0)
        for out, ref in ((ako, ak_ref), (aso, as_ref), (bko, bk_ref), (bso, bs_ref)):
            out[:, 0] = ref[: blocks // 2]
        dq = acc[:hd] * SCALE
        dq = jnp.concatenate([dq[:, h * block : (h + 1) * block] for h in range(group)], 0)
        dq = rotate_lanes(dq.T, cos_ref[...], -sin_ref[...], hd // 2)
        dq = dq.astype(BF16)
        dqk_ref[...] = dq[:half].reshape(dqk_ref.shape)
        dqs_ref[...] = dq[half:].reshape(dqs_ref.shape)

    ordered = pl.BlockSpec((split, 1, share, group * hd), lambda s, h, sc: (0, s, 0, h))
    mixed = pl.BlockSpec((split, 1, share, width), lambda s, h, sc: (0, s, 0, 0))
    parts = pl.BlockSpec((blocks // 2, 1, half, 2 * hd), lambda s, h, sc: (0, s, 0, h))
    return pl.pallas_call(
        kernel,
        grid_spec=pltpu.PrefetchScalarGridSpec(
            num_scalar_prefetch=1,
            grid=(seqs, kv_local),
            in_specs=[
                pl.BlockSpec((1, block, group * hd), lambda s, h, sc: (s, 0, h)),
                *keyval_specs(blocks, half, 2 * hd),
                pl.BlockSpec((1, 1, block), lambda s, h, sc: (s, 0, 0)),
                ordered,
                ordered,
                mixed,
                mixed,
                pl.BlockSpec((group * hd, width), lambda s, h, sc: (h, 0)),
                pl.BlockSpec((1, 1, 1, wide), lambda s, h, sc: (s, h, 0, 0)),
                whole(cosine),
                whole(sine),
            ],
            out_specs=[ordered] * 2 + [parts] * 4,
            scratch_shapes=[pltpu.VMEM((2 * hd, wide), F32)]
            + [pltpu.VMEM((blocks // 2 + 1, half, 2 * hd), BF16)] * 4,
        ),
        out_shape=[jax.ShapeDtypeStruct((split, seqs, share, q_width), BF16)] * 2
        + [jax.ShapeDtypeStruct((blocks // 2, seqs, half, kv_local * 2 * hd), BF16)] * 4,
        compiler_params=params(),
        cost_estimate=cost(
            20 * seqs * block * q_width * blocks * block, 8 * seqs * blocks * block * 2 * hd
        ),
        name="attend_back",
    )(scalars, query, *keyval_all, doc_start, *attended, *d_mixed, w_out, lse, cosine, sine)


def finish_keyval(first, last, cosine, sine, half, split):
    _, seqs, part, width = first[0].shape
    share = part // split
    terms = first + last
    count = len(first)

    def kernel(*refs):
        cos_ref, sin_ref, keep_ref, send_ref = refs[2 * count :]
        halves = [
            sum(ref[0, 0].astype(F32) for ref in some)
            for some in (refs[:count], refs[count : 2 * count])
        ]
        x = jnp.concatenate(halves, 0)
        x = rotate_lanes(x, cos_ref[...], -sin_ref[...], half).astype(BF16)
        keep_ref[...] = x[:part].reshape(keep_ref.shape)
        send_ref[...] = x[part:].reshape(send_ref.shape)

    out = pl.BlockSpec((split, 1, share, width), lambda s: (0, s, 0, 0))
    return pl.pallas_call(
        kernel,
        grid=(seqs,),
        in_specs=[pl.BlockSpec((1, 1, part, width), lambda s: (0, s, 0, 0))] * (2 * count)
        + [whole(cosine), whole(sine)],
        out_specs=[out] * 2,
        out_shape=[jax.ShapeDtypeStruct((split, seqs, share, width), BF16)] * 2,
        compiler_params=params(),
        cost_estimate=cost(0, 16 * seqs * part * width),
        name="finish_keyval",
    )(*terms, cosine, sine)


def mix(parts, weights, xf, gain):
    rows, deep = parts[0].shape
    width = weights[0].shape[1]
    count = len(parts)
    tile = math.gcd(width, 512)
    steps = width // tile

    def kernel(*refs):
        x_ref, gain_ref, resid_ref, n_ref, acc = refs[2 * count :]
        j = pl.program_id(0)
        left = jnp.concatenate([refs[k][...] for k in range(count)], 1)
        right = jnp.concatenate([refs[count + k][...] for k in range(count)], 0)
        resid = x_ref[...].astype(F32) + RESID * dot(left, right)
        resid_ref[...] = resid
        acc[j] = resid

        @pl.when(j == steps - 1)
        def _():
            square = sum(jnp.sum(acc[i] * acc[i], axis=-1, keepdims=True) for i in range(steps))
            scale = lax.rsqrt(square / width + EPS)
            for i in range(steps):
                at = pl.ds(i * tile, tile)
                n_ref[:, at] = (acc[i] * scale * gain_ref[:, at]).astype(BF16)

    fixed = lambda r, c: pl.BlockSpec((r, c), lambda j: (0, 0))
    return pl.pallas_call(
        kernel,
        grid=(steps,),
        in_specs=[fixed(rows, deep)] * count
        + [pl.BlockSpec((deep, tile), lambda j: (0, j))] * count
        + [pl.BlockSpec((rows, tile), lambda j: (0, j)), fixed(1, width)],
        out_specs=[pl.BlockSpec((rows, tile), lambda j: (0, j)), fixed(rows, width)],
        out_shape=[
            jax.ShapeDtypeStruct((rows, width), F32),
            jax.ShapeDtypeStruct((rows, width), BF16),
        ],
        scratch_shapes=[pltpu.VMEM((steps, rows, tile), F32)],
        compiler_params=params(),
        cost_estimate=cost(2 * rows * count * deep * width, 2 * count * deep * width),
        name="mix",
    )(*parts, *weights, xf, gain.reshape(1, width))


def resid_back(terms, resid, d_out, gain):
    rows, width = resid.shape
    tile = math.gcd(rows, 128)
    count = len(terms)

    def kernel(*refs):
        resid_ref, dy_ref, gain_ref, d_ref, mixed_ref = refs[count:]
        d_norm = sum(ref[...].astype(F32) for ref in refs[:count])
        resid = resid_ref[...]
        scale = lax.rsqrt(jnp.mean(resid * resid, axis=-1, keepdims=True) + EPS)
        scaled = gain_ref[...] * d_norm
        inner = jnp.mean(scaled * resid, axis=-1, keepdims=True)
        d_resid = dy_ref[...].astype(F32) + scale * scaled - resid * (scale**3 * inner)
        d_ref[...] = d_resid
        mixed_ref[...] = (RESID * d_resid).astype(BF16)

    one = pl.BlockSpec((tile, width), lambda i: (i, 0))
    return pl.pallas_call(
        kernel,
        grid=(rows // tile,),
        in_specs=[one] * (count + 2) + [pl.BlockSpec((1, width), lambda i: (0, 0))],
        out_specs=[one] * 2,
        out_shape=[
            jax.ShapeDtypeStruct((rows, width), F32),
            jax.ShapeDtypeStruct((rows, width), BF16),
        ],
        compiler_params=params(),
        cost_estimate=cost(0, 16 * rows * width),
        name="resid_back",
    )(*terms, resid, d_out, gain.reshape(1, width))


def hidden_back(d_ffn, w_down):
    rows, width = d_ffn.shape
    hidden = w_down.shape[0]
    tile = math.gcd(hidden, 512)

    def kernel(dy_ref, w_ref, o_ref):
        o_ref[...] = dot(dy_ref[...], w_ref[...], NT)

    return pl.pallas_call(
        kernel,
        grid=(hidden // tile,),
        in_specs=[whole(d_ffn), pl.BlockSpec((tile, width), lambda j: (j, 0))],
        out_specs=pl.BlockSpec((rows, tile), lambda j: (0, j)),
        out_shape=jax.ShapeDtypeStruct((rows, hidden), F32),
        compiler_params=params(),
        cost_estimate=cost(2 * rows * width * hidden, 2 * hidden * (rows + width)),
        name="hidden_back",
    )(d_ffn, w_down)


def feed_forward(normed, d_ffn, d_hidden, w_gate, w_up, w_down):
    back = d_hidden is not None
    part, width = normed[0].shape
    rows = 2 * part
    hidden = w_gate.shape[1]
    tile = math.gcd(hidden, 512)
    steps = hidden // tile

    sources = (d_hidden,) if back else d_ffn
    count = len(sources)

    def kernel(nk, ns, *refs):
        wg_ref, wu_ref, wd_ref, h_ref, dg_ref, du_ref, n_ref, *rest = refs[count:]
        at = pl.program_id(0)
        if not back:
            dy_ref, *rest = rest

        @pl.when(at == 0)
        def _():
            n_ref[:part] = nk[...]
            n_ref[part:] = ns[...]
            if not back:
                dy_ref[:part] = refs[0][...]
                dy_ref[part:] = refs[1][...]

        normed = n_ref[...]
        gate = dot(normed, wg_ref[...])
        up = dot(normed, wu_ref[...])
        d_hidden = refs[0][...] if back else dot(dy_ref[...], wd_ref[...], NT)
        sigma = jax.nn.sigmoid(gate)
        swish = gate * sigma
        hidden_tile = (swish * up).astype(BF16)
        d_gate = (d_hidden * up * sigma * (1.0 + gate * (1.0 - sigma))).astype(BF16)
        d_up = (d_hidden * swish).astype(BF16)
        h_ref[...] = hidden_tile
        dg_ref[...] = d_gate
        du_ref[...] = d_up
        if not back:
            return
        f_keep, f_send, dn_keep, dn_send, f_acc, n_acc = rest
        ffn = dot(hidden_tile, wd_ref[...])
        d_normed = dot(d_gate, wg_ref[...], NT) + dot(d_up, wu_ref[...], NT)

        @pl.when(at == 0)
        def _():
            f_acc[...] = ffn
            n_acc[...] = d_normed

        @pl.when(at > 0)
        def _():
            f_acc[...] += ffn
            n_acc[...] += d_normed

        @pl.when(at == steps - 1)
        def _():
            f_keep[...] = f_acc[:part].astype(BF16)
            f_send[...] = f_acc[part:].astype(BF16)
            dn_keep[...] = n_acc[:part].astype(BF16)
            dn_send[...] = n_acc[part:].astype(BF16)

    fixed = lambda r: pl.BlockSpec((r, width), lambda j: (0, 0))
    once = lambda r: pl.BlockSpec((r, width), lambda j: (0, 0), pipeline_mode=pl.Buffered(1))
    extra = 4 if back else 0
    return pl.pallas_call(
        kernel,
        grid=(steps,),
        in_specs=[once(part)] * 2
        + (
            [pl.BlockSpec((rows, tile), lambda j: (0, j))] if back else [once(part)] * 2
        )
        + [
            pl.BlockSpec((width, tile), lambda j: (0, j)),
            pl.BlockSpec((width, tile), lambda j: (0, j)),
            pl.BlockSpec((tile, width), lambda j: (j, 0)),
        ],
        out_specs=[pl.BlockSpec((rows, tile), lambda j: (0, j))] * 3
        + [fixed(rows)] * count
        + [fixed(part)] * extra,
        out_shape=[jax.ShapeDtypeStruct((rows, hidden), BF16)] * 3
        + [jax.ShapeDtypeStruct((rows, width), BF16)] * count
        + [jax.ShapeDtypeStruct((part, width), BF16)] * extra,
        scratch_shapes=[pltpu.VMEM((rows, width), F32)] * (extra // 2),
        compiler_params=params(),
        cost_estimate=cost(
            (10 if back else 6) * rows * width * hidden, 6 * width * hidden
        ),
        name="feed_forward" if back else "feed_forward_other",
    )(*normed, *sources, w_gate, w_up, w_down)


def grad_rows(lefts, rights, blocks_at, pieces, turned, base=(), dtypes=(F32, BF16)):
    count = blocks_at.shape[0]
    width = lefts[0].shape[1]
    piece = width // pieces
    columns = rights[0].shape[1]
    tile = math.gcd(columns, 512)
    pairs = len(lefts)
    half = count // 2 * piece

    def kernel(at, *refs):
        keep, send = refs[-2:]
        total = None
        for p in range(pairs):
            left = jnp.concatenate([refs[p * count + i][...] for i in range(count)], 1)
            right = refs[pairs * count + p][...]
            term = dot(right, left, TN) if turned else dot(left, right, TN)
            total = term if total is None else total + term
        if base:
            total = total + jnp.concatenate(
                [refs[-4][...].astype(F32), refs[-3][...].astype(F32)], int(turned)
            )
        keep[...] = (total[:, :half] if turned else total[:half]).astype(dtypes[0])
        send[...] = (total[:, half:] if turned else total[half:]).astype(dtypes[1])

    specs = [
        pl.BlockSpec((left.shape[0], piece), lambda j, at, i=i: (0, at[i]))
        for left in lefts
        for i in range(count)
    ] + [pl.BlockSpec((right.shape[0], tile), lambda j, at: (0, j)) for right in rights]
    tokens = sum(left.shape[0] for left in lefts)
    halves = [
        pl.BlockSpec((tile, half), lambda j, at: (j, 0))
        if turned
        else pl.BlockSpec((half, tile), lambda j, at: (0, j))
    ] * 2
    return pl.pallas_call(
        kernel,
        grid_spec=pltpu.PrefetchScalarGridSpec(
            num_scalar_prefetch=1,
            grid=(columns // tile,),
            in_specs=specs + halves[: len(base)],
            out_specs=halves,
        ),
        out_shape=[
            jax.ShapeDtypeStruct((columns, half) if turned else (half, columns), dtype)
            for dtype in dtypes
        ],
        compiler_params=params(),
        cost_estimate=cost(4 * tokens * half * columns, 2 * tokens * (2 * half + columns)),
        name="grad_rows",
    )(blocks_at, *[left for left in lefts for _ in range(count)], *rights, *base)


def body(
    tokens,
    seg_ids,
    norm1_gain,
    w_query,
    w_keyval,
    w_out,
    norm2_gain,
    w_gate,
    w_up,
    w_down,
    cotangent,
):
    seqs, block, width = tokens.shape
    kv_local = w_keyval.shape[1]
    hd = w_keyval.shape[2] // 2
    q_width = w_query.shape[1]
    kv_width = kv_local * 2 * hd
    dp = lax.axis_size("dp")
    nt = lax.axis_size("tensor")
    split = nt // 2
    share = block // nt
    piece = width // dp
    part = seqs * block // 2
    d_at = lax.axis_index("dp")
    t_at = lax.axis_index("tensor")
    core = t_at & 1
    x_at = t_at >> 1
    x_bits = list(range(1, nt.bit_length() - 1))
    d_bits = list(range(dp.bit_length() - 1))
    shared = d_bits[-1]
    near = d_bits[:-1]

    def ordered(array, rel):
        array = array.reshape(seqs, split, 2, share, *array.shape[2:])
        array = lax.dynamic_index_in_dim(array, core ^ rel, 2, keepdims=False)
        return jnp.swapaxes(array, 0, 1)

    def own(array):
        return lax.dynamic_index_in_dim(array.reshape(split, seqs, share, width), x_at, 0, False)

    def other_core(array):
        return swap(array, "tensor", 1)

    def flat(array):
        return array.reshape(-1, array.shape[-1])

    def tie(*arrays):
        return lax.optimization_barrier(arrays)

    def scatter_x_start(total, keep_order=lambda array: array):
        total = total.reshape(-1, seqs, share, width)
        for bit in reversed(x_bits):
            total = total.reshape(2, -1, seqs, share, width)
            mine = (t_at >> bit) & 1
            send = lax.dynamic_index_in_dim(total, mine ^ 1, 0, False).astype(BF16)
            total = lax.dynamic_index_in_dim(total, mine, 0, False).astype(F32)
            got = swap(keep_order(send), "tensor", 1 << bit)
            if bit == x_bits[0]:
                return total[0], got[0]
            total = total + got.astype(F32)

    def gather_x(total):
        total = total[None]
        for bit in x_bits:
            got = swap(total, "tensor", 1 << bit)
            low = (t_at >> bit) & 1 == 0
            total = jnp.concatenate(
                [jnp.where(low, total, got), jnp.where(low, got, total)], 0
            )
        return total

    class Summing:
        def __init__(self, keep, send, order, axis=0):
            self.terms, self.send, self.order, self.axis = [keep], send, list(order), axis
            self.size, self.result = keep.shape[axis], None

        def start(self):
            self.terms.append(swap(self.send, "dp", 1 << self.order.pop(0)))

        def add(self):
            self.size //= 2
            self.send = self.total(self.size).astype(BF16)

        def end(self):
            self.result = self.total(0)

        def total(self, first):
            return sum(
                lax.slice_in_dim(term, first, first + self.size, 1, self.axis).astype(F32)
                for term in self.terms
            )

    def slots_of(order):
        return d_at ^ jnp.array(slot_order(order), jnp.int32)

    def weight_grad(lefts, rights, order, turned=False, base=()):
        keep, send = grad_rows(lefts, rights, slots_of(order), dp, turned, base)
        return Summing(keep, send, order, int(turned))

    place = jnp.arange(block).reshape(2, split, share)
    place = ((place // share) % split * 2 + (place // (block // 2) ^ core)) * share + place % share
    positions = d_at * block + place.reshape(block)
    cosine, sine = rope_tables(positions, hd)
    cos_q = jnp.concatenate([cosine] * 4, 1)
    sin_q = jnp.concatenate([-sine, sine] * 2, 1)
    ones = jnp.ones((block, hd), F32)
    cos_kv = jnp.concatenate([cosine, cosine, ones], 1)
    sin_kv = jnp.concatenate([-sine, sine, 0.0 * ones], 1)
    keyval_weight = w_keyval.reshape(width, kv_width)
    order_first = d_bits
    order_last = d_bits[1:-1] + d_bits[:1] + d_bits[-1:]
    first_normed, *keyval = norm_keyval(
        tokens, seg_ids, norm1_gain, keyval_weight, cos_kv, sin_kv, core[None], hd // 2, split
    )
    cotangent, tokens, *keyval = tie(cotangent, tokens, *keyval)
    cot = jnp.concatenate([flat(ordered(cotangent, rel)) for rel in range(2)], 0)
    d_ffn = (RESID * cot.astype(F32)).astype(BF16)
    cot_keep = flat(ordered(cotangent, 0))
    xf_keep = flat(ordered(tokens, 0))
    keyval_all = [array[None] for array in keyval]
    for at in range(len(d_bits)):
        got = [
            swap(array, "dp", 1 << order[-1 - at], up=at == 0)
            for array, order in zip(keyval_all, (order_first, order_last))
        ]
        if at == 0:
            d_hidden = hidden_back(d_ffn, w_down)
            *got, d_hidden = tie(*got, d_hidden)
            weights = {0: w_out}
            for bit in x_bits:
                for k in list(weights):
                    weights[k | 1 << bit] = swap(weights[k], "tensor", 1 << bit)
        if at == len(d_bits) - 1:
            query = project_query(first_normed, w_query, cos_q, sin_q, hd // 2)
            d_share = lax.dynamic_slice_in_dim(cotangent, t_at * share, share, 1)
            d_share = (RESID * d_share.astype(F32)).astype(BF16)
            *got, query, d_share = tie(*got, query, d_share)
            d_share = swap(d_share, "dp", 1 << shared)
        if at == len(d_bits) - 1:
            keyval_all = [array for pair in zip(keyval_all, got) for array in pair]
        else:
            keyval_all = [jnp.concatenate([a, b], 0) for a, b in zip(keyval_all, got)]
    for k in list(weights):
        weights[k | 1] = other_core(weights[k])

    before = sum(
        jnp.sum(array[:, :, block // 2, :3].astype(F32), axis=0) for array in keyval_all[:2]
    ).astype(jnp.int32)
    seg_ordered = jnp.stack([ordered(seg_ids, rel) for rel in range(2)])
    seg_ordered = seg_ordered.transpose(2, 0, 1, 3).reshape(seqs, block)
    doc_start = jnp.sum(
        jnp.where(seg_ordered[:, :, None] > jnp.arange(3), before[:, None, :], 0), axis=2
    )
    start = jnp.min(doc_start, axis=1) // block
    clear = jnp.clip((jnp.max(doc_start, axis=1) + block - 1) // block, start, d_at)

    def slot_of(order):
        slots = slot_order(order)
        table = jnp.array([slots.index(k) for k in range(dp)], jnp.int32)
        return table[d_at ^ jnp.arange(dp)]

    scalars = jnp.concatenate(
        [d_at[None], core[None], start, clear, slot_of(order_first), slot_of(order_last)]
    ).astype(jnp.int32)
    doc_start = doc_start[:, None, :]
    attended_keep, attended_send, lse = attend(
        query, keyval_all, doc_start, scalars, kv_local, hd, split
    )
    parts = {0: flat(attended_keep), 1: other_core(flat(attended_send))}
    for bit in x_bits:
        for k in list(parts):
            parts[k | 1 << bit] = swap(parts[k], "tensor", 1 << bit)
    groups = sorted(parts)
    d_share, parts[groups[nt // 2]] = tie(d_share, parts[groups[nt // 2]])
    resid, second_keep = mix(
        [parts[k] for k in groups], [weights[k] for k in groups], xf_keep, norm2_gain
    )
    second_send = other_core(second_keep)
    second_other = swap(second_keep, "dp", 1 << shared)
    d_share, second_send = tie(d_share, second_send)
    d_ffn_other = flat(gather_x(d_share))
    hidden, d_gate, d_up, second, ffn_keep, ffn_send, d_keep, d_send = feed_forward(
        (second_keep, second_send), None, d_hidden, w_gate, w_up, w_down
    )
    up_order = near[1:] + near[:1]
    gate_own = grad_rows([second], [d_gate], slots_of(near), dp, False, (), (BF16, BF16))
    d_up, *gate_own = tie(d_up, *gate_own)
    up_own = grad_rows([second], [d_up], slots_of(up_order), dp, False, (), (BF16, BF16))
    second_other, d_ffn_other, d_keep, *up_own = tie(second_other, d_ffn_other, d_keep, *up_own)
    d_part = (d_keep.astype(F32) + other_core(d_send).astype(F32)).astype(BF16)
    terms = [d_part]
    for bit in x_bits:
        if len(terms) > 1:
            terms = [sum(term.astype(F32) for term in terms).astype(BF16)]
        terms = [terms[0], swap(terms[0], "tensor", 1 << bit)]
    second_others = (second_other, other_core(second_other))
    d_ffn_others = (d_ffn_other, other_core(d_ffn_other))
    ffn_sum = (ffn_keep.astype(F32) + other_core(ffn_send).astype(F32)).astype(BF16)
    second_other, ffn_sum, terms[0] = tie(second_other, ffn_sum, terms[0])
    second_others = (second_other, second_others[1])
    hidden_o, d_gate_o, d_up_o, second_o, d_ffn_o = feed_forward(
        second_others, d_ffn_others, None, w_gate, w_up, w_down
    )
    def own_rows(array):
        return lax.dynamic_slice_in_dim(array, d_at * piece, piece, 0).astype(F32)

    def gain_shares(totals, gains):
        total = jnp.stack([total / own_rows(gain) for total, gain in zip(totals, gains)])
        total = total.reshape(len(gains), nt, piece // nt)
        pieces = [lax.dynamic_index_in_dim(total, t_at ^ k, 1, False) for k in range(nt)]
        return sum([pieces[0]] + [swap(pieces[k], "tensor", k) for k in range(1, nt)])

    def row_sum(weight, grad):
        return jnp.sum(own_rows(weight) * grad, axis=1)

    resid, hidden_o = tie(resid, hidden_o)
    chain = [resid]

    def step(*arrays):
        *arrays, chain[0] = tie(*arrays, chain[0])
        return arrays if len(arrays) > 1 else arrays[0]

    def done(*arrays):
        *arrays, chain[0] = tie(*arrays, chain[0])
        return arrays if len(arrays) > 1 else arrays[0]

    def arrive(*sums):
        for one in sums:
            one.terms[-1] = step(one.terms[-1])

    def more(*sums):
        for one in sums:
            if one.order:
                one.add()
                one.send = done(one.send)
                one.start()
            else:
                one.end()
                one.result = done(one.result)

    terms = step(*terms) if len(terms) > 1 else [step(*terms)]
    ffn, ffn_got = scatter_x_start(step(ffn_sum))
    d_resid, d_mixed_keep = done(*resid_back(terms, resid, cot_keep, norm2_gain))
    d_mixed_send = other_core(d_mixed_keep)
    d_gate_o = step(d_gate_o)
    gate = weight_grad([second_o], [d_gate_o], near, False, gate_own)
    gate.send = done(gate.send)
    gate.start()
    d_up_o = step(d_up_o)
    up = weight_grad([second_o], [d_up_o], up_order, False, up_own)
    up.send = done(up.send)
    up.start()
    d_mixed_send = step(d_mixed_send)
    out = weight_grad(
        [d_mixed_keep, d_mixed_send], [flat(attended_keep), flat(attended_send)], d_bits, True
    )
    out.send = done(out.send)
    out.start()
    query = step(query)
    tokens_of = (split, seqs, share, width)
    d_query_keep, d_query_send, *d_keyval = done(
        *attend_back(
            query,
            keyval_all,
            doc_start,
            (attended_keep, attended_send),
            (d_mixed_keep.reshape(tokens_of), d_mixed_send.reshape(tokens_of)),
            w_out,
            lse,
            cos_q,
            sin_q,
            scalars,
            kv_local,
            hd,
        )
    )
    d_query_keep, d_query_send = flat(d_query_keep), flat(d_query_send)
    kv_first = Summing(d_keyval[0], d_keyval[1], order_first)
    kv_last = Summing(d_keyval[2], d_keyval[3], order_last)
    arrive(gate, out)
    ffn_got = step(ffn_got)
    kv_first.start()
    kv_last.start()
    hidden = step(hidden)
    down = weight_grad([d_ffn, d_ffn_o], [hidden, hidden_o], near, True)
    down.send = done(down.send)
    first_normed = first_normed.reshape(2, part, width)
    d_query_keep = step(d_query_keep)
    grad_q = weight_grad([first_normed[0], first_normed[1]], [d_query_keep, d_query_send], d_bits)
    grad_q.send = done(grad_q.send)
    d_query_keep, d_query_send = step(d_query_keep, d_query_send)
    back_send, back_keep = done(dot(d_query_send, w_query, NT), dot(d_query_keep, w_query, NT))
    arrive(up, kv_first, kv_last)
    more(kv_first, kv_last)
    for rows in (gate, up, out):
        rows.add()
        rows.send = done(rows.send)
    arrive(kv_first, kv_last)
    more(kv_first, kv_last)
    for rows in (down, up, gate):
        rows.send = step(rows.send)
        rows.start()
    for _ in range(3, len(d_bits)):
        arrive(kv_first, kv_last)
        more(kv_first, kv_last)
    arrive(kv_first, kv_last)
    out.send = step(out.send)
    out.start()
    d_keyval_keep, d_keyval_send = (
        flat(array)
        for array in done(
            *finish_keyval(kv_first.terms, kv_last.terms, cos_kv, sin_kv, hd // 2, split)
        )
    )
    back_send = done((back_send + dot(d_keyval_send, keyval_weight, NT)).astype(BF16))
    back_got = other_core(back_send)
    arrive(gate, up, out)
    grad_q.start()
    d_keyval_keep = step(d_keyval_keep)
    grad_kv = weight_grad(
        [first_normed[0], first_normed[1]], [d_keyval_keep, d_keyval_send], order_last
    )
    grad_kv.send = done(grad_kv.send)
    grad_kv.start()
    more(out)
    back_got = step(back_got)
    back_keep = back_keep + dot(d_keyval_keep, keyval_weight, NT) + back_got.astype(F32)
    back_keep = done(back_keep)
    d_norm1, back_got = scatter_x_start(back_keep, done)
    more(gate, up)
    arrive(grad_q)
    more(grad_q)
    arrive(grad_kv)
    more(grad_kv)
    arrive(down)
    more(down)
    d_norm1 = d_norm1 + step(back_got).astype(F32)
    xf_share = own(xf_keep).astype(F32)
    scale1 = lax.rsqrt(jnp.mean(xf_share * xf_share, axis=-1, keepdims=True) + EPS)
    scaled = norm1_gain * d_norm1
    grad_tokens = done(
        own(d_resid)
        + scale1 * scaled
        - xf_share * scale1**3 * jnp.mean(scaled * xf_share, axis=-1, keepdims=True)
    )
    arrive(out)
    more(out)
    for last in range(2):
        for rows in (grad_q, grad_kv):
            arrive(rows)
            more(rows)
        if not last:
            arrive(down)
    live = [out, gate, up, down, grad_q, grad_kv]
    while live := [rows for rows in live if rows.result is None]:
        for rows in live:
            arrive(rows)
            more(rows)
    grad_gate, grad_up, grad_down = gate.result, up.result, down.result
    grad_outproj, grad_query, grad_keyval = out.result, grad_q.result, grad_kv.result
    ffn = ffn.astype(F32) + ffn_got.astype(F32)
    layer_out = (own(chain[0]) + RESID * ffn).astype(BF16)
    grad_gain1, grad_gain2 = gain_shares(
        [
            row_sum(w_query, grad_query) + row_sum(keyval_weight, grad_keyval),
            row_sum(w_gate, grad_gate) + row_sum(w_up, grad_up),
        ],
        (norm1_gain, norm2_gain),
    )
    return (
        layer_out,
        grad_tokens,
        grad_gain1,
        grad_query,
        grad_keyval.reshape(piece, kv_local, 2 * hd),
        grad_outproj,
        grad_gain2,
        grad_gate,
        grad_up,
        grad_down,
    )


def solution(mesh):
    placed = (
        P(None, "dp", None),
        P(None, "dp"),
        P(),
        P(None, "tensor"),
        P(None, "tensor", None),
        P("tensor", None),
        P(),
        P(None, "tensor"),
        P(None, "tensor"),
        P("tensor", None),
        P(None, "dp", None),
    )
    return jax.shard_map(
        body,
        mesh=mesh,
        in_specs=placed,
        out_specs=(
            P(None, ("dp", "tensor"), None),
            P(None, ("dp", "tensor"), None),
            P(("dp", "tensor")),
            P("dp", "tensor"),
            P("dp", "tensor", None),
            P("tensor", "dp"),
            P(("dp", "tensor")),
            P("dp", "tensor"),
            P("dp", "tensor"),
            P("tensor", "dp"),
        ),
        check_vma=False,
    )
```

```python
import math

import jax
import jax.numpy as jnp
from jax import lax
from jax.experimental import pallas as pl
from jax.experimental.pallas import tpu as pltpu
from jax.sharding import PartitionSpec as P

EPS = 1e-05
SCALE = 0.015625
RESID = 0.22
THETA = 10000000.0
NEG = -1e30
PAD = 16
VMEM = 56 * 1024 * 1024
F32 = jnp.float32
BF16 = jnp.bfloat16
NT = (((1,), (1,)), ((), ()))
TN = (((0,), (0,)), ((), ()))


def dot(a, b, dims=None):
    if dims is None:
        return jnp.dot(a, b, preferred_element_type=F32)
    return lax.dot_general(a, b, dims, preferred_element_type=F32)


def params():
    return pltpu.CompilerParams(vmem_limit_bytes=VMEM)


def cost(flops, nbytes):
    return pl.CostEstimate(flops=int(flops) // 1024, bytes_accessed=int(nbytes) // 1024, transcendentals=0)


def slot_order(bits):
    slots = [0]
    for bit in reversed(bits):
        slots = slots + [k ^ (1 << bit) for k in slots]
    return slots


def swap(value, axis, distance, up=False):
    pairs = [(i, i ^ distance) for i in range(lax.axis_size(axis))]
    return lax.ppermute(value, axis, [(i, j) for i, j in pairs if j > i or not up])


def rope_tables(positions, head_dim):
    half = head_dim // 2
    inverse = jnp.power(F32(THETA), -(jnp.arange(half).astype(F32) * (2.0 / head_dim)))
    angle = positions.astype(F32)[:, None] * inverse[None, :]
    return (jnp.cos(angle), jnp.sin(angle))


def rotate_lanes(x, cosine, sine, half):
    width = x.shape[1]
    lane = lax.broadcasted_iota(jnp.int32, x.shape, 1)
    ahead = pltpu.roll(x, width - half, 1)
    behind = pltpu.roll(x, half, 1)
    partner = jnp.where((lane & (2 * half - 1)) < half, ahead, behind)
    times = width // cosine.shape[1]
    if times > 1:
        cosine = jnp.concatenate([cosine] * times, 1)
        sine = jnp.concatenate([sine] * times, 1)
    return x * cosine + partner * sine


def whole(array):
    rank = array.ndim
    return pl.BlockSpec(array.shape, lambda *_: (0,) * rank)


def norm_keyval(tokens, seg_ids, gain, weight, cosine, sine, core, half, split):
    seqs, block, width = tokens.shape
    out = weight.shape[1]
    share = block // (2 * split)

    def kernel(at, tok_ref, seg_ref, gain_ref, w_ref, cos_ref, sin_ref, n_ref, a_ref, b_ref):
        pieces = []
        for rel in range(2):
            for x in range(split):
                begin = pl.multiple_of((2 * x + (at[0] ^ rel)) * share, share)
                pieces.append(tok_ref[0, pl.ds(begin, share), :])
        xf = jnp.concatenate(pieces, 0).astype(F32)
        scale = lax.rsqrt(jnp.mean(xf * xf, axis=-1, keepdims=True) + EPS)
        normed = (xf * scale * gain_ref[...]).astype(BF16)
        n_ref[...] = normed.reshape(n_ref.shape)
        raw = dot(normed, w_ref[...])
        keyval = rotate_lanes(raw, cos_ref[...], sin_ref[...], half).astype(BF16)
        a_ref[0, : block // 2, :] = keyval[: block // 2]
        b_ref[0] = keyval[block // 2 :]
        lane = lax.broadcasted_iota(jnp.int32, (PAD, out), 1)
        row = jnp.zeros((PAD, out), F32)
        for v in range(3):
            count = jnp.sum(jnp.where(seg_ref[0] == v, 1.0, 0.0))
            row = jnp.where(lane == v, count, row)
        a_ref[0, block // 2 :, :] = row.astype(BF16)

    return pl.pallas_call(
        kernel,
        grid_spec=pltpu.PrefetchScalarGridSpec(
            num_scalar_prefetch=1,
            grid=(seqs,),
            in_specs=[
                pl.BlockSpec((1, block, width), lambda s, at: (s, 0, 0)),
                pl.BlockSpec((1, 1, block), lambda s, at: (s, 0, 0)),
                pl.BlockSpec((1, width), lambda s, at: (0, 0)),
                whole(weight),
                whole(cosine),
                whole(sine),
            ],
            out_specs=[
                pl.BlockSpec((2, split, 1, share, width), lambda s, at: (0, 0, s, 0, 0)),
                pl.BlockSpec((1, block // 2 + PAD, out), lambda s, at: (s, 0, 0)),
                pl.BlockSpec((1, block // 2, out), lambda s, at: (s, 0, 0)),
            ],
        ),
        out_shape=[
            jax.ShapeDtypeStruct((2, split, seqs, share, width), BF16),
            jax.ShapeDtypeStruct((seqs, block // 2 + PAD, out), BF16),
            jax.ShapeDtypeStruct((seqs, block // 2, out), BF16),
        ],
        compiler_params=params(),
        cost_estimate=cost(2 * seqs * block * width * out, 4 * seqs * block * width),
        name="norm_keyval",
    )(core, tokens, seg_ids[:, None, :], gain.reshape(1, width), weight, cosine, sine)


def project_query(normed, weight, cosine, sine, half):
    _, split, seqs, share, width = normed.shape
    block = 2 * split * share
    out = weight.shape[1]

    def kernel(n_ref, w_ref, cos_ref, sin_ref, q_ref):
        raw = dot(n_ref[...].reshape(block, width), w_ref[...])
        q_ref[0] = rotate_lanes(raw, cos_ref[...], sin_ref[...], half).astype(BF16)

    return pl.pallas_call(
        kernel,
        grid=(seqs,),
        in_specs=[
            pl.BlockSpec((2, split, 1, share, width), lambda s: (0, 0, s, 0, 0)),
            whole(weight),
            whole(cosine),
            whole(sine),
        ],
        out_specs=pl.BlockSpec((1, block, out), lambda s: (s, 0, 0)),
        out_shape=jax.ShapeDtypeStruct((seqs, block, out), BF16),
        compiler_params=params(),
        cost_estimate=cost(2 * seqs * block * width * out, 2 * seqs * block * width),
        name="project_query",
    )(normed, weight, cosine, sine)


def stacked_lanes(x, group, hd, low):
    rows = x.shape[1]
    flat = jnp.concatenate([x[h * hd : (h + 1) * hd] for h in range(group)], 1)
    zero = jnp.zeros((hd, group * rows), flat.dtype)
    return jnp.concatenate([flat, zero] if low else [zero, flat], 0)


def stacked_rows(x, group, hd, low):
    parts = []
    for h in range(group):
        at = (h * hd) // (2 * hd) * (2 * hd)
        piece = x[:, at : at + 2 * hd]
        if (h % 2 == 0) != low:
            piece = pltpu.roll(piece, hd, 1)
        lane = lax.broadcasted_iota(jnp.int32, piece.shape, 1)
        parts.append(jnp.where((lane < hd) == low, piece, 0.0))
    return jnp.concatenate(parts, 0)


def keyval_of(last, count, sc, base, refs, blocks, half):
    parts = []
    for back in reversed(range(count)):
        chunk = jnp.maximum(last - back, 0) if back else last
        for low, high, table in ((refs[0], refs[1], 0), (refs[2], refs[3], blocks)):
            at = sc[base + table + chunk]
            one = low[jnp.minimum(at, blocks // 2 - 1), 0, :half, :]
            two = high[jnp.maximum(at - blocks // 2, 0), 0, :half, :]
            parts.append(jnp.where(at < blocks // 2, one, two))
    return jnp.concatenate(parts, 0)


def keyval_specs(blocks, half, width):
    return [
        pl.BlockSpec((blocks // 2, 1, rows, width), lambda s, h, sc: (0, s, 0, h))
        for rows in (half + PAD, half + PAD, half, half)
    ]


def mask_bias(last, count, block, position_block, doc_start, core, share, group):
    half = block // 2

    def place(axis):
        row = lax.broadcasted_iota(jnp.int32, (count * block, block), axis)
        chunk = row // block * block if axis == 0 else 0
        row = row - chunk
        rel = jnp.where(row >= half, 1, 0)
        row = row - half * rel
        return (row // share * 2 + (rel ^ core)) * share + row % share + chunk

    key_pos = (last - count + 1) * block + place(0)
    query_pos = position_block * block + place(1)
    visible = (key_pos >= doc_start) & (key_pos <= query_pos)
    bias = jnp.where(visible, 0.0, NEG)
    return jnp.concatenate([bias] * group, 1)


def pair_loops(mine, start, clear, visit, carry):
    whole_pairs = jnp.maximum(mine - 1 - clear, 0) // 2
    pairs = (mine - start) // 2
    run = lambda masked: lambda p, carry: visit(mine - 2 * p, masked, carry)
    carry = lax.fori_loop(1, 1 + whole_pairs, run(False), carry)
    return lax.fori_loop(1 + whole_pairs, 1 + pairs, run(True), carry)


def attend(query, keyval_all, doc_start, scalars, kv_local, hd, split):
    seqs, block, q_width = query.shape
    blocks = 2 * keyval_all[0].shape[0]
    group = q_width // kv_local // hd
    wide = group * block
    share = block // (2 * split)

    base = 2 + 2 * seqs
    half = block // 2

    def kernel(sc, q_ref, *refs):
        kv_refs, (doc_ref, keep_ref, send_ref, lse_ref, acc) = refs[:4], refs[4:]
        seq = pl.program_id(0)
        mine = sc[0]
        core = sc[1]
        start = sc[2 + seq]
        clear = sc[2 + seqs + seq]
        q_lanes = stacked_lanes((q_ref[0].astype(F32) * SCALE).astype(BF16).T, group, hd, True)
        doc = doc_ref[0]

        def scores_of(last, masked):
            kv = keyval_of(last, 2, sc, base, kv_refs, blocks, half)
            scores = dot(kv, q_lanes)
            if masked:
                scores = scores + mask_bias(last, 2, block, mine, doc, core, share, group)
            return kv, scores

        kv, scores = scores_of(mine, True)
        peak = jnp.max(scores, axis=0, keepdims=True)
        probs = jnp.exp(scores - peak)
        total = jnp.sum(probs, axis=0, keepdims=True)
        acc[...] = dot(kv, probs.astype(BF16), TN)

        def visit(last, masked, carry):
            peak, total = carry
            kv, scores = scores_of(last, masked)
            higher = jnp.maximum(peak, jnp.max(scores, axis=0, keepdims=True))
            shrink = jnp.exp(peak - higher)
            probs = jnp.exp(scores - higher)
            total = total * shrink + jnp.sum(probs, axis=0, keepdims=True)
            acc[...] = acc[...] * shrink + dot(kv, probs.astype(BF16), TN)
            return higher, total

        peak, total = pair_loops(mine, start, clear, visit, (peak, total))
        lse_ref[0, 0] = peak + jnp.log(total)
        result = acc[hd:] / total
        result = jnp.concatenate([result[:, h * block : (h + 1) * block] for h in range(group)], 0)
        result = result.T.astype(BF16)
        keep_ref[...] = result[:half].reshape(keep_ref.shape)
        send_ref[...] = result[half:].reshape(send_ref.shape)

    return pl.pallas_call(
        kernel,
        grid_spec=pltpu.PrefetchScalarGridSpec(
            num_scalar_prefetch=1,
            grid=(seqs, kv_local),
            in_specs=[
                pl.BlockSpec((1, block, group * hd), lambda s, h, sc: (s, 0, h)),
                *keyval_specs(blocks, half, 2 * hd),
                pl.BlockSpec((1, 1, block), lambda s, h, sc: (s, 0, 0)),
            ],
            out_specs=[
                pl.BlockSpec((split, 1, share, group * hd), lambda s, h, sc: (0, s, 0, h)),
                pl.BlockSpec((split, 1, share, group * hd), lambda s, h, sc: (0, s, 0, h)),
                pl.BlockSpec((1, 1, 1, wide), lambda s, h, sc: (s, h, 0, 0)),
            ],
            scratch_shapes=[pltpu.VMEM((2 * hd, wide), F32)],
        ),
        out_shape=[
            jax.ShapeDtypeStruct((split, seqs, share, q_width), BF16),
            jax.ShapeDtypeStruct((split, seqs, share, q_width), BF16),
            jax.ShapeDtypeStruct((seqs, kv_local, 1, wide), F32),
        ],
        compiler_params=params(),
        cost_estimate=cost(
            8 * seqs * block * q_width * blocks * block, 4 * seqs * blocks * block * 2 * hd
        ),
        name="attend",
    )(scalars, query, *keyval_all, doc_start)


def attend_back(
    query, keyval_all, doc_start, attended, d_mixed, w_out, lse, cosine, sine, scalars, kv_local, hd
):
    seqs, block, q_width = query.shape
    split, _, share, _ = attended[0].shape
    width = w_out.shape[1]
    blocks = 2 * keyval_all[0].shape[0]
    group = q_width // kv_local // hd
    wide = group * block
    base = 2 + 2 * seqs
    half = block // 2

    def kernel(sc, q_ref, *refs):
        kv_refs, refs = refs[:4], refs[4:]
        doc_ref, ok_ref, os_ref, keep_ref, send_ref, w_ref, lse_ref, cos_ref, sin_ref = refs[:9]
        dqk_ref, dqs_ref, ako, aso, bko, bso, acc, ak_ref, as_ref, bk_ref, bs_ref = refs[9:]
        seq = pl.program_id(0)
        mine = sc[0]
        core = sc[1]
        start = sc[2 + seq]
        clear = sc[2 + seqs + seq]
        doc = doc_ref[0]
        q = q_ref[0].astype(F32) * SCALE
        mixed = jnp.concatenate(
            [keep_ref[...].reshape(half, width), send_ref[...].reshape(half, width)], 0
        )
        d_out = dot(mixed, w_ref[...], NT).astype(BF16)
        d_out_t = d_out.T
        d_out = d_out.astype(F32)
        q_lanes = stacked_lanes(q.astype(BF16).T, group, hd, True)
        attended = jnp.concatenate(
            [ok_ref[...].reshape(half, group * hd), os_ref[...].reshape(half, group * hd)], 0
        )
        o_lanes = d_out_t.astype(F32) * attended.T.astype(F32)
        delta = jnp.concatenate(
            [
                jnp.sum(o_lanes[h * hd : (h + 1) * hd], axis=0, keepdims=True)
                for h in range(group)
            ],
            1,
        )
        d_lanes = stacked_lanes(d_out_t, group, hd, False)
        q_rows = stacked_rows(q, group, hd, True).astype(BF16)
        d_rows = stacked_rows(d_out, group, hd, False).astype(BF16)
        total = lse_ref[0, 0]
        acc[...] = jnp.zeros_like(acc)

        def put(chunk, value):
            for table, kept, sent, rows in (
                (0, ak_ref, as_ref, value[:half]),
                (blocks, bk_ref, bs_ref, value[half:]),
            ):
                at = sc[base + table + chunk]
                kept[jnp.minimum(at, blocks // 2)] = rows
                sent[jnp.where(at < blocks // 2, blocks // 2, at - blocks // 2)] = rows

        def work(chunk, masked):
            kv = keyval_of(chunk, 1, sc, base, kv_refs, blocks, half)
            scores = dot(kv, q_lanes)
            if masked:
                scores = scores + mask_bias(chunk, 1, block, mine, doc, core, share, group)
            probs = jnp.exp(scores - total)
            d_probs = dot(kv, d_lanes)
            d_scores = (probs * (d_probs - delta)).astype(BF16)
            d_kv = dot(probs.astype(BF16), d_rows) + dot(d_scores, q_rows)
            put(chunk, d_kv.astype(BF16))
            acc[...] += dot(kv, d_scores, TN)

        def clean(chunk, carry):
            put(chunk, jnp.zeros((block, 2 * hd), BF16))
            return carry

        def step(masked):
            def run(chunk, carry):
                work(chunk, masked)
                return carry

            return run

        lax.fori_loop(0, start, clean, 0)
        lax.fori_loop(start, clear, step(True), 0)
        lax.fori_loop(clear, mine, step(False), 0)
        work(mine, True)
        lax.fori_loop(mine + 1, blocks, clean, 0)
        for out, ref in ((ako, ak_ref), (aso, as_ref), (bko, bk_ref), (bso, bs_ref)):
            out[:, 0] = ref[: blocks // 2]
        dq = acc[:hd] * SCALE
        dq = jnp.concatenate([dq[:, h * block : (h + 1) * block] for h in range(group)], 0)
        dq = rotate_lanes(dq.T, cos_ref[...], -sin_ref[...], hd // 2)
        dq = dq.astype(BF16)
        dqk_ref[...] = dq[:half].reshape(dqk_ref.shape)
        dqs_ref[...] = dq[half:].reshape(dqs_ref.shape)

    ordered = pl.BlockSpec((split, 1, share, group * hd), lambda s, h, sc: (0, s, 0, h))
    mixed = pl.BlockSpec((split, 1, share, width), lambda s, h, sc: (0, s, 0, 0))
    parts = pl.BlockSpec((blocks // 2, 1, half, 2 * hd), lambda s, h, sc: (0, s, 0, h))
    return pl.pallas_call(
        kernel,
        grid_spec=pltpu.PrefetchScalarGridSpec(
            num_scalar_prefetch=1,
            grid=(seqs, kv_local),
            in_specs=[
                pl.BlockSpec((1, block, group * hd), lambda s, h, sc: (s, 0, h)),
                *keyval_specs(blocks, half, 2 * hd),
                pl.BlockSpec((1, 1, block), lambda s, h, sc: (s, 0, 0)),
                ordered,
                ordered,
                mixed,
                mixed,
                pl.BlockSpec((group * hd, width), lambda s, h, sc: (h, 0)),
                pl.BlockSpec((1, 1, 1, wide), lambda s, h, sc: (s, h, 0, 0)),
                whole(cosine),
                whole(sine),
            ],
            out_specs=[ordered] * 2 + [parts] * 4,
            scratch_shapes=[pltpu.VMEM((2 * hd, wide), F32)]
            + [pltpu.VMEM((blocks // 2 + 1, half, 2 * hd), BF16)] * 4,
        ),
        out_shape=[jax.ShapeDtypeStruct((split, seqs, share, q_width), BF16)] * 2
        + [jax.ShapeDtypeStruct((blocks // 2, seqs, half, kv_local * 2 * hd), BF16)] * 4,
        compiler_params=params(),
        cost_estimate=cost(
            20 * seqs * block * q_width * blocks * block, 8 * seqs * blocks * block * 2 * hd
        ),
        name="attend_back",
    )(scalars, query, *keyval_all, doc_start, *attended, *d_mixed, w_out, lse, cosine, sine)


def finish_keyval(first, last, cosine, sine, half, split):
    _, seqs, part, width = first[0].shape
    share = part // split
    terms = first + last
    count = len(first)

    def kernel(*refs):
        cos_ref, sin_ref, keep_ref, send_ref = refs[2 * count :]
        halves = [
            sum(ref[0, 0].astype(F32) for ref in some)
            for some in (refs[:count], refs[count : 2 * count])
        ]
        x = jnp.concatenate(halves, 0)
        x = rotate_lanes(x, cos_ref[...], -sin_ref[...], half).astype(BF16)
        keep_ref[...] = x[:part].reshape(keep_ref.shape)
        send_ref[...] = x[part:].reshape(send_ref.shape)

    out = pl.BlockSpec((split, 1, share, width), lambda s: (0, s, 0, 0))
    return pl.pallas_call(
        kernel,
        grid=(seqs,),
        in_specs=[pl.BlockSpec((1, 1, part, width), lambda s: (0, s, 0, 0))] * (2 * count)
        + [whole(cosine), whole(sine)],
        out_specs=[out] * 2,
        out_shape=[jax.ShapeDtypeStruct((split, seqs, share, width), BF16)] * 2,
        compiler_params=params(),
        cost_estimate=cost(0, 16 * seqs * part * width),
        name="finish_keyval",
    )(*terms, cosine, sine)


def mix(parts, weights, xf, gain):
    rows, deep = parts[0].shape
    width = weights[0].shape[1]
    count = len(parts)
    tile = math.gcd(width, 512)
    steps = width // tile

    def kernel(*refs):
        x_ref, gain_ref, resid_ref, n_ref, acc = refs[2 * count :]
        j = pl.program_id(0)
        left = jnp.concatenate([refs[k][...] for k in range(count)], 1)
        right = jnp.concatenate([refs[count + k][...] for k in range(count)], 0)
        resid = x_ref[...].astype(F32) + RESID * dot(left, right)
        resid_ref[...] = resid
        acc[j] = resid

        @pl.when(j == steps - 1)
        def _():
            square = sum(jnp.sum(acc[i] * acc[i], axis=-1, keepdims=True) for i in range(steps))
            scale = lax.rsqrt(square / width + EPS)
            for i in range(steps):
                at = pl.ds(i * tile, tile)
                n_ref[:, at] = (acc[i] * scale * gain_ref[:, at]).astype(BF16)

    fixed = lambda r, c: pl.BlockSpec((r, c), lambda j: (0, 0))
    return pl.pallas_call(
        kernel,
        grid=(steps,),
        in_specs=[fixed(rows, deep)] * count
        + [pl.BlockSpec((deep, tile), lambda j: (0, j))] * count
        + [pl.BlockSpec((rows, tile), lambda j: (0, j)), fixed(1, width)],
        out_specs=[pl.BlockSpec((rows, tile), lambda j: (0, j)), fixed(rows, width)],
        out_shape=[
            jax.ShapeDtypeStruct((rows, width), F32),
            jax.ShapeDtypeStruct((rows, width), BF16),
        ],
        scratch_shapes=[pltpu.VMEM((steps, rows, tile), F32)],
        compiler_params=params(),
        cost_estimate=cost(2 * rows * count * deep * width, 2 * count * deep * width),
        name="mix",
    )(*parts, *weights, xf, gain.reshape(1, width))


def resid_back(terms, resid, d_out, gain):
    rows, width = resid.shape
    tile = math.gcd(rows, 128)
    count = len(terms)

    def kernel(*refs):
        resid_ref, dy_ref, gain_ref, d_ref, mixed_ref = refs[count:]
        d_norm = sum(ref[...].astype(F32) for ref in refs[:count])
        resid = resid_ref[...]
        scale = lax.rsqrt(jnp.mean(resid * resid, axis=-1, keepdims=True) + EPS)
        scaled = gain_ref[...] * d_norm
        inner = jnp.mean(scaled * resid, axis=-1, keepdims=True)
        d_resid = dy_ref[...].astype(F32) + scale * scaled - resid * (scale**3 * inner)
        d_ref[...] = d_resid
        mixed_ref[...] = (RESID * d_resid).astype(BF16)

    one = pl.BlockSpec((tile, width), lambda i: (i, 0))
    return pl.pallas_call(
        kernel,
        grid=(rows // tile,),
        in_specs=[one] * (count + 2) + [pl.BlockSpec((1, width), lambda i: (0, 0))],
        out_specs=[one] * 2,
        out_shape=[
            jax.ShapeDtypeStruct((rows, width), F32),
            jax.ShapeDtypeStruct((rows, width), BF16),
        ],
        compiler_params=params(),
        cost_estimate=cost(0, 16 * rows * width),
        name="resid_back",
    )(*terms, resid, d_out, gain.reshape(1, width))


def hidden_back(d_ffn, w_down):
    rows, width = d_ffn.shape
    hidden = w_down.shape[0]
    tile = math.gcd(hidden, 512)

    def kernel(dy_ref, w_ref, o_ref):
        o_ref[...] = dot(dy_ref[...], w_ref[...], NT)

    return pl.pallas_call(
        kernel,
        grid=(hidden // tile,),
        in_specs=[whole(d_ffn), pl.BlockSpec((tile, width), lambda j: (j, 0))],
        out_specs=pl.BlockSpec((rows, tile), lambda j: (0, j)),
        out_shape=jax.ShapeDtypeStruct((rows, hidden), F32),
        compiler_params=params(),
        cost_estimate=cost(2 * rows * width * hidden, 2 * hidden * (rows + width)),
        name="hidden_back",
    )(d_ffn, w_down)


def feed_forward(normed, d_ffn, d_hidden, w_gate, w_up, w_down):
    back = d_hidden is not None
    part, width = normed[0].shape
    rows = 2 * part
    hidden = w_gate.shape[1]
    tile = math.gcd(hidden, 512)
    steps = hidden // tile

    sources = (d_hidden,) if back else d_ffn
    count = len(sources)

    def kernel(nk, ns, *refs):
        wg_ref, wu_ref, wd_ref, h_ref, dg_ref, du_ref, n_ref, *rest = refs[count:]
        at = pl.program_id(0)
        if not back:
            dy_ref, *rest = rest

        @pl.when(at == 0)
        def _():
            n_ref[:part] = nk[...]
            n_ref[part:] = ns[...]
            if not back:
                dy_ref[:part] = refs[0][...]
                dy_ref[part:] = refs[1][...]

        normed = n_ref[...]
        gate = dot(normed, wg_ref[...])
        up = dot(normed, wu_ref[...])
        d_hidden = refs[0][...] if back else dot(dy_ref[...], wd_ref[...], NT)
        sigma = jax.nn.sigmoid(gate)
        swish = gate * sigma
        hidden_tile = (swish * up).astype(BF16)
        d_gate = (d_hidden * up * sigma * (1.0 + gate * (1.0 - sigma))).astype(BF16)
        d_up = (d_hidden * swish).astype(BF16)
        h_ref[...] = hidden_tile
        dg_ref[...] = d_gate
        du_ref[...] = d_up
        if not back:
            return
        f_keep, f_send, dn_keep, dn_send, f_acc, n_acc = rest
        ffn = dot(hidden_tile, wd_ref[...])
        d_normed = dot(d_gate, wg_ref[...], NT) + dot(d_up, wu_ref[...], NT)

        @pl.when(at == 0)
        def _():
            f_acc[...] = ffn
            n_acc[...] = d_normed

        @pl.when(at > 0)
        def _():
            f_acc[...] += ffn
            n_acc[...] += d_normed

        @pl.when(at == steps - 1)
        def _():
            f_keep[...] = f_acc[:part].astype(BF16)
            f_send[...] = f_acc[part:].astype(BF16)
            dn_keep[...] = n_acc[:part].astype(BF16)
            dn_send[...] = n_acc[part:].astype(BF16)

    fixed = lambda r: pl.BlockSpec((r, width), lambda j: (0, 0))
    once = lambda r: pl.BlockSpec((r, width), lambda j: (0, 0), pipeline_mode=pl.Buffered(1))
    extra = 4 if back else 0
    return pl.pallas_call(
        kernel,
        grid=(steps,),
        in_specs=[once(part)] * 2
        + (
            [pl.BlockSpec((rows, tile), lambda j: (0, j))] if back else [once(part)] * 2
        )
        + [
            pl.BlockSpec((width, tile), lambda j: (0, j)),
            pl.BlockSpec((width, tile), lambda j: (0, j)),
            pl.BlockSpec((tile, width), lambda j: (j, 0)),
        ],
        out_specs=[pl.BlockSpec((rows, tile), lambda j: (0, j))] * 3
        + [fixed(rows)] * count
        + [fixed(part)] * extra,
        out_shape=[jax.ShapeDtypeStruct((rows, hidden), BF16)] * 3
        + [jax.ShapeDtypeStruct((rows, width), BF16)] * count
        + [jax.ShapeDtypeStruct((part, width), BF16)] * extra,
        scratch_shapes=[pltpu.VMEM((rows, width), F32)] * (extra // 2),
        compiler_params=params(),
        cost_estimate=cost(
            (10 if back else 6) * rows * width * hidden, 6 * width * hidden
        ),
        name="feed_forward" if back else "feed_forward_other",
    )(*normed, *sources, w_gate, w_up, w_down)


def grad_rows(lefts, rights, blocks_at, pieces, turned, base=(), dtypes=(F32, BF16)):
    count = blocks_at.shape[0]
    width = lefts[0].shape[1]
    piece = width // pieces
    columns = rights[0].shape[1]
    tile = math.gcd(columns, 512)
    pairs = len(lefts)
    half = count // 2 * piece

    def kernel(at, *refs):
        keep, send = refs[-2:]
        total = None
        for p in range(pairs):
            left = jnp.concatenate([refs[p * count + i][...] for i in range(count)], 1)
            right = refs[pairs * count + p][...]
            term = dot(right, left, TN) if turned else dot(left, right, TN)
            total = term if total is None else total + term
        if base:
            total = total + jnp.concatenate(
                [refs[-4][...].astype(F32), refs[-3][...].astype(F32)], int(turned)
            )
        keep[...] = (total[:, :half] if turned else total[:half]).astype(dtypes[0])
        send[...] = (total[:, half:] if turned else total[half:]).astype(dtypes[1])

    specs = [
        pl.BlockSpec((left.shape[0], piece), lambda j, at, i=i: (0, at[i]))
        for left in lefts
        for i in range(count)
    ] + [pl.BlockSpec((right.shape[0], tile), lambda j, at: (0, j)) for right in rights]
    tokens = sum(left.shape[0] for left in lefts)
    halves = [
        pl.BlockSpec((tile, half), lambda j, at: (j, 0))
        if turned
        else pl.BlockSpec((half, tile), lambda j, at: (0, j))
    ] * 2
    return pl.pallas_call(
        kernel,
        grid_spec=pltpu.PrefetchScalarGridSpec(
            num_scalar_prefetch=1,
            grid=(columns // tile,),
            in_specs=specs + halves[: len(base)],
            out_specs=halves,
        ),
        out_shape=[
            jax.ShapeDtypeStruct((columns, half) if turned else (half, columns), dtype)
            for dtype in dtypes
        ],
        compiler_params=params(),
        cost_estimate=cost(4 * tokens * half * columns, 2 * tokens * (2 * half + columns)),
        name="grad_rows",
    )(blocks_at, *[left for left in lefts for _ in range(count)], *rights, *base)


def body(
    tokens,
    seg_ids,
    norm1_gain,
    w_query,
    w_keyval,
    w_out,
    norm2_gain,
    w_gate,
    w_up,
    w_down,
    cotangent,
):
    seqs, block, width = tokens.shape
    kv_local = w_keyval.shape[1]
    hd = w_keyval.shape[2] // 2
    q_width = w_query.shape[1]
    kv_width = kv_local * 2 * hd
    dp = lax.axis_size("dp")
    nt = lax.axis_size("tensor")
    split = nt // 2
    share = block // nt
    piece = width // dp
    part = seqs * block // 2
    d_at = lax.axis_index("dp")
    t_at = lax.axis_index("tensor")
    core = t_at & 1
    x_at = t_at >> 1
    x_bits = list(range(1, nt.bit_length() - 1))
    d_bits = list(range(dp.bit_length() - 1))
    shared = d_bits[-1]
    near = d_bits[:-1]

    def ordered(array, rel):
        array = array.reshape(seqs, split, 2, share, *array.shape[2:])
        array = lax.dynamic_index_in_dim(array, core ^ rel, 2, keepdims=False)
        return jnp.swapaxes(array, 0, 1)

    def own(array):
        return lax.dynamic_index_in_dim(array.reshape(split, seqs, share, width), x_at, 0, False)

    def other_core(array):
        return swap(array, "tensor", 1)

    def flat(array):
        return array.reshape(-1, array.shape[-1])

    def tie(*arrays):
        return lax.optimization_barrier(arrays)

    def scatter_x_start(total, keep_order=lambda array: array):
        total = total.reshape(-1, seqs, share, width)
        for bit in reversed(x_bits):
            total = total.reshape(2, -1, seqs, share, width)
            mine = (t_at >> bit) & 1
            send = lax.dynamic_index_in_dim(total, mine ^ 1, 0, False).astype(BF16)
            total = lax.dynamic_index_in_dim(total, mine, 0, False).astype(F32)
            got = swap(keep_order(send), "tensor", 1 << bit)
            if bit == x_bits[0]:
                return total[0], got[0]
            total = total + got.astype(F32)

    def gather_x(total):
        total = total[None]
        for bit in x_bits:
            got = swap(total, "tensor", 1 << bit)
            low = (t_at >> bit) & 1 == 0
            total = jnp.concatenate(
                [jnp.where(low, total, got), jnp.where(low, got, total)], 0
            )
        return total

    class Summing:
        def __init__(self, keep, send, order, axis=0):
            self.terms, self.send, self.order, self.axis = [keep], send, list(order), axis
            self.size, self.result = keep.shape[axis], None

        def start(self):
            self.terms.append(swap(self.send, "dp", 1 << self.order.pop(0)))

        def add(self):
            self.size //= 2
            self.send = self.total(self.size).astype(BF16)

        def end(self):
            self.result = self.total(0)

        def total(self, first):
            return sum(
                lax.slice_in_dim(term, first, first + self.size, 1, self.axis).astype(F32)
                for term in self.terms
            )

    def slots_of(order):
        return d_at ^ jnp.array(slot_order(order), jnp.int32)

    def weight_grad(lefts, rights, order, turned=False, base=()):
        keep, send = grad_rows(lefts, rights, slots_of(order), dp, turned, base)
        return Summing(keep, send, order, int(turned))

    place = jnp.arange(block).reshape(2, split, share)
    place = ((place // share) % split * 2 + (place // (block // 2) ^ core)) * share + place % share
    positions = d_at * block + place.reshape(block)
    cosine, sine = rope_tables(positions, hd)
    cos_q = jnp.concatenate([cosine] * 4, 1)
    sin_q = jnp.concatenate([-sine, sine] * 2, 1)
    ones = jnp.ones((block, hd), F32)
    cos_kv = jnp.concatenate([cosine, cosine, ones], 1)
    sin_kv = jnp.concatenate([-sine, sine, 0.0 * ones], 1)
    keyval_weight = w_keyval.reshape(width, kv_width)
    order_first = d_bits
    order_last = d_bits[1:-1] + d_bits[:1] + d_bits[-1:]
    first_normed, *keyval = norm_keyval(
        tokens, seg_ids, norm1_gain, keyval_weight, cos_kv, sin_kv, core[None], hd // 2, split
    )
    cotangent, tokens, *keyval = tie(cotangent, tokens, *keyval)
    cot = jnp.concatenate([flat(ordered(cotangent, rel)) for rel in range(2)], 0)
    d_ffn = (RESID * cot.astype(F32)).astype(BF16)
    cot_keep = flat(ordered(cotangent, 0))
    xf_keep = flat(ordered(tokens, 0))
    keyval_all = [array[None] for array in keyval]
    for at in range(len(d_bits)):
        got = [
            swap(array, "dp", 1 << order[-1 - at], up=at == 0)
            for array, order in zip(keyval_all, (order_first, order_last))
        ]
        if at == 0:
            d_hidden = hidden_back(d_ffn, w_down)
            *got, d_hidden = tie(*got, d_hidden)
            weights = {0: w_out}
            for bit in x_bits:
                for k in list(weights):
                    weights[k | 1 << bit] = swap(weights[k], "tensor", 1 << bit)
        if at == len(d_bits) - 1:
            query = project_query(first_normed, w_query, cos_q, sin_q, hd // 2)
            d_share = lax.dynamic_slice_in_dim(cotangent, t_at * share, share, 1)
            d_share = (RESID * d_share.astype(F32)).astype(BF16)
            *got, query, d_share = tie(*got, query, d_share)
            d_share = swap(d_share, "dp", 1 << shared)
        if at == len(d_bits) - 1:
            keyval_all = [array for pair in zip(keyval_all, got) for array in pair]
        else:
            keyval_all = [jnp.concatenate([a, b], 0) for a, b in zip(keyval_all, got)]
    for k in list(weights):
        weights[k | 1] = other_core(weights[k])

    before = sum(
        jnp.sum(array[:, :, block // 2, :3].astype(F32), axis=0) for array in keyval_all[:2]
    ).astype(jnp.int32)
    seg_ordered = jnp.stack([ordered(seg_ids, rel) for rel in range(2)])
    seg_ordered = seg_ordered.transpose(2, 0, 1, 3).reshape(seqs, block)
    doc_start = jnp.sum(
        jnp.where(seg_ordered[:, :, None] > jnp.arange(3), before[:, None, :], 0), axis=2
    )
    start = jnp.min(doc_start, axis=1) // block
    clear = jnp.clip((jnp.max(doc_start, axis=1) + block - 1) // block, start, d_at)

    def slot_of(order):
        slots = slot_order(order)
        table = jnp.array([slots.index(k) for k in range(dp)], jnp.int32)
        return table[d_at ^ jnp.arange(dp)]

    scalars = jnp.concatenate(
        [d_at[None], core[None], start, clear, slot_of(order_first), slot_of(order_last)]
    ).astype(jnp.int32)
    doc_start = doc_start[:, None, :]
    attended_keep, attended_send, lse = attend(
        query, keyval_all, doc_start, scalars, kv_local, hd, split
    )
    parts = {0: flat(attended_keep), 1: other_core(flat(attended_send))}
    for bit in x_bits:
        for k in list(parts):
            parts[k | 1 << bit] = swap(parts[k], "tensor", 1 << bit)
    groups = sorted(parts)
    d_share, parts[groups[nt // 2]] = tie(d_share, parts[groups[nt // 2]])
    resid, second_keep = mix(
        [parts[k] for k in groups], [weights[k] for k in groups], xf_keep, norm2_gain
    )
    second_send = other_core(second_keep)
    second_other = swap(second_keep, "dp", 1 << shared)
    d_share, second_send = tie(d_share, second_send)
    d_ffn_other = flat(gather_x(d_share))
    hidden, d_gate, d_up, second, ffn_keep, ffn_send, d_keep, d_send = feed_forward(
        (second_keep, second_send), None, d_hidden, w_gate, w_up, w_down
    )
    up_order = near[1:] + near[:1]
    gate_own = grad_rows([second], [d_gate], slots_of(near), dp, False, (), (BF16, BF16))
    d_up, *gate_own = tie(d_up, *gate_own)
    up_own = grad_rows([second], [d_up], slots_of(up_order), dp, False, (), (BF16, BF16))
    second_other, d_ffn_other, d_keep, *up_own = tie(second_other, d_ffn_other, d_keep, *up_own)
    d_part = (d_keep.astype(F32) + other_core(d_send).astype(F32)).astype(BF16)
    terms = [d_part]
    for bit in x_bits:
        if len(terms) > 1:
            terms = [sum(term.astype(F32) for term in terms).astype(BF16)]
        terms = [terms[0], swap(terms[0], "tensor", 1 << bit)]
    second_others = (second_other, other_core(second_other))
    d_ffn_others = (d_ffn_other, other_core(d_ffn_other))
    ffn_sum = (ffn_keep.astype(F32) + other_core(ffn_send).astype(F32)).astype(BF16)
    second_other, ffn_sum, terms[0] = tie(second_other, ffn_sum, terms[0])
    second_others = (second_other, second_others[1])
    hidden_o, d_gate_o, d_up_o, second_o, d_ffn_o = feed_forward(
        second_others, d_ffn_others, None, w_gate, w_up, w_down
    )
    def own_rows(array):
        return lax.dynamic_slice_in_dim(array, d_at * piece, piece, 0).astype(F32)

    def gain_shares(totals, gains):
        total = jnp.stack([total / own_rows(gain) for total, gain in zip(totals, gains)])
        total = total.reshape(len(gains), nt, piece // nt)
        pieces = [lax.dynamic_index_in_dim(total, t_at ^ k, 1, False) for k in range(nt)]
        return sum([pieces[0]] + [swap(pieces[k], "tensor", k) for k in range(1, nt)])

    def row_sum(weight, grad):
        return jnp.sum(own_rows(weight) * grad, axis=1)

    resid, hidden_o = tie(resid, hidden_o)
    chain = [resid]

    def step(*arrays):
        *arrays, chain[0] = tie(*arrays, chain[0])
        return arrays if len(arrays) > 1 else arrays[0]

    def done(*arrays):
        *arrays, chain[0] = tie(*arrays, chain[0])
        return arrays if len(arrays) > 1 else arrays[0]

    def arrive(*sums):
        for one in sums:
            one.terms[-1] = step(one.terms[-1])

    def more(*sums):
        for one in sums:
            if one.order:
                one.add()
                one.send = done(one.send)
                one.start()
            else:
                one.end()
                one.result = done(one.result)

    terms = step(*terms) if len(terms) > 1 else [step(*terms)]
    ffn, ffn_got = scatter_x_start(step(ffn_sum))
    d_resid, d_mixed_keep = done(*resid_back(terms, resid, cot_keep, norm2_gain))
    d_mixed_send = other_core(d_mixed_keep)
    d_gate_o = step(d_gate_o)
    gate = weight_grad([second_o], [d_gate_o], near, False, gate_own)
    gate.send = done(gate.send)
    gate.start()
    d_up_o = step(d_up_o)
    up = weight_grad([second_o], [d_up_o], up_order, False, up_own)
    up.send = done(up.send)
    up.start()
    d_mixed_send = step(d_mixed_send)
    out = weight_grad(
        [d_mixed_keep, d_mixed_send], [flat(attended_keep), flat(attended_send)], d_bits, True
    )
    out.send = done(out.send)
    out.start()
    query = step(query)
    tokens_of = (split, seqs, share, width)
    d_query_keep, d_query_send, *d_keyval = done(
        *attend_back(
            query,
            keyval_all,
            doc_start,
            (attended_keep, attended_send),
            (d_mixed_keep.reshape(tokens_of), d_mixed_send.reshape(tokens_of)),
            w_out,
            lse,
            cos_q,
            sin_q,
            scalars,
            kv_local,
            hd,
        )
    )
    d_query_keep, d_query_send = flat(d_query_keep), flat(d_query_send)
    kv_first = Summing(d_keyval[0], d_keyval[1], order_first)
    kv_last = Summing(d_keyval[2], d_keyval[3], order_last)
    arrive(gate, out)
    ffn_got = step(ffn_got)
    kv_first.start()
    kv_last.start()
    hidden = step(hidden)
    down = weight_grad([d_ffn, d_ffn_o], [hidden, hidden_o], near, True)
    down.send = done(down.send)
    first_normed = first_normed.reshape(2, part, width)
    d_query_keep = step(d_query_keep)
    grad_q = weight_grad([first_normed[0], first_normed[1]], [d_query_keep, d_query_send], d_bits)
    grad_q.send = done(grad_q.send)
    d_query_keep, d_query_send = step(d_query_keep, d_query_send)
    back_send, back_keep = done(dot(d_query_send, w_query, NT), dot(d_query_keep, w_query, NT))
    arrive(up, kv_first, kv_last)
    more(kv_first, kv_last)
    for rows in (gate, up, out):
        rows.add()
        rows.send = done(rows.send)
    arrive(kv_first, kv_last)
    more(kv_first, kv_last)
    for rows in (down, up, gate):
        rows.send = step(rows.send)
        rows.start()
    for _ in range(3, len(d_bits)):
        arrive(kv_first, kv_last)
        more(kv_first, kv_last)
    arrive(kv_first, kv_last)
    out.send = step(out.send)
    out.start()
    d_keyval_keep, d_keyval_send = (
        flat(array)
        for array in done(
            *finish_keyval(kv_first.terms, kv_last.terms, cos_kv, sin_kv, hd // 2, split)
        )
    )
    back_send = done((back_send + dot(d_keyval_send, keyval_weight, NT)).astype(BF16))
    back_got = other_core(back_send)
    arrive(gate, up, out)
    grad_q.start()
    d_keyval_keep = step(d_keyval_keep)
    grad_kv = weight_grad(
        [first_normed[0], first_normed[1]], [d_keyval_keep, d_keyval_send], order_last
    )
    grad_kv.send = done(grad_kv.send)
    grad_kv.start()
    more(out)
    back_got = step(back_got)
    back_keep = back_keep + dot(d_keyval_keep, keyval_weight, NT) + back_got.astype(F32)
    back_keep = done(back_keep)
    d_norm1, back_got = scatter_x_start(back_keep, done)
    more(gate, up)
    arrive(grad_q)
    more(grad_q)
    arrive(grad_kv)
    more(grad_kv)
    d_norm1 = d_norm1 + step(back_got).astype(F32)
    xf_share = own(xf_keep).astype(F32)
    scale1 = lax.rsqrt(jnp.mean(xf_share * xf_share, axis=-1, keepdims=True) + EPS)
    scaled = norm1_gain * d_norm1
    grad_tokens = done(
        own(d_resid)
        + scale1 * scaled
        - xf_share * scale1**3 * jnp.mean(scaled * xf_share, axis=-1, keepdims=True)
    )
    arrive(out)
    more(out)
    for last in range(2):
        for rows in (grad_q, grad_kv):
            arrive(rows)
            more(rows)
        if not last:
            arrive(down)
            more(down)
    live = [out, gate, up, down, grad_q, grad_kv]
    while live := [rows for rows in live if rows.result is None]:
        for rows in live:
            arrive(rows)
            more(rows)
    grad_gate, grad_up, grad_down = gate.result, up.result, down.result
    grad_outproj, grad_query, grad_keyval = out.result, grad_q.result, grad_kv.result
    ffn = ffn.astype(F32) + ffn_got.astype(F32)
    layer_out = (own(chain[0]) + RESID * ffn).astype(BF16)
    grad_gain1, grad_gain2 = gain_shares(
        [
            row_sum(w_query, grad_query) + row_sum(keyval_weight, grad_keyval),
            row_sum(w_gate, grad_gate) + row_sum(w_up, grad_up),
        ],
        (norm1_gain, norm2_gain),
    )
    return (
        layer_out,
        grad_tokens,
        grad_gain1,
        grad_query,
        grad_keyval.reshape(piece, kv_local, 2 * hd),
        grad_outproj,
        grad_gain2,
        grad_gate,
        grad_up,
        grad_down,
    )


def solution(mesh):
    placed = (
        P(None, "dp", None),
        P(None, "dp"),
        P(),
        P(None, "tensor"),
        P(None, "tensor", None),
        P("tensor", None),
        P(),
        P(None, "tensor"),
        P(None, "tensor"),
        P("tensor", None),
        P(None, "dp", None),
    )
    return jax.shard_map(
        body,
        mesh=mesh,
        in_specs=placed,
        out_specs=(
            P(None, ("dp", "tensor"), None),
            P(None, ("dp", "tensor"), None),
            P(("dp", "tensor")),
            P("dp", "tensor"),
            P("dp", "tensor", None),
            P("tensor", "dp"),
            P(("dp", "tensor")),
            P("dp", "tensor"),
            P("dp", "tensor"),
            P("tensor", "dp"),
        ),
        check_vma=False,
    )
```
